256 devices in a mesh: freq: 2 (over core), xs: 64 (over z, y, x_hi), yh: 2 (over x_lo).
Axes of the slice: x: 4 (x_hi: 2, x_lo: 2; x = x_hi * 2 + x_lo), y: 4, z: 8, core: 2. Of those that a mesh axis runs over, the one named last changes fastest.
Arguments:
- field: float32 [2, 64, 1024, 2048], P(None, 'freq', 'xs', 'yh'), may hold values from -6 to 6
- spectral_phase: float32 [64, 2048], P('freq'), may hold values from -3.140625 to 3.140625
- chirp_shift: int32 [64], P('freq'), may hold values from -4 to 4, as said below
- tile_map: int32 [256], P('xs'), may hold values from 0 to 3
- tile_phase: float32 [4, 64], P(None, 'freq'), may hold values from -3.140625 to 3.140625
Outputs:
- pulse: float32 [2, 32, 1024, 2048], P(None, None, 'xs', ('freq', 'yh'))
The draws below stay inside these ranges and needn't reach their ends.
Inputs may be any that keep to these rules, and one draw needn't show every extreme that they name: `chirp_shift`: some frequency has the offset 4 and another the offset -4.
All inputs are finite; a program needn't handle non-finite values.
Results may differ from the reference program's by a relative error of at most 0.0003.
Values sent between devices are 32-bit elements; how exact they have to be, the bound alone decides.
A program may use at most 128 MiB of HBM per device.

```python
import math
import jax
import jax.numpy as jnp
from jax import lax

NF = 64
NY = 2048
NT = 32
NTILE = 4
RB = 4
MAXS = 4
NX = 1024
NXB = 256


def draw_chirp_shift(key, part):
    key = jax.random.fold_in(key, 7)
    first, second = jax.random.split(key)
    values = jax.random.randint(first, (NF,), -MAXS, MAXS + 1)
    order = jax.random.permutation(second, NF)
    values = values.at[order[0]].set(MAXS)
    values = values.at[order[1]].set(-MAXS)
    return values.astype(jnp.int32)


def place_ends(entries, stream_key, least, top_value):
    place = [jax.random.randint(jax.random.fold_in(stream_key, axis), (), 0, length) for axis, length in enumerate(entries.shape)]
    widest = entries.shape.index(max(entries.shape))
    next_to = place[:widest] + [(place[widest] + 1) % entries.shape[widest]] + place[widest + 1:]
    return entries.at[tuple(place)].set(least).at[tuple(next_to)].set(top_value)


def block_levels(key, shape, pieces, low, high):
    level, own = 1.0, jax.random.fold_in(key, 6)
    for position, parts in pieces:
        draws = jnp.exp(jax.random.uniform(jax.random.fold_in(own, position), (parts,), jnp.float32, low / len(pieces), high / len(pieces)))
        level = level * jnp.repeat(draws, shape[position] // parts).reshape([-1 if axis == position else 1 for axis in range(len(shape))])
    return level


def centred(key, extent, spread, most, cuts=(), held_as=jnp.bfloat16):
    values = jax.random.normal(key, extent, jnp.float32) * spread
    if len(cuts) > 0:
        values = block_levels(key, extent, cuts, -0.22, 0.18) * values
    return jnp.clip(values, min=-most, max=most).astype(held_as)


def setup_inputs(seed: int = 0) -> dict:
    streams_of = jax.random.split(jax.random.key(seed), 6)
    return {
        "field": centred(streams_of[0], (2, NF, NX, NY), 1.0, 6.0, ((1, 2), (2, 64), (3, 2)), jnp.float32),
        "spectral_phase": jnp.clip(jax.random.uniform(streams_of[1], (NF, NY), jnp.float32, -3.140625, 3.140625), -3.140625, 3.140625),
        "chirp_shift": draw_chirp_shift(jax.random.fold_in(streams_of[5], 71), 0),
        "tile_map": place_ends(jax.random.randint(streams_of[3], (NXB,), 0, NTILE), jax.random.fold_in(streams_of[3], 1), 0, NTILE - 1).astype(jnp.int32),
        "tile_phase": jnp.clip(jax.random.uniform(streams_of[4], (NTILE, NF), jnp.float32, -3.140625, 3.140625), -3.140625, 3.140625),
    }


def reference(field, spectral_phase, chirp_shift, tile_map, tile_phase):
    near = lax.complex(field[0], field[1])
    spectrum = jnp.fft.fft(near, axis=-1) / math.sqrt(NY)
    gap = lax.complex(jnp.cos(spectral_phase), jnp.sin(spectral_phase))
    propagated = spectrum * gap[:, None, :]
    margin = MAXS * RB
    padded = jnp.pad(propagated, ((0, 0), (margin, margin), (0, 0)))

    def move_rows(block, offset):
        return lax.dynamic_slice_in_dim(block, (margin - RB * offset).astype(jnp.int32), NX, 0)
    shifted = jax.vmap(move_rows)(padded, chirp_shift)
    row_tiles = jnp.repeat(tile_map, RB)
    angle = tile_phase[row_tiles, :].T
    tiled = shifted * lax.complex(jnp.cos(angle), jnp.sin(angle))[:, :, None]
    times = jnp.arange(NT, dtype=jnp.int32)
    freqs = jnp.arange(NF, dtype=jnp.int32)
    turns = times[:, None] * freqs[None, :] % NF
    phase = 2.0 * math.pi / NF * turns.astype(jnp.float32)
    weights = lax.complex(jnp.cos(phase), jnp.sin(phase)) / math.sqrt(NF)
    result = jnp.einsum('tf,fxk->txk', weights, tiled)
    return jnp.stack([jnp.real(result), jnp.imag(result)])
```

```python
import functools
import math

import jax
import jax.numpy as jnp
import numpy as np
from jax import lax
from jax.experimental import pallas as pl
from jax.experimental.pallas import tpu as pltpu
from jax.sharding import PartitionSpec as P

NF = 64
NY = 2048
NT = 32
AHEAD = 3
BF = jnp.bfloat16
F32 = jnp.float32
AXES = ("freq", "xs", "yh")
MESH = pl.DeviceIdType.MESH


def dft_tables():
    m = np.arange(256)
    angle = 2.0 * np.pi * (np.outer(m, m) % 256) / 256
    waves = np.stack([np.cos(angle), np.sin(angle)]) / math.sqrt(NY)
    odd_order = np.concatenate([np.arange(64) + 64 * b for b in (1, 0, 3, 2)])
    turn = 2.0 * np.pi * np.outer(np.arange(8), m) / NY
    twiddle = np.stack([np.cos(turn), np.sin(turn)])
    return np.stack([waves, waves[:, :, odd_order]]).astype(np.float32), twiddle.astype(np.float32)


def split(value):
    high = value.astype(BF)
    return high, (value - high.astype(F32)).astype(BF)


def dot(a, b):
    return jnp.dot(a, b, preferred_element_type=F32)


def dot_t(a, b):
    return lax.dot_general(a, b, (((1,), (1,)), ((), ())), preferred_element_type=F32)


def butterflies(re, im, tw):
    a = [(re[:, 256 * c : 256 * c + 256], im[:, 256 * c : 256 * c + 256]) for c in range(4)]
    r = math.sqrt(0.5)

    def add(u, v):
        return u[0] + v[0], u[1] + v[1]

    def sub(u, v):
        return u[0] - v[0], u[1] - v[1]

    def mi(u):
        return u[1], -u[0]

    def four(b):
        e0, e1 = add(b[0], b[2]), sub(b[0], b[2])
        e2, e3 = add(b[1], b[3]), mi(sub(b[1], b[3]))
        return add(e0, e2), add(e1, e3), sub(e0, e2), sub(e1, e3)

    even = four(a)
    b1 = ((a[1][0] + a[1][1]) * r, (a[1][1] - a[1][0]) * r)
    b3 = ((a[3][1] - a[3][0]) * r, (-a[3][0] - a[3][1]) * r)
    odd = four((a[0], b1, mi(a[2]), b3))
    both = []
    for side, parts in enumerate((even, odd)):
        row = []
        for j in range(4):
            p = 2 * j + side
            u = parts[j]
            if p:
                c, s = tw[0, p : p + 1, :], tw[1, p : p + 1, :]
                u = u[0] * c + u[1] * s, u[1] * c - u[0] * s
            row.append(u)
        both.append(row)
    return both


def kernel(
    strips, field, phi, prm, waves, tw, out,
    flat, snd, keep, other, halo_a, halo_b, prm_out, prm_in, prm_pair,
    e_own, e_other, t_hi, t_lo, perm, ww, w_lo, wh, wh_lo,
    l_hi, l_lo, spec, own, own_in, pp, msg, msg_in, *rest,
):
    by_lane = rest[:4]
    (load_sem, snd_s, snd_r, ha_s, ha_r, hb_s, hb_r, prm_s, prm_r, own_s, own_r, msg_s, msg_r) = rest[4:]
    g, s, h = (lax.axis_index(a) for a in AXES)
    odd = lax.rem(s, 2)
    pair = s + 1 - 2 * odd
    onward = lax.rem(s + strips + 4 * odd - 2, strips)
    back = lax.rem(s + strips + 2 - 4 * odd, strips)
    core = (1 - g, s, h)

    def peer(dg, ds, dh):
        return (lax.rem(g + dg, 2), pair if ds else s, lax.rem(h + dh, 2))

    def remote(src, dst, a, b, to):
        return pltpu.make_async_remote_copy(
            src_ref=src, dst_ref=dst, send_sem=a, recv_sem=b, device_id=to, device_id_type=MESH
        )

    def block_of(n):
        return n + odd * (3 - 2 * n)

    loads = [
        pltpu.make_async_copy(field.at[:, :, pl.ds(128 * y, 128)], flat.at[y], load_sem.at[y]) for y in range(8)
    ]
    for c in loads:
        c.start()
    barrier = pltpu.get_barrier_semaphore()
    greet = [peer(dg, ds, dh) for dg in range(2) for ds in range(2) for dh in range(2) if dg + ds + dh]
    greet += [(g, onward, h), (g, back, h)]
    for to in greet:
        pl.semaphore_signal(barrier, inc=1, device_id=to, device_id_type=MESH)
    for c in loads:
        c.wait()

    def snd_copy(i):
        return remote(snd.at[i], other.at[i], snd_s.at[i], snd_r.at[i], core)

    def a_copy(i):
        return remote(keep.at[i], halo_a.at[i], ha_s.at[i], ha_r.at[i], (g, onward, h))

    def b_copy(i):
        return remote(other.at[i], halo_b.at[i], hb_s.at[i], hb_r.at[i], (g, onward, h))

    def gather_rows(i, side, into):
        row = 4 * block_of(i // 2) + 2 * side + lax.rem(i, 2)
        for c in range(2):
            for y in range(8):
                into[i, c, :, 128 * y : 128 * y + 128] = flat[y, c, pl.ds(row, 32, stride=16), :]

    def pack_send(i, carry):
        gather_rows(i, 1 - g, snd)
        return carry

    lax.fori_loop(0, 8, pack_send, 0)
    pl.semaphore_wait(barrier, len(greet))
    prm_out[...] = pltpu.roll(prm[...], 32, 1)
    prm_core = remote(prm_out, prm_in, prm_s.at[0], prm_r.at[0], core)
    prm_strip = remote(prm, prm_pair, prm_s.at[1], prm_r.at[1], peer(0, 1, 0))
    prm_core.start()
    prm_strip.start()
    for i in range(8):
        snd_copy(i).start()

    def pack_keep(i, carry):
        gather_rows(i, g, keep)
        return carry

    lax.fori_loop(0, 8, pack_keep, 0)
    for i in range(AHEAD):
        a_copy(i).start()
        snd_copy(i).wait_recv()
        b_copy(i).start()

    lane = lax.broadcasted_iota(jnp.int32, (512, 512), 0)
    wave = lax.broadcasted_iota(jnp.int32, (512, 512), 1)
    turn = lax.rem(lane, 128)
    for half in range(2):
        side = (turn >= 64).astype(jnp.int32)
        side = side if half == 0 else 1 - side
        perm[half] = (8 * lax.rem(turn, 64) + 2 * (lane // 128) + side == wave).astype(F32).astype(BF)
        c_hi, c_lo = split(waves[half, 0])
        s_hi, s_lo = split(waves[half, 1])
        for table, c, w in ((t_hi, c_hi, s_hi), (t_lo, c_lo, s_lo)):
            table[half, 0:256, 0:256] = c
            table[half, 0:256, 256:512] = -w
            table[half, 256:512, 0:256] = w
            table[half, 256:512, 256:512] = c

    lanes = lax.rem(lax.broadcasted_iota(jnp.int32, (1, 512), 1), 128)
    for b in range(4):
        x = phi[:, 512 * b : 512 * b + 512]
        late = lanes >= 64 if b % 2 == 0 else lanes < 64
        sign = 1.0 - 2.0 * jnp.where(late, h, 0).astype(F32)
        for part, value in enumerate((jnp.cos(x), jnp.sin(x))):
            hi, lo = split(value)
            e_own[part, :, 512 * b : 512 * b + 512] = (dot_t(hi, perm[b % 2]) + dot_t(lo, perm[b % 2])) * sign
    e_copy = remote(e_own, e_other, prm_s.at[2], prm_r.at[2], core)
    e_copy.start()

    prm_core.wait()
    prm_strip.wait()
    both = prm[...] + prm_in[...]
    shift = both[0:1, :]
    col = lax.broadcasted_iota(jnp.int32, (NT, 128), 1)
    freq = lax.rem(lax.rem(col, 64) + 32 * g, NF)
    angle = (2.0 * math.pi / NF) * lax.rem(lax.broadcasted_iota(jnp.int32, (NT, 128), 0) * freq, NF).astype(F32)
    scale = 1.0 / math.sqrt(NF)
    real_in = col < 64

    def base(tile):
        phase = jnp.zeros((1, 128), F32)
        for t in range(4):
            phase = phase + jnp.where(tile == float(t), both[1 + t : 2 + t, :], 0.0)
        re, im = jnp.cos(angle + phase) * scale, jnp.sin(angle + phase) * scale
        return jnp.concatenate([jnp.where(real_in, re, -im), jnp.where(real_in, im, re)], axis=0)

    far = (4 * (1 - 2 * odd)).astype(F32)
    inside = jnp.where(odd == 1, (s > 1).astype(F32), (s < strips - 2).astype(F32))
    for nd in range(4):
        dest = block_of(nd)
        here, there = base(prm[8 + nd : 9 + nd, :]), base(prm_pair[pl.ds(8 + dest, 1), :])
        rows = slice(64 * nd, 64 * nd + 64)
        for n in range(4):
            source = block_of(n)
            own_hi, own_lo = split(jnp.where(shift == (nd - source).astype(F32), here, 0.0))
            step = (dest - source).astype(F32)
            pair_hi, pair_lo = split(jnp.where(shift == step + far, there, 0.0))
            halo_hi, halo_lo = split(jnp.where(shift == step - far, there * inside, 0.0))
            at = 128 * n
            below = slice(256 + 64 * nd, 320 + 64 * nd)
            ww[rows, at : at + 128] = own_hi
            ww[rows, 512 + at : 640 + at] = own_hi
            w_lo[rows, at : at + 128] = own_lo
            ww[below, at : at + 128] = pair_hi
            ww[below, 512 + at : 640 + at] = pair_hi
            w_lo[below, at : at + 128] = pair_lo
            wh[n, rows, 0:128] = halo_hi
            wh[n, rows, 128:256] = halo_hi
            wh_lo[n, rows, :] = halo_lo
    e_copy.wait()

    def spectrum(a, b, i, at, depth):
        re = jnp.concatenate([a[i, 0], b[i, 0]], axis=0)
        im = jnp.concatenate([a[i, 1], b[i, 1]], axis=0)
        for side, parts in enumerate(butterflies(re, im, tw)):
            for j, pieces in enumerate(parts):
                for half, w in enumerate(pieces):
                    hi, lo = split(w)
                    l_hi[side, 64 * j : 64 * j + 64, 256 * half : 256 * half + 256] = hi
                    l_lo[side, 64 * j : 64 * j + 64, 256 * half : 256 * half + 256] = lo
        even, uneven = (
            dot(l_hi[side], t_hi[side]) + dot(l_lo[side], t_hi[side]) + dot(l_hi[side], t_lo[side])
            for side in range(2)
        )
        early = lax.broadcasted_iota(jnp.int32, (64, 128), 1) < 64
        for j in range(4):
            for b4 in range(4):
                first, second = (even, uneven) if b4 % 2 == 0 else (uneven, even)
                rows = slice(64 * j, 64 * j + 64)
                c0 = 128 * (b4 // 2)
                u = jnp.where(early, first[rows, c0 : c0 + 128], second[rows, c0 : c0 + 128])
                v = jnp.where(early, first[rows, 256 + c0 : 384 + c0], second[rows, 256 + c0 : 384 + c0])
                e0 = 512 * b4 + 128 * j
                c, w = (
                    jnp.concatenate([e_own[part, :, e0 : e0 + 128], e_other[part, :, e0 : e0 + 128]], axis=0)
                    for part in range(2)
                )
                for half, value in enumerate((u * c - v * w, u * w + v * c)):
                    hi, lo = split(value)
                    spec[b4, pl.ds(at + 64 * half, 64), 128 * j : 128 * j + 128] = hi
                    spec[b4, pl.ds(depth + at + 64 * half, 64), 128 * j : 128 * j + 128] = lo

    def block_at(blk):
        dg, dh = divmod(blk, 2)
        return 2 * lax.rem(g + dg, 2) + lax.rem(h + dh, 2)

    def own_copy(blk, ii):
        return remote(
            own.at[blk, ii], own_in.at[blk - 1, ii], own_s.at[blk - 1, ii], own_r.at[blk - 1, ii],
            peer(blk // 2, 0, blk % 2),
        )

    def msg_copy(blk, i):
        return remote(
            msg.at[blk, i], msg_in.at[blk, i], msg_s.at[blk, i], msg_r.at[blk, i], peer(blk // 2, 1, blk % 2)
        )

    for i in range(AHEAD, 8):
        snd_copy(i).wait_recv()

    def own_rows(ii, carry):
        def one(n, carry):
            spectrum(keep, other, 2 * n + ii, pl.multiple_of(128 * n, 128), 512)
            return carry

        lax.fori_loop(0, 4, one, 0)
        for blk in range(4):
            b4 = block_at(blk)
            total = dot(ww[...], spec[b4]) + dot(w_lo[...], spec[b4, 0:512, :])
            own[blk, ii] = total[0:256]
            pp[blk, ii] = total[256:512]
        for blk in range(1, 4):
            own_copy(blk, ii).start()
        return carry

    lax.fori_loop(0, 2, own_rows, 0)

    def halo_rows(i, carry):
        n, ii = i // 2, lax.rem(i, 2)

        @pl.when(i < 8 - AHEAD)
        def _():
            a_copy(i).wait_send()
            b_copy(i).wait_send()
            a_copy(i + AHEAD).start()
            b_copy(i + AHEAD).start()

        a_copy(i).wait_recv()
        b_copy(i).wait_recv()
        spectrum(halo_a, halo_b, i, 0, 128)
        for blk in range(4):
            b4 = block_at(blk)
            total = dot(wh[n], spec[b4, 0:256, :]) + dot(wh_lo[n], spec[b4, 0:128, :])
            pp[blk, ii] = pp[blk, ii] + total
            msg[blk, i] = pp[blk, ii, pl.ds(pl.multiple_of(64 * n, 64), 64), :]
        for blk in range(4):
            msg_copy(blk, i).start()
        return carry

    lax.fori_loop(0, 8, halo_rows, 0)

    for blk in range(1, 4):
        for ii in range(2):
            own_copy(blk, ii).wait()

    def collect(i, carry):
        n, ii = i // 2, lax.rem(i, 2)
        for blk in range(4):
            msg_copy(blk, i).wait()
        dest = 3 - block_of(n)
        at = pl.ds(pl.multiple_of(64 * dest, 64), 64)
        parts = [
            (own[0, ii, at, :] + own_in[0, ii, at, :]) + (msg_in[0, i] + msg_in[1, i]),
            (own_in[1, ii, at, :] + own_in[2, ii, at, :]) + (msg_in[2, i] + msg_in[3, i]),
        ]
        hi, lo = split(jnp.concatenate(parts, axis=0))
        order = perm[h]
        rows = dot(hi, order) + dot(lo, order)
        for dg in range(2):
            row = 4 * dest + 2 * lax.rem(g + dg, 2) + ii
            for c in range(4):
                by_lane[c][pl.ds(row, 64, stride=16), :] = rows[64 * dg : 64 * dg + 64, 128 * c : 128 * c + 128]
        return carry

    lax.fori_loop(0, 8, collect, 0)
    for c in range(4):
        out[:, 128 * c : 128 * c + 128] = by_lane[c][...]
    for i in range(8):
        snd_copy(i).wait_send()
        if i >= 8 - AHEAD:
            a_copy(i).wait_send()
            b_copy(i).wait_send()


def local(strips, field, spectral_phase, chirp_shift, tile_map, tile_phase):
    freq_rows = jnp.concatenate([chirp_shift.astype(F32)[None], tile_phase, jnp.zeros((3, 32), F32)], axis=0)
    gap = jnp.zeros_like(freq_rows)
    tile_rows = jnp.broadcast_to(tile_map.astype(F32)[:, None], (4, 128))
    prm = jnp.concatenate(
        [jnp.concatenate([freq_rows, gap, freq_rows, gap], axis=1), tile_rows, jnp.zeros((4, 128), F32)], axis=0
    )
    waves, tw = dft_tables()
    vmem = pl.BlockSpec(memory_space=pltpu.VMEM)
    rows = pltpu.VMEM((8, 2, 32, 1024), F32)
    small = pltpu.VMEM((16, 128), F32)
    phase = pltpu.VMEM((2, 32, NY), F32)
    dma = pltpu.SemaphoreType.DMA
    out = pl.pallas_call(
        functools.partial(kernel, strips),
        in_specs=[pl.BlockSpec(memory_space=pl.ANY)] + [vmem] * 4,
        out_specs=vmem,
        out_shape=jax.ShapeDtypeStruct((1024, 512), F32),
        scratch_shapes=[
            pltpu.VMEM((8, 2, 512, 128), F32),
            rows, rows, rows, rows, rows,
            small, small, small,
            phase, phase,
            pltpu.VMEM((2, 512, 512), BF),
            pltpu.VMEM((2, 512, 512), BF),
            pltpu.VMEM((2, 512, 512), BF),
            pltpu.VMEM((512, 1024), BF),
            pltpu.VMEM((512, 512), BF),
            pltpu.VMEM((4, 256, 256), BF),
            pltpu.VMEM((4, 256, 128), BF),
            pltpu.VMEM((2, 256, 512), BF),
            pltpu.VMEM((2, 256, 512), BF),
            pltpu.VMEM((4, 1024, 512), BF),
            pltpu.VMEM((4, 2, 256, 512), F32),
            pltpu.VMEM((3, 2, 256, 512), F32),
            pltpu.VMEM((4, 2, 256, 512), F32),
            pltpu.VMEM((4, 8, 64, 512), F32),
            pltpu.VMEM((4, 8, 64, 512), F32),
            *[pltpu.VMEM((1024, 128), F32)] * 4,
            dma((8,)),
            *[dma((8,))] * 6,
            dma((3,)), dma((3,)),
            dma((3, 2)), dma((3, 2)),
            dma((4, 8)), dma((4, 8)),
        ],
        compiler_params=pltpu.CompilerParams(
            collective_id=0, has_side_effects=True, vmem_limit_bytes=60 * 2**20
        ),
        cost_estimate=pl.CostEstimate(flops=40 * 10**9, bytes_accessed=10 * 2**20, transcendentals=0),
    )(field.reshape(2, 512, 1024), spectral_phase, prm, jnp.asarray(waves), jnp.asarray(tw))
    return out.reshape(2, NT, 16, 512)


def solution(mesh):
    placed = (P(None, "freq", "xs", "yh"), P("freq", None), P("freq"), P("xs"), P(None, "freq"))
    return jax.shard_map(
        functools.partial(local, mesh.shape["xs"]),
        mesh=mesh,
        in_specs=placed,
        out_specs=P(None, None, "xs", ("freq", "yh")),
        check_vma=False,
    )
```

```python
import functools
import math

import jax
import jax.numpy as jnp
import numpy as np
from jax import lax
from jax.experimental import pallas as pl
from jax.experimental.pallas import tpu as pltpu
from jax.sharding import PartitionSpec as P

NF = 64
NY = 2048
NT = 32
BF = jnp.bfloat16
F32 = jnp.float32
AXES = ("freq", "xs", "yh")
MESH = pl.DeviceIdType.MESH


def dft_tables():
    m = np.arange(256)
    angle = 2.0 * np.pi * (np.outer(m, m) % 256) / 256
    waves = np.stack([np.cos(angle), np.sin(angle)]) / math.sqrt(NY)
    odd_order = np.concatenate([np.arange(64) + 64 * b for b in (1, 0, 3, 2)])
    turn = 2.0 * np.pi * np.outer(np.arange(8), m) / NY
    twiddle = np.stack([np.cos(turn), np.sin(turn)])
    return np.stack([waves, waves[:, :, odd_order]]).astype(np.float32), twiddle.astype(np.float32)


def split(value):
    high = value.astype(BF)
    return high, (value - high.astype(F32)).astype(BF)


def dot(a, b):
    return jnp.dot(a, b, preferred_element_type=F32)


def dot_t(a, b):
    return lax.dot_general(a, b, (((1,), (1,)), ((), ())), preferred_element_type=F32)


def butterflies(re, im, tw):
    a = [(re[:, 256 * c : 256 * c + 256], im[:, 256 * c : 256 * c + 256]) for c in range(4)]
    r = math.sqrt(0.5)

    def add(u, v):
        return u[0] + v[0], u[1] + v[1]

    def sub(u, v):
        return u[0] - v[0], u[1] - v[1]

    def mi(u):
        return u[1], -u[0]

    def four(b):
        e0, e1 = add(b[0], b[2]), sub(b[0], b[2])
        e2, e3 = add(b[1], b[3]), mi(sub(b[1], b[3]))
        return add(e0, e2), add(e1, e3), sub(e0, e2), sub(e1, e3)

    even = four(a)
    b1 = ((a[1][0] + a[1][1]) * r, (a[1][1] - a[1][0]) * r)
    b3 = ((a[3][1] - a[3][0]) * r, (-a[3][0] - a[3][1]) * r)
    odd = four((a[0], b1, mi(a[2]), b3))
    both = []
    for side, parts in enumerate((even, odd)):
        row = []
        for j in range(4):
            p = 2 * j + side
            u = parts[j]
            if p:
                c, s = tw[0, p : p + 1, :], tw[1, p : p + 1, :]
                u = u[0] * c + u[1] * s, u[1] * c - u[0] * s
            row.append(u)
        both.append(row)
    return both


def kernel(
    strips, field, phi_hbm, waves_hbm, tw_hbm, shift_row, tile_phase, tile_ids, out,
    flat, snd, keep, other, halo_a, halo_b, prm, prm_out, prm_in, prm_pair,
    phi, waves, tw, e_own, e_other, t_hi, t_lo, perm, ww, w_lo, wh, wh_lo,
    l_hi, l_lo, spec, near, near_in, side, side_in, pp, opp, relay_in, cross, cross_in, *rest,
):
    by_lane = rest[:4]
    (load_sem, snd_s, snd_r, ha_s, ha_r, hb_s, hb_r, prm_s, prm_r,
     near_s, near_r, row_s, row_r, all_s, all_r, rel_s, rel_r, crs_s, crs_r) = rest[4:]
    g, s, h = (lax.axis_index(a) for a in AXES)
    odd = lax.rem(s, 2)
    pair = s + 1 - 2 * odd
    onward = lax.rem(s + strips + 4 * odd - 2, strips)
    back = lax.rem(s + strips + 2 - 4 * odd, strips)
    core = (1 - g, s, h)

    def peer(dg, ds, dh):
        return (lax.rem(g + dg, 2), pair if ds else s, lax.rem(h + dh, 2))

    def remote(src, dst, a, b, to):
        return pltpu.make_async_remote_copy(
            src_ref=src, dst_ref=dst, send_sem=a, recv_sem=b, device_id=to, device_id_type=MESH
        )

    def block_of(n):
        return n + odd * (3 - 2 * n)

    loads = [
        pltpu.make_async_copy(field.at[:, :, pl.ds(128 * y, 128)], flat.at[y], load_sem.at[y]) for y in range(8)
    ]
    tables = [
        pltpu.make_async_copy(src, dst, load_sem.at[8 + k])
        for k, (src, dst) in enumerate(((waves_hbm, waves), (tw_hbm, tw), (phi_hbm, phi)))
    ]
    for c in loads + tables:
        c.start()
    barrier = pltpu.get_barrier_semaphore()
    greet = [core, peer(0, 0, 1), peer(1, 0, 1), peer(0, 1, 1), peer(1, 1, 1), (g, onward, h), (g, back, h)]
    for to in greet:
        pl.semaphore_signal(barrier, inc=1, device_id=to, device_id_type=MESH)

    def snd_copy(i):
        return remote(snd.at[i], other.at[i], snd_s.at[i], snd_r.at[i], core)

    def a_copy(i):
        return remote(keep.at[i], halo_a.at[i], ha_s.at[i], ha_r.at[i], (g, onward, h))

    def b_copy(i):
        return remote(other.at[i], halo_b.at[i], hb_s.at[i], hb_r.at[i], (g, onward, h))

    def gather_rows(i, whose, into):
        row = 4 * block_of(lax.rem(i, 4)) + 2 * whose + i // 4
        for c in range(2):
            for y in range(8):
                into[i, c, :, 128 * y : 128 * y + 128] = flat[y, c, pl.ds(row, 32, stride=16), :]

    gap = jnp.zeros((8, 32), F32)
    rows = jnp.concatenate([shift_row[...].astype(F32), tile_phase[...], jnp.zeros((3, 32), F32)], axis=0)
    prm[0:8, :] = jnp.concatenate([rows, gap, rows, gap], axis=1)
    for rb in range(4):
        prm[8 + rb : 9 + rb, :] = jnp.full((1, 128), tile_ids[rb], jnp.int32).astype(F32)
    prm[12:16, :] = jnp.zeros((4, 128), F32)
    prm_out[...] = pltpu.roll(prm[...], 32, 1)
    prm_core = remote(prm_out, prm_in, prm_s.at[0], prm_r.at[0], core)
    prm_strip = remote(prm, prm_pair, prm_s.at[1], prm_r.at[1], peer(0, 1, 1))

    for c in loads:
        c.wait()

    def pack_first(i, carry):
        gather_rows(i, g, keep)
        return carry

    def pack_send(i, carry):
        gather_rows(i, 1 - g, snd)
        snd_copy(i).start()
        return carry

    def pack_keep(i, carry):
        gather_rows(i, g, keep)
        return carry

    lax.fori_loop(0, 2, pack_first, 0)
    pl.semaphore_wait(barrier, len(greet))
    a_copy(0).start()
    a_copy(1).start()
    lax.fori_loop(0, 8, pack_send, 0)
    prm_core.start()
    prm_strip.start()
    lax.fori_loop(2, 8, pack_keep, 0)
    for i in range(2):
        snd_copy(i).wait_recv()
        b_copy(i).start()

    for c in tables:
        c.wait()
    lane = lax.broadcasted_iota(jnp.int32, (512, 512), 0)
    wave = lax.broadcasted_iota(jnp.int32, (512, 512), 1)
    turn = lax.rem(lane, 128)
    for half in range(2):
        late = (turn >= 64).astype(jnp.int32)
        late = late if half == 0 else 1 - late
        perm[half] = (8 * lax.rem(turn, 64) + 2 * (lane // 128) + late == wave).astype(F32).astype(BF)
        c_hi, c_lo = split(waves[half, 0])
        s_hi, s_lo = split(waves[half, 1])
        for table, c, w in ((t_hi, c_hi, s_hi), (t_lo, c_lo, s_lo)):
            table[half, 0:256, 0:256] = c
            table[half, 0:256, 256:512] = -w
            table[half, 256:512, 0:256] = w
            table[half, 256:512, 256:512] = c

    lanes = lax.rem(lax.broadcasted_iota(jnp.int32, (1, 512), 1), 128)
    for b in range(4):
        x = phi[:, 512 * b : 512 * b + 512]
        late = lanes >= 64 if b % 2 == 0 else lanes < 64
        sign = 1.0 - 2.0 * jnp.where(late, h, 0).astype(F32)
        for part, value in enumerate((jnp.cos(x), jnp.sin(x))):
            hi, lo = split(value)
            e_own[part, :, 512 * b : 512 * b + 512] = (dot_t(hi, perm[b % 2]) + dot_t(lo, perm[b % 2])) * sign
    e_copy = remote(e_own, e_other, prm_s.at[2], prm_r.at[2], core)
    e_copy.start()

    prm_core.wait()
    prm_strip.wait()
    both = prm[...] + prm_in[...]
    shift = both[0:1, :]
    col = lax.broadcasted_iota(jnp.int32, (NT, 128), 1)
    freq = lax.rem(lax.rem(col, 64) + 32 * g, NF)
    angle = (2.0 * math.pi / NF) * lax.rem(lax.broadcasted_iota(jnp.int32, (NT, 128), 0) * freq, NF).astype(F32)
    scale = 1.0 / math.sqrt(NF)
    real_in = col < 64

    def base(tile):
        phase = jnp.zeros((1, 128), F32)
        for t in range(4):
            phase = phase + jnp.where(tile == float(t), both[1 + t : 2 + t, :], 0.0)
        re, im = jnp.cos(angle + phase) * scale, jnp.sin(angle + phase) * scale
        return jnp.concatenate([jnp.where(real_in, re, -im), jnp.where(real_in, im, re)], axis=0)

    far = (4 * (1 - 2 * odd)).astype(F32)
    inside = jnp.where(odd == 1, (s > 1).astype(F32), (s < strips - 2).astype(F32))
    for nd in range(4):
        dest = block_of(nd)
        here, there = base(prm[8 + nd : 9 + nd, :]), base(prm_pair[pl.ds(8 + dest, 1), :])
        rows = slice(64 * nd, 64 * nd + 64)
        for n in range(4):
            source = block_of(n)
            own_hi, own_lo = split(jnp.where(shift == (nd - source).astype(F32), here, 0.0))
            step = (dest - source).astype(F32)
            pair_hi, pair_lo = split(jnp.where(shift == step + far, there, 0.0))
            halo_hi, halo_lo = split(jnp.where(shift == step - far, there * inside, 0.0))
            at = 128 * n
            below = slice(256 + 64 * nd, 320 + 64 * nd)
            ww[rows, at : at + 128] = own_hi
            ww[rows, 512 + at : 640 + at] = own_hi
            w_lo[rows, at : at + 128] = own_lo
            ww[below, at : at + 128] = pair_hi
            ww[below, 512 + at : 640 + at] = pair_hi
            w_lo[below, at : at + 128] = pair_lo
            wh[n, rows, 0:128] = halo_hi
            wh[n, rows, 128:256] = halo_hi
            wh_lo[n, rows, :] = halo_lo
    e_copy.wait()

    def spectrum(a, b, i, at, depth):
        re = jnp.concatenate([a[i, 0], b[i, 0]], axis=0)
        im = jnp.concatenate([a[i, 1], b[i, 1]], axis=0)
        for half_p, parts in enumerate(butterflies(re, im, tw)):
            for j, pieces in enumerate(parts):
                for half, w in enumerate(pieces):
                    hi, lo = split(w)
                    l_hi[half_p, 64 * j : 64 * j + 64, 256 * half : 256 * half + 256] = hi
                    l_lo[half_p, 64 * j : 64 * j + 64, 256 * half : 256 * half + 256] = lo
        even, uneven = (
            dot(l_hi[k], t_hi[k]) + dot(l_lo[k], t_hi[k]) + dot(l_hi[k], t_lo[k]) for k in range(2)
        )
        early = lax.broadcasted_iota(jnp.int32, (64, 128), 1) < 64
        for j in range(4):
            for b4 in range(4):
                first, second = (even, uneven) if b4 % 2 == 0 else (uneven, even)
                rows = slice(64 * j, 64 * j + 64)
                c0 = 128 * (b4 // 2)
                u = jnp.where(early, first[rows, c0 : c0 + 128], second[rows, c0 : c0 + 128])
                v = jnp.where(early, first[rows, 256 + c0 : 384 + c0], second[rows, 256 + c0 : 384 + c0])
                e0 = 512 * b4 + 128 * j
                c, w = (
                    jnp.concatenate([e_own[part, :, e0 : e0 + 128], e_other[part, :, e0 : e0 + 128]], axis=0)
                    for part in range(2)
                )
                for half, value in enumerate((u * c - v * w, u * w + v * c)):
                    hi, lo = split(value)
                    spec[b4, pl.ds(at + 64 * half, 64), 128 * j : 128 * j + 128] = hi
                    spec[b4, pl.ds(depth + at + 64 * half, 64), 128 * j : 128 * j + 128] = lo

    def block_at(dg, dh):
        return 2 * lax.rem(g + dg, 2) + lax.rem(h + dh, 2)

    def near_copy(ii):
        return remote(near.at[1, ii], near_in.at[ii], near_s.at[ii], near_r.at[ii], core)

    def dest_rows(n):
        return pl.ds(pl.multiple_of(64 * (3 - block_of(n)), 64), 64)

    def row_copy(dg, n):
        at = dest_rows(n)
        return remote(side.at[dg, 0, at], side_in.at[dg, 0, at], row_s.at[dg, n], row_r.at[dg, n], peer(dg, 0, 1))

    def all_copy(dg):
        return remote(side.at[dg, 1], side_in.at[dg, 1], all_s.at[dg], all_r.at[dg], peer(dg, 0, 1))

    def opp_cross(i):
        return remote(opp.at[i], relay_in.at[i], rel_s.at[i], rel_r.at[i], peer(0, 1, 1))

    def opp_direct(i):
        return remote(opp.at[i], relay_in.at[i], rel_s.at[i], rel_r.at[i], peer(0, 0, 1))

    def cross_copy(dg, i):
        return remote(cross.at[dg, i], cross_in.at[dg, i], crs_s.at[dg, i], crs_r.at[dg, i], peer(dg, 1, 1))

    for i in range(2, 8):
        snd_copy(i).wait_recv()

    def own_rows(ii):
        def one(n, carry):
            @pl.when(jnp.logical_and(ii == 0, n == 2))
            def _():
                a_copy(2).start()
                b_copy(2).start()

            spectrum(keep, other, 4 * ii + n, pl.multiple_of(128 * n, 128), 512)
            return carry

        lax.fori_loop(0, 4, one, 0)
        for dg in range(2):
            for dh in range(2):
                b4 = block_at(dg, dh)
                total = dot(ww[...], spec[b4]) + dot(w_lo[...], spec[b4, 0:512, :])
                if dh == 0:
                    near[dg, ii] = total[0:256]
                else:
                    side[dg, ii] = total[0:256]
                pp[2 * dg + dh, ii] = total[256:512]
        near_copy(ii).start()

    def collect(i):
        n, ii = lax.rem(i, 4), i // 4
        at = dest_rows(n)
        for dg in range(2):
            cross_copy(dg, i).wait()
        parts = [
            near[0, ii, at, :] + side_in[0, ii, at, :] + cross_in[0, i],
            near_in[ii, at, :] + side_in[1, ii, at, :] + cross_in[1, i],
        ]
        hi, lo = split(jnp.concatenate(parts, axis=0))
        order = perm[h]
        rows = dot(hi, order) + dot(lo, order)
        for dg in range(2):
            row = 4 * (3 - block_of(n)) + 2 * lax.rem(g + dg, 2) + ii
            for c in range(4):
                by_lane[c][pl.ds(row, 64, stride=16), :] = rows[64 * dg : 64 * dg + 64, 128 * c : 128 * c + 128]

    def step(i, carry):
        n, ii = lax.rem(i, 4), i // 4

        @pl.when(jnp.logical_or(i == 0, i == 3))
        def _():
            own_rows(i // 3)

            @pl.when(i == 3)
            def _():
                for dg in range(2):
                    all_copy(dg).start()

        a_copy(i).wait_recv()
        b_copy(i).wait_recv()

        @pl.when(i < 5)
        def _():
            a_copy(i).wait_send()
            b_copy(i).wait_send()
            a_copy(i + 3).start()
            b_copy(i + 3).start()

        spectrum(halo_a, halo_b, i, 0, 128)
        mine = pl.ds(pl.multiple_of(64 * n, 64), 64)
        for dh in range(2):
            for dg in range(2):
                b4 = block_at(dg, dh)
                total = dot(wh[n], spec[b4, 0:256, :]) + dot(wh_lo[n], spec[b4, 0:128, :])
                pp[2 * dg + dh, ii] = pp[2 * dg + dh, ii] + total
                if dh == 0:
                    opp[i, dg] = pp[2 * dg, ii, mine, :]
                else:
                    cross[dg, i] = pp[2 * dg + 1, ii, mine, :]
            if dh == 0:

                @pl.when(i < 4)
                def _():
                    opp_cross(i).start()

                @pl.when(i >= 4)
                def _():
                    opp_direct(i).start()

        @pl.when(i < 4)
        def _():
            for dg in range(2):
                cross_copy(dg, i).start()

        @pl.when(jnp.logical_and(i >= 1, i < 5))
        def _():
            opp_cross(i - 1).wait()
            at = dest_rows(i - 1)
            for dg in range(2):
                side[dg, 0, at, :] = side[dg, 0, at, :] + relay_in[i - 1, dg]
                row_copy(dg, i - 1).start()

        @pl.when(i >= 5)
        def _():
            forward(i - 1)

        @pl.when(i >= 4)
        def _():
            @pl.when(i == 4)
            def _():
                near_copy(0).wait()

            for dg in range(2):
                row_copy(dg, i - 4).wait()
            collect(i - 4)

        return carry

    def forward(i):
        opp_direct(i).wait()
        for dg in range(2):
            cross[dg, i] = cross[dg, i] + relay_in[i, dg]
            cross_copy(dg, i).start()

    lax.fori_loop(0, 8, step, 0)
    forward(7)
    near_copy(1).wait()
    for dg in range(2):
        all_copy(dg).wait()

    def last(i, carry):
        collect(i)
        return carry

    lax.fori_loop(4, 8, last, 0)
    results = [
        pltpu.make_async_copy(by_lane[c], out.at[:, pl.ds(128 * c, 128)], load_sem.at[c]) for c in range(4)
    ]
    for c in results:
        c.start()
    for i in range(8):
        snd_copy(i).wait_send()
        if i >= 5:
            a_copy(i).wait_send()
            b_copy(i).wait_send()
    for c in results:
        c.wait()


def local(strips, field, spectral_phase, chirp_shift, tile_map, tile_phase):
    waves, tw = dft_tables()
    vmem = pl.BlockSpec(memory_space=pltpu.VMEM)
    hbm = pl.BlockSpec(memory_space=pl.ANY)
    rows = pltpu.VMEM((8, 2, 32, 1024), F32)
    small = pltpu.VMEM((16, 128), F32)
    phase = pltpu.VMEM((2, 32, NY), F32)
    sums = pltpu.VMEM((2, 2, 256, 512), F32)
    dma = pltpu.SemaphoreType.DMA
    out = pl.pallas_call(
        functools.partial(kernel, strips),
        in_specs=[hbm, hbm, hbm, hbm, vmem, vmem, pl.BlockSpec(memory_space=pltpu.SMEM)],
        out_specs=hbm,
        out_shape=jax.ShapeDtypeStruct((1024, 512), F32),
        scratch_shapes=[
            pltpu.VMEM((8, 2, 512, 128), F32),
            rows, rows, rows, rows, rows,
            small, small, small, small,
            pltpu.VMEM((32, NY), F32),
            pltpu.VMEM(waves.shape, F32),
            pltpu.VMEM(tw.shape, F32),
            phase, phase,
            pltpu.VMEM((2, 512, 512), BF),
            pltpu.VMEM((2, 512, 512), BF),
            pltpu.VMEM((2, 512, 512), BF),
            pltpu.VMEM((512, 1024), BF),
            pltpu.VMEM((512, 512), BF),
            pltpu.VMEM((4, 256, 256), BF),
            pltpu.VMEM((4, 256, 128), BF),
            pltpu.VMEM((2, 256, 512), BF),
            pltpu.VMEM((2, 256, 512), BF),
            pltpu.VMEM((4, 1024, 512), BF),
            sums,
            pltpu.VMEM((2, 256, 512), F32),
            sums, sums,
            pltpu.VMEM((4, 2, 256, 512), F32),
            pltpu.VMEM((8, 2, 64, 512), F32),
            pltpu.VMEM((8, 2, 64, 512), F32),
            pltpu.VMEM((2, 8, 64, 512), F32),
            pltpu.VMEM((2, 8, 64, 512), F32),
            *[pltpu.VMEM((1024, 128), F32)] * 4,
            dma((11,)),
            *[dma((8,))] * 6,
            dma((3,)), dma((3,)),
            dma((2,)), dma((2,)),
            dma((2, 4)), dma((2, 4)),
            dma((2,)), dma((2,)),
            dma((8,)), dma((8,)),
            dma((2, 8)), dma((2, 8)),
        ],
        compiler_params=pltpu.CompilerParams(
            collective_id=0, has_side_effects=True, vmem_limit_bytes=60 * 2**20
        ),
        cost_estimate=pl.CostEstimate(flops=40 * 10**9, bytes_accessed=10 * 2**20, transcendentals=0),
    )(
        field.reshape(2, 512, 1024), spectral_phase, jnp.asarray(waves), jnp.asarray(tw),
        chirp_shift.reshape(1, 32), tile_phase, tile_map,
    )
    return out.reshape(2, NT, 16, 512)


def solution(mesh):
    placed = (P(None, "freq", "xs", "yh"), P("freq", None), P("freq"), P("xs"), P(None, "freq"))
    return jax.shard_map(
        functools.partial(local, mesh.shape["xs"]),
        mesh=mesh,
        in_specs=placed,
        out_specs=P(None, None, "xs", ("freq", "yh")),
        check_vma=False,
    )
```

```python
import functools
import math

import jax
import jax.numpy as jnp
import numpy as np
from jax import lax
from jax.experimental import pallas as pl
from jax.experimental.pallas import tpu as pltpu
from jax.sharding import PartitionSpec as P

NF = 64
NY = 2048
NT = 32
VMEM = 58
BF = jnp.bfloat16
F32 = jnp.float32
AXES = ("freq", "xs", "yh")
MESH = pl.DeviceIdType.MESH


def dft_tables():
    m = np.arange(256)
    angle = 2.0 * np.pi * (np.outer(m, m) % 256) / 256
    waves = np.stack([np.cos(angle), np.sin(angle)]) / math.sqrt(NY)
    odd_order = np.concatenate([np.arange(64) + 64 * b for b in (1, 0, 3, 2)])
    turn = 2.0 * np.pi * np.outer(np.arange(8), m) / NY
    twiddle = np.stack([np.cos(turn), np.sin(turn)])
    return np.stack([waves, waves[:, :, odd_order]]).astype(np.float32), twiddle.astype(np.float32)


def split(value):
    high = value.astype(BF)
    return high, (value - high.astype(F32)).astype(BF)


def dot(a, b):
    return jnp.dot(a, b, preferred_element_type=F32)


def dot_t(a, b):
    return lax.dot_general(a, b, (((1,), (1,)), ((), ())), preferred_element_type=F32)


def sincos(x):
    k = jnp.floor(x * (2.0 / math.pi) + 0.5)
    r = ((x - k * 1.5703125) - k * 4.837512969970703125e-4) - k * 7.54978995489188216e-8
    z = r * r
    sine = r + r * z * (-1.6666654611e-1 + z * (8.3321608736e-3 - z * 1.9515295891e-4))
    cosine = (1.0 - 0.5 * z) + z * z * (4.166664568298827e-2 + z * (-1.388731625493765e-3 + z * 2.443315711809948e-5))
    half = jnp.floor(k * 0.5)
    swap = (k - 2.0 * half) > 0.5
    sign = 1.0 - 2.0 * (half - 2.0 * jnp.floor(half * 0.5))
    return sign * jnp.where(swap, cosine, sine), sign * jnp.where(swap, -sine, cosine)


def butterflies(re, im, tw):
    a = [(re[:, 256 * c : 256 * c + 256], im[:, 256 * c : 256 * c + 256]) for c in range(4)]
    r = math.sqrt(0.5)

    def add(u, v):
        return u[0] + v[0], u[1] + v[1]

    def sub(u, v):
        return u[0] - v[0], u[1] - v[1]

    def mi(u):
        return u[1], -u[0]

    def four(b):
        e0, e1 = add(b[0], b[2]), sub(b[0], b[2])
        e2, e3 = add(b[1], b[3]), mi(sub(b[1], b[3]))
        return add(e0, e2), add(e1, e3), sub(e0, e2), sub(e1, e3)

    even = four(a)
    b1 = ((a[1][0] + a[1][1]) * r, (a[1][1] - a[1][0]) * r)
    b3 = ((a[3][1] - a[3][0]) * r, (-a[3][0] - a[3][1]) * r)
    odd = four((a[0], b1, mi(a[2]), b3))
    both = []
    for side, parts in enumerate((even, odd)):
        row = []
        for j in range(4):
            p = 2 * j + side
            u = parts[j]
            if p:
                c, s = tw[0, p : p + 1, :], tw[1, p : p + 1, :]
                u = u[0] * c + u[1] * s, u[1] * c - u[0] * s
            row.append(u)
        both.append(row)
    return both


def kernel(
    strips, field, phi_hbm, waves_hbm, tw_hbm, shift_row, tile_phase, tile_ids, out,
    flat, snd, keep, other, halo_a, halo_b, prm, prm_out, prm_in, prm_pair,
    phi, waves, tw, e_own, e_other, t_hi, t_lo, perm, ww, w_lo, wh, wh_lo,
    l_hi, l_lo, spec, near, near_in, side, side_in, pp, opp, relay_in, cross, cross_in, via_1, via_2, *rest,
):
    by_lane = rest[:4]
    (load_sem, snd_s, snd_r, ha_s, ha_r, hb_s, hb_r, prm_s, prm_r,
     near_s, near_r, row_s, row_r, rel_s, rel_r, crs_s, crs_r, v1_s, v1_r, v2_s, v2_r) = rest[4:]
    g, s, h = (lax.axis_index(a) for a in AXES)
    odd = lax.rem(s, 2)
    pair = s + 1 - 2 * odd
    onward = lax.rem(s + strips + 4 * odd - 2, strips)
    back = lax.rem(s + strips + 2 - 4 * odd, strips)
    core = (1 - g, s, h)

    z, y, turns = s // 8, lax.rem(s // 2, 4), strips // 8
    hop = 1 - 2 * odd
    across = 8 * z + 2 * lax.rem(y + 4 + hop, 4) + odd
    across_from = 8 * z + 2 * lax.rem(y + 4 - hop, 4) + odd
    z_on = 8 * lax.rem(z + turns - hop, turns) + odd
    z_back = 8 * lax.rem(z + turns + hop, turns) + odd
    leaves = (y == 2 - odd).astype(jnp.int32)
    third = across + leaves * (z_on + 2 * (3 - 3 * odd) - across)
    enters = (y == 3 - 3 * odd).astype(jnp.int32)
    third_from = across_from + enters * (z_back + 2 * (2 - odd) - across_from)

    def peer(dg, ds, dh):
        return (lax.rem(g + dg, 2), pair if ds else s, lax.rem(h + dh, 2))

    def remote(src, dst, a, b, to):
        return pltpu.make_async_remote_copy(
            src_ref=src, dst_ref=dst, send_sem=a, recv_sem=b, device_id=to, device_id_type=MESH
        )

    def block_of(n):
        return n + odd * (3 - 2 * n)

    loads = [
        pltpu.make_async_copy(field.at[:, :, pl.ds(128 * y, 128)], flat.at[y], load_sem.at[y]) for y in range(8)
    ]
    tables = [
        pltpu.make_async_copy(src, dst, load_sem.at[8 + k])
        for k, (src, dst) in enumerate(((waves_hbm, waves), (tw_hbm, tw), (phi_hbm, phi)))
    ]
    for c in loads + tables:
        c.start()
    barrier = pltpu.get_barrier_semaphore()
    greet = [core, peer(0, 0, 1), peer(1, 0, 1), peer(0, 1, 1), peer(1, 1, 1), (g, onward, h), (g, back, h)]
    greet += [(g, across, h), (g, across_from, h), (g, third, h), (g, third_from, h)]
    for to in greet:
        pl.semaphore_signal(barrier, inc=1, device_id=to, device_id_type=MESH)

    def snd_copy(i):
        return remote(snd.at[i], other.at[i], snd_s.at[i], snd_r.at[i], core)

    def a_copy(i):
        return remote(keep.at[i], halo_a.at[i], ha_s.at[i], ha_r.at[i], (g, onward, h))

    def b_copy(i):
        return remote(other.at[i], halo_b.at[i], hb_s.at[i], hb_r.at[i], (g, onward, h))

    def via_copy(hops, k, which):
        i = 4 + 3 * k
        if hops == 1:
            src = (keep, other)[which].at[i]
            return remote(src, via_1.at[k, which], v1_s.at[k, which], v1_r.at[k, which], (g, across, h))
        if hops == 2:
            return remote(
                via_1.at[k, which], via_2.at[k, which], v2_s.at[k, which], v2_r.at[k, which], (g, across, h)
            )
        dst, sems = ((halo_a, (ha_s, ha_r)), (halo_b, (hb_s, hb_r)))[which]
        return remote(via_2.at[k, which], dst.at[i], sems[0].at[i], sems[1].at[i], (g, third, h))

    def pass_on(hops, k):
        for which in range(2):
            via_copy(hops - 1, k, which).wait_recv()
            via_copy(hops, k, which).start()

    def gather_rows(i, whose, into):
        row = 4 * block_of(lax.rem(i, 4)) + 2 * whose + i // 4
        for c in range(2):
            for y in range(8):
                into[i, c, :, 128 * y : 128 * y + 128] = flat[y, c, pl.ds(row, 32, stride=16), :]

    gap = jnp.zeros((8, 32), F32)
    rows = jnp.concatenate([shift_row[...].astype(F32), tile_phase[...], jnp.zeros((3, 32), F32)], axis=0)
    prm[0:8, :] = jnp.concatenate([rows, gap, rows, gap], axis=1)
    for rb in range(4):
        prm[8 + rb : 9 + rb, :] = jnp.full((1, 128), tile_ids[rb], jnp.int32).astype(F32)
    prm[12:16, :] = jnp.zeros((4, 128), F32)
    prm_out[...] = pltpu.roll(prm[...], 32, 1)
    prm_core = remote(prm_out, prm_in, prm_s.at[0], prm_r.at[0], core)
    prm_strip = remote(prm, prm_pair, prm_s.at[1], prm_r.at[1], peer(0, 1, 1))

    for c in loads:
        c.wait()

    def pack_send(i, carry):
        gather_rows(i, 1 - g, snd)
        snd_copy(i).start()
        return carry

    def pack_keep(i, carry):
        gather_rows(i, g, keep)
        return carry

    for i in (0, 4, 1):
        gather_rows(i, g, keep)
    pl.semaphore_wait(barrier, len(greet))
    a_copy(0).start()
    via_copy(1, 0, 0).start()
    a_copy(1).start()
    lax.fori_loop(0, 8, pack_send, 0)
    prm_core.start()
    prm_strip.start()
    lax.fori_loop(2, 4, pack_keep, 0)
    lax.fori_loop(5, 8, pack_keep, 0)
    for i in (0, 4, 1):
        snd_copy(i).wait_recv()
        if i == 4:
            via_copy(1, 0, 1).start()
        else:
            b_copy(i).start()

    for c in tables:
        c.wait()
    lane = lax.broadcasted_iota(jnp.int32, (512, 1), 0)
    wave = lax.broadcasted_iota(jnp.int32, (1, 512), 1)
    turn = lax.rem(lane, 128)
    for half in range(2):
        late = (turn >= 64).astype(jnp.int32)
        late = late if half == 0 else 1 - late
        target = 8 * lax.rem(turn, 64) + 2 * (lane // 128) + late
        perm[half] = jnp.where(target == wave, 1.0, 0.0).astype(BF)
        c_hi, c_lo = split(waves[half, 0])
        s_hi, s_lo = split(waves[half, 1])
        for table, c, w in ((t_hi, c_hi, s_hi), (t_lo, c_lo, s_lo)):
            table[half, 0:256, 0:256] = c
            table[half, 0:256, 256:512] = -w
            table[half, 256:512, 0:256] = w
            table[half, 256:512, 256:512] = c

    lanes = lax.rem(lax.broadcasted_iota(jnp.int32, (1, 512), 1), 128)
    for half in range(2):
        late = lanes >= 64 if half == 0 else lanes < 64
        sign = 1.0 - 2.0 * jnp.where(late, h, 0).astype(F32)
        stack = []
        for b in (half, half + 2):
            sine, cosine = sincos(phi[:, 512 * b : 512 * b + 512])
            stack += [*split(cosine), *split(sine)]
        got = dot_t(jnp.concatenate(stack, axis=0), perm[half])
        for k, b in enumerate((half, half + 2)):
            for part in range(2):
                at = 128 * k + 64 * part
                e_own[part, :, 512 * b : 512 * b + 512] = (got[at : at + 32] + got[at + 32 : at + 64]) * sign
    e_copy = remote(e_own, e_other, prm_s.at[2], prm_r.at[2], core)
    e_copy.start()

    prm_core.wait()
    prm_strip.wait()
    both = prm[...] + prm_in[...]
    shift = both[0:1, :]
    col = lax.broadcasted_iota(jnp.int32, (NT, 128), 1)
    freq = lax.rem(lax.rem(col, 64) + 32 * g, NF)
    angle = (2.0 * math.pi / NF) * lax.rem(lax.broadcasted_iota(jnp.int32, (NT, 128), 0) * freq, NF).astype(F32)
    scale = 1.0 / math.sqrt(NF)
    real_in = col < 64

    def base(tile):
        phase = jnp.zeros((1, 128), F32)
        for t in range(4):
            phase = phase + jnp.where(tile == float(t), both[1 + t : 2 + t, :], 0.0)
        im, re = sincos(angle + phase)
        im, re = im * scale, re * scale
        return jnp.concatenate([jnp.where(real_in, re, -im), jnp.where(real_in, im, re)], axis=0)

    far = (4 * (1 - 2 * odd)).astype(F32)
    inside = jnp.where(odd == 1, (s > 1).astype(F32), (s < strips - 2).astype(F32))
    for nd in range(4):
        dest = block_of(nd)
        here, there = base(prm[8 + nd : 9 + nd, :]), base(prm_pair[pl.ds(8 + dest, 1), :])
        rows = slice(64 * nd, 64 * nd + 64)
        for n in range(4):
            source = block_of(n)
            own_hi, own_lo = split(jnp.where(shift == (nd - source).astype(F32), here, 0.0))
            step = (dest - source).astype(F32)
            pair_hi, pair_lo = split(jnp.where(shift == step + far, there, 0.0))
            halo_hi, halo_lo = split(jnp.where(shift == step - far, there * inside, 0.0))
            at = 128 * n
            below = slice(256 + 64 * nd, 320 + 64 * nd)
            ww[rows, at : at + 128] = own_hi
            ww[rows, 512 + at : 640 + at] = own_hi
            w_lo[rows, at : at + 128] = own_lo
            ww[below, at : at + 128] = pair_hi
            ww[below, 512 + at : 640 + at] = pair_hi
            w_lo[below, at : at + 128] = pair_lo
            wh[n, rows, 0:128] = halo_hi
            wh[n, rows, 128:256] = halo_hi
            wh_lo[n, rows, :] = halo_lo
    for i in (2, 3, 5, 6, 7):
        snd_copy(i).wait_recv()
    pass_on(2, 0)
    for which in range(2):
        via_copy(1, 1, which).start()
    e_copy.wait()

    def spectrum(a, b, i, at, depth):
        re = jnp.concatenate([a[i, 0], b[i, 0]], axis=0)
        im = jnp.concatenate([a[i, 1], b[i, 1]], axis=0)
        for half_p, parts in enumerate(butterflies(re, im, tw)):
            for j, pieces in enumerate(parts):
                for half, w in enumerate(pieces):
                    hi, lo = split(w)
                    l_hi[half_p, 64 * j : 64 * j + 64, 256 * half : 256 * half + 256] = hi
                    l_lo[half_p, 64 * j : 64 * j + 64, 256 * half : 256 * half + 256] = lo
        even, uneven = (
            dot(l_hi[k], t_hi[k]) + dot(l_lo[k], t_hi[k]) + dot(l_hi[k], t_lo[k]) for k in range(2)
        )
        early = lax.broadcasted_iota(jnp.int32, (64, 128), 1) < 64
        for j in range(4):
            for b4 in range(4):
                first, second = (even, uneven) if b4 % 2 == 0 else (uneven, even)
                rows = slice(64 * j, 64 * j + 64)
                c0 = 128 * (b4 // 2)
                u = jnp.where(early, first[rows, c0 : c0 + 128], second[rows, c0 : c0 + 128])
                v = jnp.where(early, first[rows, 256 + c0 : 384 + c0], second[rows, 256 + c0 : 384 + c0])
                e0 = 512 * b4 + 128 * j
                c, w = (
                    jnp.concatenate([e_own[part, :, e0 : e0 + 128], e_other[part, :, e0 : e0 + 128]], axis=0)
                    for part in range(2)
                )
                for half, value in enumerate((u * c - v * w, u * w + v * c)):
                    hi, lo = split(value)
                    spec[b4, pl.ds(at + 64 * half, 64), 128 * j : 128 * j + 128] = hi
                    spec[b4, pl.ds(depth + at + 64 * half, 64), 128 * j : 128 * j + 128] = lo

    def block_at(dg, dh):
        return 2 * lax.rem(g + dg, 2) + lax.rem(h + dh, 2)

    def near_copy(ii):
        return remote(near.at[1, ii], near_in.at[ii], near_s.at[ii], near_r.at[ii], core)

    def dest_rows(n):
        return pl.ds(pl.multiple_of(64 * (3 - block_of(n)), 64), 64)

    def row_copy(dg, i):
        at, ii = dest_rows(lax.rem(i, 4)), i // 4
        return remote(side.at[dg, ii, at], side_in.at[dg, ii, at], row_s.at[dg, i], row_r.at[dg, i], peer(dg, 0, 1))

    def opp_cross(i):
        return remote(opp.at[i], relay_in.at[i], rel_s.at[i], rel_r.at[i], peer(0, 1, 1))

    def opp_direct(i):
        return remote(opp.at[i], relay_in.at[i], rel_s.at[i], rel_r.at[i], peer(0, 0, 1))

    def cross_copy(dg, i):
        return remote(cross.at[dg, i], cross_in.at[dg, i], crs_s.at[dg, i], crs_r.at[dg, i], peer(dg, 1, 1))

    def own_rows(ii):
        def one(n, carry):
            @pl.when(jnp.logical_and(ii == 0, n == 2))
            def _():
                a_copy(2).start()
                b_copy(2).start()

            spectrum(keep, other, 4 * ii + n, pl.multiple_of(128 * n, 128), 512)
            return carry

        lax.fori_loop(0, 4, one, 0)
        for dg in range(2):
            for dh in range(2):
                b4 = block_at(dg, dh)
                total = dot(ww[...], spec[b4]) + dot(w_lo[...], spec[b4, 0:512, :])
                if dh == 0:
                    near[dg, ii] = total[0:256]
                else:
                    side[dg, ii] = total[0:256]
                pp[2 * dg + dh, ii] = total[256:512]
        for n in (1, 3):
            for dg in range(2):
                row_copy(dg, 4 * ii + n).start()
        near_copy(ii).start()

    def collect(i):
        n, ii = lax.rem(i, 4), i // 4
        at = dest_rows(n)
        for dg in range(2):
            cross_copy(dg, i).wait()
        parts = [
            near[0, ii, at, :] + side_in[0, ii, at, :] + cross_in[0, i],
            near_in[ii, at, :] + side_in[1, ii, at, :] + cross_in[1, i],
        ]
        got = dot(jnp.concatenate(split(jnp.concatenate(parts, axis=0)), axis=0), perm[h])
        rows = got[0:128] + got[128:256]
        for dg in range(2):
            row = 4 * (3 - block_of(n)) + 2 * lax.rem(g + dg, 2) + ii
            for c in range(4):
                by_lane[c][pl.ds(row, 64, stride=16), :] = rows[64 * dg : 64 * dg + 64, 128 * c : 128 * c + 128]

    def relay(i):
        n, ii = lax.rem(i, 4), i // 4

        @pl.when(lax.rem(i, 2) == 0)
        def _():
            opp_cross(i).wait()
            at = dest_rows(n)
            for dg in range(2):
                side[dg, ii, at, :] = side[dg, ii, at, :] + relay_in[i, dg]
                row_copy(dg, i).start()

        @pl.when(lax.rem(i, 2) == 1)
        def _():
            opp_direct(i).wait()
            for dg in range(2):
                cross[dg, i] = cross[dg, i] + relay_in[i, dg]
                cross_copy(dg, i).start()

    def step(i, carry):
        n, ii = lax.rem(i, 4), i // 4

        @pl.when(i == 2)
        def _():
            pass_on(3, 0)

        @pl.when(i == 3)
        def _():
            pass_on(2, 1)

        @pl.when(i == 5)
        def _():
            pass_on(3, 1)

        @pl.when(jnp.logical_or(i == 0, i == 3))
        def _():
            own_rows(i // 3)

        a_copy(i).wait_recv()
        b_copy(i).wait_recv()

        for now, start in ((0, 3), (2, 5), (3, 6)):

            @pl.when(i == now)
            def _():
                a_copy(start).start()
                b_copy(start).start()

        spectrum(halo_a, halo_b, i, 0, 128)
        mine = pl.ds(pl.multiple_of(64 * n, 64), 64)
        for dh in range(2):
            for dg in range(2):
                b4 = block_at(dg, dh)
                total = dot(wh[n], spec[b4, 0:256, :]) + dot(wh_lo[n], spec[b4, 0:128, :])
                pp[2 * dg + dh, ii] = pp[2 * dg + dh, ii] + total
                if dh == 0:
                    opp[i, dg] = pp[2 * dg, ii, mine, :]
                else:
                    cross[dg, i] = pp[2 * dg + 1, ii, mine, :]
            if dh == 0:

                @pl.when(lax.rem(i, 2) == 0)
                def _():
                    opp_cross(i).start()

                @pl.when(lax.rem(i, 2) == 1)
                def _():
                    opp_direct(i).start()

        @pl.when(lax.rem(i, 2) == 0)
        def _():
            for dg in range(2):
                cross_copy(dg, i).start()

        @pl.when(i >= 1)
        def _():
            relay(i - 1)

        @pl.when(i >= 4)
        def _():
            @pl.when(i == 4)
            def _():
                near_copy(0).wait()

            for dg in range(2):
                row_copy(dg, i - 4).wait()
            collect(i - 4)

        return carry

    lax.fori_loop(0, 8, step, 0)
    relay(7)
    near_copy(1).wait()

    def last(i, carry):
        for dg in range(2):
            row_copy(dg, i).wait()
        collect(i)
        return carry

    lax.fori_loop(4, 8, last, 0)
    results = [
        pltpu.make_async_copy(by_lane[c], out.at[:, pl.ds(128 * c, 128)], load_sem.at[c]) for c in range(4)
    ]
    for c in results:
        c.start()
    for i in range(8):
        snd_copy(i).wait_send()
        if i not in (4, 7):
            a_copy(i).wait_send()
            b_copy(i).wait_send()
    for hops in range(1, 4):
        for k in range(2):
            for which in range(2):
                via_copy(hops, k, which).wait_send()
    for c in results:
        c.wait()


def local(strips, field, spectral_phase, chirp_shift, tile_map, tile_phase):
    waves, tw = dft_tables()
    vmem = pl.BlockSpec(memory_space=pltpu.VMEM)
    hbm = pl.BlockSpec(memory_space=pltpu.HBM)
    rows = pltpu.VMEM((8, 2, 32, 1024), F32)
    small = pltpu.VMEM((16, 128), F32)
    phase = pltpu.VMEM((2, 32, NY), F32)
    sums = pltpu.VMEM((2, 2, 256, 512), F32)
    dma = pltpu.SemaphoreType.DMA
    out = pl.pallas_call(
        functools.partial(kernel, strips),
        in_specs=[hbm, hbm, hbm, hbm, vmem, vmem, pl.BlockSpec(memory_space=pltpu.SMEM)],
        out_specs=pl.BlockSpec(memory_space=pl.ANY),
        out_shape=jax.ShapeDtypeStruct((1024, 512), F32),
        scratch_shapes=[
            pltpu.VMEM((8, 2, 512, 128), F32),
            rows, rows, rows, rows, rows,
            small, small, small, small,
            pltpu.VMEM((32, NY), F32),
            pltpu.VMEM(waves.shape, F32),
            pltpu.VMEM(tw.shape, F32),
            phase, phase,
            pltpu.VMEM((2, 512, 512), BF),
            pltpu.VMEM((2, 512, 512), BF),
            pltpu.VMEM((2, 512, 512), BF),
            pltpu.VMEM((512, 1024), BF),
            pltpu.VMEM((512, 512), BF),
            pltpu.VMEM((4, 256, 256), BF),
            pltpu.VMEM((4, 256, 128), BF),
            pltpu.VMEM((2, 256, 512), BF),
            pltpu.VMEM((2, 256, 512), BF),
            pltpu.VMEM((4, 1024, 512), BF),
            sums,
            pltpu.VMEM((2, 256, 512), F32),
            sums, sums,
            pltpu.VMEM((4, 2, 256, 512), F32),
            pltpu.VMEM((8, 2, 64, 512), F32),
            pltpu.VMEM((8, 2, 64, 512), F32),
            pltpu.VMEM((2, 8, 64, 512), F32),
            pltpu.VMEM((2, 8, 64, 512), F32),
            pltpu.VMEM((2, 2, 2, 32, 1024), F32),
            pltpu.VMEM((2, 2, 2, 32, 1024), F32),
            *[pltpu.VMEM((1024, 128), F32)] * 4,
            dma((11,)),
            *[dma((8,))] * 6,
            dma((3,)), dma((3,)),
            dma((2,)), dma((2,)),
            dma((2, 8)), dma((2, 8)),
            dma((8,)), dma((8,)),
            dma((2, 8)), dma((2, 8)),
            *[dma((2, 2))] * 4,
        ],
        compiler_params=pltpu.CompilerParams(
            collective_id=0, has_side_effects=True, vmem_limit_bytes=VMEM * 2**20
        ),
        cost_estimate=pl.CostEstimate(flops=40 * 10**9, bytes_accessed=10 * 2**20, transcendentals=0),
    )(
        field.reshape(2, 512, 1024), spectral_phase, jnp.asarray(waves), jnp.asarray(tw),
        chirp_shift.reshape(1, 32), tile_phase, tile_map,
    )
    return out.reshape(2, NT, 16, 512)


def solution(mesh):
    placed = (P(None, "freq", "xs", "yh"), P("freq", None), P("freq"), P("xs"), P(None, "freq"))
    return jax.shard_map(
        functools.partial(local, mesh.shape["xs"]),
        mesh=mesh,
        in_specs=placed,
        out_specs=P(None, None, "xs", ("freq", "yh")),
        check_vma=False,
    )
```

```python
import functools
import math

import jax
import jax.numpy as jnp
import numpy as np
from jax import lax
from jax.experimental import pallas as pl
from jax.experimental.pallas import tpu as pltpu
from jax.sharding import PartitionSpec as P

NF = 64
NY = 2048
NT = 32
VMEM = 58
BF = jnp.bfloat16
F32 = jnp.float32
AXES = ("freq", "xs", "yh")
MESH = pl.DeviceIdType.MESH


def dft_tables():
    m = np.arange(256)
    angle = 2.0 * np.pi * (np.outer(m, m) % 256) / 256
    waves = np.stack([np.cos(angle), np.sin(angle)]) / math.sqrt(NY)
    odd_order = np.concatenate([np.arange(64) + 64 * b for b in (1, 0, 3, 2)])
    turn = 2.0 * np.pi * np.outer(np.arange(8), m) / NY
    twiddle = np.stack([np.cos(turn), np.sin(turn)])
    return np.stack([waves, waves[:, :, odd_order]]).astype(np.float32), twiddle.astype(np.float32)


def split(value):
    high = value.astype(BF)
    return high, (value - high.astype(F32)).astype(BF)


def dot(a, b):
    return jnp.dot(a, b, preferred_element_type=F32)


def dot_t(a, b):
    return lax.dot_general(a, b, (((1,), (1,)), ((), ())), preferred_element_type=F32)


def sincos(x):
    k = jnp.floor(x * (2.0 / math.pi) + 0.5)
    r = ((x - k * 1.5703125) - k * 4.837512969970703125e-4) - k * 7.54978995489188216e-8
    z = r * r
    sine = r + r * z * (-1.6666654611e-1 + z * (8.3321608736e-3 - z * 1.9515295891e-4))
    cosine = (1.0 - 0.5 * z) + z * z * (4.166664568298827e-2 + z * (-1.388731625493765e-3 + z * 2.443315711809948e-5))
    half = jnp.floor(k * 0.5)
    swap = (k - 2.0 * half) > 0.5
    sign = 1.0 - 2.0 * (half - 2.0 * jnp.floor(half * 0.5))
    return sign * jnp.where(swap, cosine, sine), sign * jnp.where(swap, -sine, cosine)


def butterflies(re, im, tw):
    a = [(re[:, 256 * c : 256 * c + 256], im[:, 256 * c : 256 * c + 256]) for c in range(4)]
    r = math.sqrt(0.5)

    def add(u, v):
        return u[0] + v[0], u[1] + v[1]

    def sub(u, v):
        return u[0] - v[0], u[1] - v[1]

    def mi(u):
        return u[1], -u[0]

    def four(b):
        e0, e1 = add(b[0], b[2]), sub(b[0], b[2])
        e2, e3 = add(b[1], b[3]), mi(sub(b[1], b[3]))
        return add(e0, e2), add(e1, e3), sub(e0, e2), sub(e1, e3)

    even = four(a)
    b1 = ((a[1][0] + a[1][1]) * r, (a[1][1] - a[1][0]) * r)
    b3 = ((a[3][1] - a[3][0]) * r, (-a[3][0] - a[3][1]) * r)
    odd = four((a[0], b1, mi(a[2]), b3))
    both = []
    for side, parts in enumerate((even, odd)):
        row = []
        for j in range(4):
            p = 2 * j + side
            u = parts[j]
            if p:
                c, s = tw[0, p : p + 1, :], tw[1, p : p + 1, :]
                u = u[0] * c + u[1] * s, u[1] * c - u[0] * s
            row.append(u)
        both.append(row)
    return both


def kernel(
    strips, field, phi_hbm, waves_hbm, tw_hbm, shift_row, tile_phase, tile_ids, out,
    flat, snd, keep, other, halo_a, halo_b, prm, prm_out, prm_in, prm_pair,
    phi, waves, tw, e_own, e_other, t_hi, t_lo, perm, ww, w_lo, wh, wh_lo,
    l_hi, l_lo, spec, near, near_in, side, side_in, pp, opp, relay_in, cross, cross_in, via_1, via_2, *rest,
):
    (load_sem, snd_s, snd_r, ha_s, ha_r, hb_s, hb_r, prm_s, prm_r,
     near_s, near_r, row_s, row_r, rel_s, rel_r, crs_s, crs_r, v1_s, v1_r, v2_s, v2_r) = rest
    g, s, h = (lax.axis_index(a) for a in AXES)
    odd = lax.rem(s, 2)
    pair = s + 1 - 2 * odd
    onward = lax.rem(s + strips + 4 * odd - 2, strips)
    back = lax.rem(s + strips + 2 - 4 * odd, strips)
    core = (1 - g, s, h)

    z, y, turns = s // 8, lax.rem(s // 2, 4), strips // 8
    hop = 1 - 2 * odd
    across = 8 * z + 2 * lax.rem(y + 4 + hop, 4) + odd
    across_from = 8 * z + 2 * lax.rem(y + 4 - hop, 4) + odd
    z_on = 8 * (lax.rem(z + turns - hop, turns) - z)
    z_back = 8 * (lax.rem(z + turns + hop, turns) - z)
    first = across + (y == 3 * odd).astype(jnp.int32) * z_on
    first_from = across_from + (y == 1 + odd).astype(jnp.int32) * z_back

    def peer(dg, ds, dh):
        return (lax.rem(g + dg, 2), pair if ds else s, lax.rem(h + dh, 2))

    def remote(src, dst, a, b, to):
        return pltpu.make_async_remote_copy(
            src_ref=src, dst_ref=dst, send_sem=a, recv_sem=b, device_id=to, device_id_type=MESH
        )

    def block_of(n):
        return n + odd * (3 - 2 * n)

    loads = [
        pltpu.make_async_copy(field.at[:, :, pl.ds(128 * y, 128)], flat.at[y], load_sem.at[y]) for y in range(8)
    ]
    tables = [
        pltpu.make_async_copy(src, dst, load_sem.at[8 + k])
        for k, (src, dst) in enumerate(((waves_hbm, waves), (tw_hbm, tw), (phi_hbm, phi)))
    ]
    for c in loads + tables:
        c.start()
    barrier = pltpu.get_barrier_semaphore()
    greet = [core, peer(0, 0, 1), peer(1, 0, 1), peer(0, 1, 1), peer(1, 1, 1), (g, onward, h), (g, back, h)]
    greet += [(g, across, h), (g, across_from, h), (g, first, h), (g, first_from, h)]
    for to in greet:
        pl.semaphore_signal(barrier, inc=1, device_id=to, device_id_type=MESH)

    def snd_copy(i):
        return remote(snd.at[i], other.at[i], snd_s.at[i], snd_r.at[i], core)

    def a_copy(i):
        return remote(keep.at[i], halo_a.at[i], ha_s.at[i], ha_r.at[i], (g, onward, h))

    def b_copy(i):
        return remote(other.at[i], halo_b.at[i], hb_s.at[i], hb_r.at[i], (g, onward, h))

    def via_copy(hops, k, which):
        i = 4 + 3 * k
        if hops == 1:
            src = (keep, other)[which].at[i]
            return remote(src, via_1.at[k, which], v1_s.at[k, which], v1_r.at[k, which], (g, first, h))
        if hops == 2:
            return remote(
                via_1.at[k, which], via_2.at[k, which], v2_s.at[k, which], v2_r.at[k, which], (g, across, h)
            )
        dst, sems = ((halo_a, (ha_s, ha_r)), (halo_b, (hb_s, hb_r)))[which]
        return remote(via_2.at[k, which], dst.at[i], sems[0].at[i], sems[1].at[i], (g, across, h))

    def pass_on(hops, k):
        for which in range(2):
            via_copy(hops - 1, k, which).wait_recv()
            via_copy(hops, k, which).start()

    def gather_rows(i, whose, into):
        row = 4 * block_of(lax.rem(i, 4)) + 2 * whose + i // 4
        for c in range(2):
            for y in range(8):
                into[i, c, :, 128 * y : 128 * y + 128] = flat[y, c, pl.ds(row, 32, stride=16), :]

    gap = jnp.zeros((8, 32), F32)
    rows = jnp.concatenate([shift_row[...].astype(F32), tile_phase[...], jnp.zeros((3, 32), F32)], axis=0)
    prm[0:8, :] = jnp.concatenate([rows, gap, rows, gap], axis=1)
    for rb in range(4):
        prm[8 + rb : 9 + rb, :] = jnp.full((1, 128), tile_ids[rb], jnp.int32).astype(F32)
    prm[12:16, :] = jnp.zeros((4, 128), F32)
    prm_out[...] = pltpu.roll(prm[...], 32, 1)
    prm_core = remote(prm_out, prm_in, prm_s.at[0], prm_r.at[0], core)
    prm_strip = remote(prm, prm_pair, prm_s.at[1], prm_r.at[1], peer(0, 1, 1))

    for c in loads:
        c.wait()

    def pack_send(i, carry):
        gather_rows(i, 1 - g, snd)
        snd_copy(i).start()
        return carry

    def pack_keep(i, carry):
        gather_rows(i, g, keep)
        return carry

    for i in (0, 4, 1):
        gather_rows(i, g, keep)
    pl.semaphore_wait(barrier, len(greet))
    a_copy(0).start()
    via_copy(1, 0, 0).start()
    a_copy(1).start()
    lax.fori_loop(0, 8, pack_send, 0)
    prm_core.start()
    prm_strip.start()
    lax.fori_loop(2, 4, pack_keep, 0)
    lax.fori_loop(5, 8, pack_keep, 0)
    for i in (0, 4, 1):
        snd_copy(i).wait_recv()
        if i == 4:
            via_copy(1, 0, 1).start()
        else:
            b_copy(i).start()

    for c in tables:
        c.wait()
    lane = lax.broadcasted_iota(jnp.int32, (512, 1), 0)
    wave = lax.broadcasted_iota(jnp.int32, (1, 512), 1)
    turn = lax.rem(lane, 128)
    for half in range(2):
        late = (turn >= 64).astype(jnp.int32)
        late = late if half == 0 else 1 - late
        target = 8 * lax.rem(turn, 64) + 2 * (lane // 128) + late
        perm[half] = jnp.where(target == wave, 1.0, 0.0).astype(BF)
        c_hi, c_lo = split(waves[half, 0])
        s_hi, s_lo = split(waves[half, 1])
        for table, c, w in ((t_hi, c_hi, s_hi), (t_lo, c_lo, s_lo)):
            table[half, 0:256, 0:256] = c
            table[half, 0:256, 256:512] = -w
            table[half, 256:512, 0:256] = w
            table[half, 256:512, 256:512] = c

    lanes = lax.rem(lax.broadcasted_iota(jnp.int32, (1, 512), 1), 128)
    for half in range(2):
        late = lanes >= 64 if half == 0 else lanes < 64
        sign = 1.0 - 2.0 * jnp.where(late, h, 0).astype(F32)
        stack = []
        for b in (half, half + 2):
            sine, cosine = sincos(phi[:, 512 * b : 512 * b + 512])
            stack += [*split(cosine), *split(sine)]
        got = dot_t(jnp.concatenate(stack, axis=0), perm[half])
        for k, b in enumerate((half, half + 2)):
            for part in range(2):
                at = 128 * k + 64 * part
                e_own[part, :, 512 * b : 512 * b + 512] = (got[at : at + 32] + got[at + 32 : at + 64]) * sign
    e_copy = remote(e_own, e_other, prm_s.at[2], prm_r.at[2], core)
    e_copy.start()

    prm_core.wait()
    prm_strip.wait()
    both = prm[...] + prm_in[...]
    shift = both[0:1, :]
    col = lax.broadcasted_iota(jnp.int32, (NT, 128), 1)
    freq = lax.rem(lax.rem(col, 64) + 32 * g, NF)
    angle = (2.0 * math.pi / NF) * lax.rem(lax.broadcasted_iota(jnp.int32, (NT, 128), 0) * freq, NF).astype(F32)
    scale = 1.0 / math.sqrt(NF)
    real_in = col < 64

    def base(tile):
        phase = jnp.zeros((1, 128), F32)
        for t in range(4):
            phase = phase + jnp.where(tile == float(t), both[1 + t : 2 + t, :], 0.0)
        im, re = sincos(angle + phase)
        im, re = im * scale, re * scale
        return jnp.concatenate([jnp.where(real_in, re, -im), jnp.where(real_in, im, re)], axis=0)

    far = (4 * (1 - 2 * odd)).astype(F32)
    inside = jnp.where(odd == 1, (s > 1).astype(F32), (s < strips - 2).astype(F32))
    for nd in range(4):
        dest = block_of(nd)
        here, there = base(prm[8 + nd : 9 + nd, :]), base(prm_pair[pl.ds(8 + dest, 1), :])
        rows = slice(64 * nd, 64 * nd + 64)
        for n in range(4):
            source = block_of(n)
            own_hi, own_lo = split(jnp.where(shift == (nd - source).astype(F32), here, 0.0))
            step = (dest - source).astype(F32)
            pair_hi, pair_lo = split(jnp.where(shift == step + far, there, 0.0))
            halo_hi, halo_lo = split(jnp.where(shift == step - far, there * inside, 0.0))
            at = 128 * n
            below = slice(256 + 64 * nd, 320 + 64 * nd)
            ww[rows, at : at + 128] = own_hi
            ww[rows, 512 + at : 640 + at] = own_hi
            w_lo[rows, at : at + 128] = own_lo
            ww[below, at : at + 128] = pair_hi
            ww[below, 512 + at : 640 + at] = pair_hi
            w_lo[below, at : at + 128] = pair_lo
            wh[n, rows, 0:128] = halo_hi
            wh[n, rows, 128:256] = halo_hi
            wh_lo[n, rows, :] = halo_lo
    for i in (2, 3, 5, 6, 7):
        snd_copy(i).wait_recv()
    pass_on(2, 0)
    for which in range(2):
        via_copy(1, 1, which).start()
    e_copy.wait()

    def spread(a, b, i, k):
        re = jnp.concatenate([a[i, 0], b[i, 0]], axis=0)
        im = jnp.concatenate([a[i, 1], b[i, 1]], axis=0)
        for half_p, parts in enumerate(butterflies(re, im, tw)):
            for j, pieces in enumerate(parts):
                for half, w in enumerate(pieces):
                    hi, lo = split(w)
                    l_hi[k, half_p, 64 * j : 64 * j + 64, 256 * half : 256 * half + 256] = hi
                    l_lo[k, half_p, 64 * j : 64 * j + 64, 256 * half : 256 * half + 256] = lo

    def transform(k):
        return [
            dot(l_hi[k, p], t_hi[p]) + dot(l_lo[k, p], t_hi[p]) + dot(l_hi[k, p], t_lo[p]) for p in range(2)
        ]

    def turn_phase(even, uneven, at, depth):
        early = lax.broadcasted_iota(jnp.int32, (64, 128), 1) < 64
        for j in range(4):
            for b4 in range(4):
                first_p, second_p = (even, uneven) if b4 % 2 == 0 else (uneven, even)
                rows = slice(64 * j, 64 * j + 64)
                c0 = 128 * (b4 // 2)
                u = jnp.where(early, first_p[rows, c0 : c0 + 128], second_p[rows, c0 : c0 + 128])
                v = jnp.where(early, first_p[rows, 256 + c0 : 384 + c0], second_p[rows, 256 + c0 : 384 + c0])
                e0 = 512 * b4 + 128 * j
                c, w = (
                    jnp.concatenate([e_own[part, :, e0 : e0 + 128], e_other[part, :, e0 : e0 + 128]], axis=0)
                    for part in range(2)
                )
                for half, value in enumerate((u * c - v * w, u * w + v * c)):
                    hi, lo = split(value)
                    spec[b4, pl.ds(at + 64 * half, 64), 128 * j : 128 * j + 128] = hi
                    spec[b4, pl.ds(depth + at + 64 * half, 64), 128 * j : 128 * j + 128] = lo

    def block_at(dg, dh):
        return 2 * lax.rem(g + dg, 2) + lax.rem(h + dh, 2)

    def near_copy(ii):
        return remote(near.at[1, ii], near_in.at[ii], near_s.at[ii], near_r.at[ii], core)

    def dest_rows(n):
        return pl.ds(pl.multiple_of(64 * (3 - block_of(n)), 64), 64)

    def row_copy(dg, i):
        at, ii = dest_rows(lax.rem(i, 4)), i // 4
        return remote(side.at[dg, ii, at], side_in.at[dg, ii, at], row_s.at[dg, i], row_r.at[dg, i], peer(dg, 0, 1))

    def opp_cross(i):
        return remote(opp.at[i], relay_in.at[i], rel_s.at[i], rel_r.at[i], peer(0, 1, 1))

    def opp_direct(i):
        return remote(opp.at[i], relay_in.at[i], rel_s.at[i], rel_r.at[i], peer(0, 0, 1))

    def cross_copy(dg, i):
        return remote(cross.at[dg, i], cross_in.at[dg, i], crs_s.at[dg, i], crs_r.at[dg, i], peer(dg, 1, 1))

    def own_rows(ii):
        def two(m, carry):
            @pl.when(jnp.logical_and(ii == 0, m == 1))
            def _():
                a_copy(2).start()
                b_copy(2).start()

            i, at = 4 * ii + 2 * m, pl.multiple_of(256 * m, 256)
            spread(keep, other, i, 0)
            got = transform(0)
            spread(keep, other, i + 1, 1)
            turn_phase(*got, at, 512)
            turn_phase(*transform(1), at + 128, 512)
            return carry

        lax.fori_loop(0, 2, two, 0)
        for dh in (1, 0):
            for dg in range(2):
                b4 = block_at(dg, dh)
                total = dot(ww[...], spec[b4]) + dot(w_lo[...], spec[b4, 0:512, :])
                if dh == 0:
                    near[dg, ii] = total[0:256]
                else:
                    side[dg, ii] = total[0:256]
                    for n in (1, 3):
                        row_copy(dg, 4 * ii + n).start()
                pp[2 * dg + dh, ii] = total[256:512]
        near_copy(ii).start()

    def collect(i):
        n, ii = lax.rem(i, 4), i // 4
        at = dest_rows(n)
        for dg in range(2):
            cross_copy(dg, i).wait()
        parts = [
            near[0, ii, at, :] + side_in[0, ii, at, :] + cross_in[0, i],
            near_in[ii, at, :] + side_in[1, ii, at, :] + cross_in[1, i],
        ]
        got = dot(jnp.concatenate(split(jnp.concatenate(parts, axis=0)), axis=0), perm[h])
        rows = got[0:128] + got[128:256]
        for dg in range(2):
            row = 4 * (3 - block_of(n)) + 2 * lax.rem(g + dg, 2) + ii
            for c in range(4):
                for part in range(2):
                    at = 64 * dg + 32 * part
                    flat[c, part, pl.ds(row, 32, stride=16), :] = rows[at : at + 32, 128 * c : 128 * c + 128]

    def relay(i):
        n, ii = lax.rem(i, 4), i // 4

        @pl.when(lax.rem(i, 2) == 0)
        def _():
            opp_cross(i).wait()
            at = dest_rows(n)
            for dg in range(2):
                side[dg, ii, at, :] = side[dg, ii, at, :] + relay_in[i, dg]
                row_copy(dg, i).start()

        @pl.when(lax.rem(i, 2) == 1)
        def _():
            opp_direct(i).wait()
            for dg in range(2):
                cross[dg, i] = cross[dg, i] + relay_in[i, dg]
                cross_copy(dg, i).start()

    def step(i, carry):
        n, ii = lax.rem(i, 4), i // 4

        @pl.when(i == 2)
        def _():
            pass_on(3, 0)

        @pl.when(i == 3)
        def _():
            pass_on(2, 1)

        @pl.when(i == 5)
        def _():
            pass_on(3, 1)

        @pl.when(jnp.logical_or(i == 0, i == 3))
        def _():
            own_rows(i // 3)

        a_copy(i).wait_recv()
        b_copy(i).wait_recv()

        for now, start in ((0, 3), (2, 5), (3, 6)):

            @pl.when(i == now)
            def _():
                a_copy(start).start()
                b_copy(start).start()

        spread(halo_a, halo_b, i, 0)
        turn_phase(*transform(0), 0, 128)
        mine = pl.ds(pl.multiple_of(64 * n, 64), 64)
        for dh in range(2):
            for dg in range(2):
                b4 = block_at(dg, dh)
                total = dot(wh[n], spec[b4, 0:256, :]) + dot(wh_lo[n], spec[b4, 0:128, :])
                pp[2 * dg + dh, ii] = pp[2 * dg + dh, ii] + total
                if dh == 0:
                    opp[i, dg] = pp[2 * dg, ii, mine, :]
                else:
                    cross[dg, i] = pp[2 * dg + 1, ii, mine, :]
            if dh == 0:

                @pl.when(lax.rem(i, 2) == 0)
                def _():
                    opp_cross(i).start()

                @pl.when(lax.rem(i, 2) == 1)
                def _():
                    opp_direct(i).start()

        @pl.when(lax.rem(i, 2) == 0)
        def _():
            for dg in range(2):
                cross_copy(dg, i).start()

        @pl.when(i >= 1)
        def _():
            relay(i - 1)

        @pl.when(i >= 4)
        def _():
            @pl.when(i == 4)
            def _():
                near_copy(0).wait()

            for dg in range(2):
                row_copy(dg, i - 4).wait()
            collect(i - 4)

        return carry

    lax.fori_loop(0, 8, step, 0)
    relay(7)
    near_copy(1).wait()

    def last(i, carry):
        for dg in range(2):
            row_copy(dg, i).wait()
        collect(i)
        return carry

    lax.fori_loop(4, 8, last, 0)
    results = [
        pltpu.make_async_copy(flat.at[c], out.at[:, :, pl.ds(128 * c, 128)], load_sem.at[c]) for c in range(4)
    ]
    for c in results:
        c.start()
    for i in range(8):
        snd_copy(i).wait_send()
        if i not in (4, 7):
            a_copy(i).wait_send()
            b_copy(i).wait_send()
    for hops in range(1, 4):
        for k in range(2):
            for which in range(2):
                via_copy(hops, k, which).wait_send()
    for c in results:
        c.wait()


def local(strips, field, spectral_phase, chirp_shift, tile_map, tile_phase):
    waves, tw = dft_tables()
    vmem = pl.BlockSpec(memory_space=pltpu.VMEM)
    hbm = pl.BlockSpec(memory_space=pl.ANY)
    rows = pltpu.VMEM((8, 2, 32, 1024), F32)
    small = pltpu.VMEM((16, 128), F32)
    phase = pltpu.VMEM((2, 32, NY), F32)
    sums = pltpu.VMEM((2, 2, 256, 512), F32)
    dma = pltpu.SemaphoreType.DMA
    out = pl.pallas_call(
        functools.partial(kernel, strips),
        in_specs=[hbm, hbm, hbm, hbm, vmem, vmem, pl.BlockSpec(memory_space=pltpu.SMEM)],
        out_specs=pl.BlockSpec(memory_space=pl.ANY),
        out_shape=jax.ShapeDtypeStruct((2, 512, 512), F32),
        scratch_shapes=[
            pltpu.VMEM((8, 2, 512, 128), F32),
            rows, rows, rows, rows, rows,
            small, small, small, small,
            pltpu.VMEM((32, NY), F32),
            pltpu.VMEM(waves.shape, F32),
            pltpu.VMEM(tw.shape, F32),
            phase, phase,
            pltpu.VMEM((2, 512, 512), BF),
            pltpu.VMEM((2, 512, 512), BF),
            pltpu.VMEM((2, 512, 512), BF),
            pltpu.VMEM((512, 1024), BF),
            pltpu.VMEM((512, 512), BF),
            pltpu.VMEM((4, 256, 256), BF),
            pltpu.VMEM((4, 256, 128), BF),
            pltpu.VMEM((2, 2, 256, 512), BF),
            pltpu.VMEM((2, 2, 256, 512), BF),
            pltpu.VMEM((4, 1024, 512), BF),
            sums,
            pltpu.VMEM((2, 256, 512), F32),
            sums, sums,
            pltpu.VMEM((4, 2, 256, 512), F32),
            pltpu.VMEM((8, 2, 64, 512), F32),
            pltpu.VMEM((8, 2, 64, 512), F32),
            pltpu.VMEM((2, 8, 64, 512), F32),
            pltpu.VMEM((2, 8, 64, 512), F32),
            pltpu.VMEM((2, 2, 2, 32, 1024), F32),
            pltpu.VMEM((2, 2, 2, 32, 1024), F32),
            dma((11,)),
            *[dma((8,))] * 6,
            dma((3,)), dma((3,)),
            dma((2,)), dma((2,)),
            dma((2, 8)), dma((2, 8)),
            dma((8,)), dma((8,)),
            dma((2, 8)), dma((2, 8)),
            *[dma((2, 2))] * 4,
        ],
        compiler_params=pltpu.CompilerParams(
            collective_id=0, has_side_effects=True, vmem_limit_bytes=VMEM * 2**20
        ),
        cost_estimate=pl.CostEstimate(flops=40 * 10**9, bytes_accessed=10 * 2**20, transcendentals=0),
    )(
        field.reshape(2, 512, 1024), spectral_phase, jnp.asarray(waves), jnp.asarray(tw),
        chirp_shift.reshape(1, 32), tile_phase, tile_map,
    )
    return out.reshape(2, NT, 16, 512)


def solution(mesh):
    placed = (P(None, "freq", "xs", "yh"), P("freq", None), P("freq"), P("xs"), P(None, "freq"))
    return jax.shard_map(
        functools.partial(local, mesh.shape["xs"]),
        mesh=mesh,
        in_specs=placed,
        out_specs=P(None, None, "xs", ("freq", "yh")),
        check_vma=False,
    )
```

```python
import functools
import math

import jax
import jax.numpy as jnp
import numpy as np
from jax import lax
from jax.experimental import pallas as pl
from jax.experimental.pallas import tpu as pltpu
from jax.sharding import PartitionSpec as P

NF = 64
NY = 2048
NT = 32
VMEM = 60
BF = jnp.bfloat16
F32 = jnp.float32
AXES = ("freq", "xs", "yh")
MESH = pl.DeviceIdType.MESH


def dft_tables():
    m = np.arange(256)
    angle = 2.0 * np.pi * (np.outer(m, m) % 256) / 256
    waves = np.stack([np.cos(angle), np.sin(angle)]) / math.sqrt(NY)
    odd_order = np.concatenate([np.arange(64) + 64 * b for b in (1, 0, 3, 2)])
    turn = 2.0 * np.pi * np.outer(np.arange(8), m) / NY
    twiddle = np.stack([np.cos(turn), np.sin(turn)])
    return np.stack([waves, waves[:, :, odd_order]]).astype(np.float32), twiddle.astype(np.float32)


def split(value):
    high = value.astype(BF)
    return high, (value - high.astype(F32)).astype(BF)


def dot(a, b):
    return jnp.dot(a, b, preferred_element_type=F32)


def dot_t(a, b):
    return lax.dot_general(a, b, (((1,), (1,)), ((), ())), preferred_element_type=F32)


def sincos(x):
    k = jnp.floor(x * (2.0 / math.pi) + 0.5)
    r = ((x - k * 1.5703125) - k * 4.837512969970703125e-4) - k * 7.54978995489188216e-8
    z = r * r
    sine = r + r * z * (-1.6666654611e-1 + z * (8.3321608736e-3 - z * 1.9515295891e-4))
    cosine = (1.0 - 0.5 * z) + z * z * (4.166664568298827e-2 + z * (-1.388731625493765e-3 + z * 2.443315711809948e-5))
    half = jnp.floor(k * 0.5)
    swap = (k - 2.0 * half) > 0.5
    sign = 1.0 - 2.0 * (half - 2.0 * jnp.floor(half * 0.5))
    return sign * jnp.where(swap, cosine, sine), sign * jnp.where(swap, -sine, cosine)


def butterflies(re, im, tw):
    a = [(re[:, 256 * c : 256 * c + 256], im[:, 256 * c : 256 * c + 256]) for c in range(4)]
    r = math.sqrt(0.5)

    def add(u, v):
        return u[0] + v[0], u[1] + v[1]

    def sub(u, v):
        return u[0] - v[0], u[1] - v[1]

    def mi(u):
        return u[1], -u[0]

    def four(b):
        e0, e1 = add(b[0], b[2]), sub(b[0], b[2])
        e2, e3 = add(b[1], b[3]), mi(sub(b[1], b[3]))
        return add(e0, e2), add(e1, e3), sub(e0, e2), sub(e1, e3)

    even = four(a)
    b1 = ((a[1][0] + a[1][1]) * r, (a[1][1] - a[1][0]) * r)
    b3 = ((a[3][1] - a[3][0]) * r, (-a[3][0] - a[3][1]) * r)
    odd = four((a[0], b1, mi(a[2]), b3))
    both = []
    for side, parts in enumerate((even, odd)):
        row = []
        for j in range(4):
            p = 2 * j + side
            u = parts[j]
            if p:
                c, s = tw[0, p : p + 1, :], tw[1, p : p + 1, :]
                u = u[0] * c + u[1] * s, u[1] * c - u[0] * s
            row.append(u)
        both.append(row)
    return both


def kernel(
    strips, field, phi_hbm, waves_hbm, tw_hbm, shift_row, tile_phase, tile_ids, out,
    flat, snd, keep, other, halo_a, halo_b, prm, prm_out, prm_in, prm_pair,
    phi, waves, tw, e_own, e_other, table, perm, ww, wh,
    spread, spec, near, near_in, side, side_in, pp, opp, relay_in, cross, cross_in, via_1, via_2, *rest,
):
    (load_sem, snd_s, snd_r, ha_s, ha_r, hb_s, hb_r, prm_s, prm_r,
     near_s, near_r, row_s, row_r, rel_s, rel_r, crs_s, crs_r, v1_s, v1_r, v2_s, v2_r) = rest
    g, s, h = (lax.axis_index(a) for a in AXES)
    odd = lax.rem(s, 2)
    pair = s + 1 - 2 * odd
    onward = lax.rem(s + strips + 4 * odd - 2, strips)
    back = lax.rem(s + strips + 2 - 4 * odd, strips)
    core = (1 - g, s, h)

    z, y, turns = s // 8, lax.rem(s // 2, 4), strips // 8
    hop = 1 - 2 * odd
    across = 8 * z + 2 * lax.rem(y + 4 + hop, 4) + odd
    across_from = 8 * z + 2 * lax.rem(y + 4 - hop, 4) + odd
    z_on = 8 * (lax.rem(z + turns - hop, turns) - z)
    z_back = 8 * (lax.rem(z + turns + hop, turns) - z)
    first = across + (y == 3 * odd).astype(jnp.int32) * z_on
    first_from = across_from + (y == 1 + odd).astype(jnp.int32) * z_back

    def peer(dg, ds, dh):
        return (lax.rem(g + dg, 2), pair if ds else s, lax.rem(h + dh, 2))

    def remote(src, dst, a, b, to):
        return pltpu.make_async_remote_copy(
            src_ref=src, dst_ref=dst, send_sem=a, recv_sem=b, device_id=to, device_id_type=MESH
        )

    def block_of(n):
        return n + odd * (3 - 2 * n)

    loads = [
        pltpu.make_async_copy(field.at[:, :, pl.ds(128 * y, 128)], flat.at[y], load_sem.at[y]) for y in range(8)
    ]
    tables = [
        pltpu.make_async_copy(src, dst, load_sem.at[8 + k])
        for k, (src, dst) in enumerate(((waves_hbm, waves), (tw_hbm, tw), (phi_hbm, phi)))
    ]
    for c in loads + tables:
        c.start()
    barrier = pltpu.get_barrier_semaphore()
    greet = [core, peer(0, 0, 1), peer(1, 0, 1), peer(0, 1, 1), peer(1, 1, 1), (g, onward, h), (g, back, h)]
    greet += [(g, across, h), (g, across_from, h), (g, first, h), (g, first_from, h)]
    for to in greet:
        pl.semaphore_signal(barrier, inc=1, device_id=to, device_id_type=MESH)

    def snd_copy(i):
        return remote(snd.at[i], other.at[i], snd_s.at[i], snd_r.at[i], core)

    def a_copy(i):
        return remote(keep.at[i], halo_a.at[i], ha_s.at[i], ha_r.at[i], (g, onward, h))

    def b_copy(i):
        return remote(other.at[i], halo_b.at[i], hb_s.at[i], hb_r.at[i], (g, onward, h))

    def via_copy(hops, k, which):
        i = 4 + 3 * k
        if hops == 1:
            src = (keep, other)[which].at[i]
            return remote(src, via_1.at[k, which], v1_s.at[k, which], v1_r.at[k, which], (g, first, h))
        if hops == 2:
            return remote(
                via_1.at[k, which], via_2.at[k, which], v2_s.at[k, which], v2_r.at[k, which], (g, across, h)
            )
        dst, sems = ((halo_a, (ha_s, ha_r)), (halo_b, (hb_s, hb_r)))[which]
        return remote(via_2.at[k, which], dst.at[i], sems[0].at[i], sems[1].at[i], (g, across, h))

    def pass_on(hops, k):
        for which in range(2):
            via_copy(hops - 1, k, which).wait_recv()
            via_copy(hops, k, which).start()

    def gather_rows(i, whose, into):
        row = 4 * block_of(lax.rem(i, 4)) + 2 * whose + i // 4
        for c in range(2):
            for y in range(8):
                into[i, c, :, 128 * y : 128 * y + 128] = flat[y, c, pl.ds(row, 32, stride=16), :]

    gap = jnp.zeros((8, 32), F32)
    rows = jnp.concatenate([shift_row[...].astype(F32), tile_phase[...], jnp.zeros((3, 32), F32)], axis=0)
    prm[0:8, :] = jnp.concatenate([rows, gap, rows, gap], axis=1)
    for rb in range(4):
        prm[8 + rb : 9 + rb, :] = jnp.full((1, 128), tile_ids[rb], jnp.int32).astype(F32)
    prm[12:16, :] = jnp.zeros((4, 128), F32)
    prm_out[...] = pltpu.roll(prm[...], 32, 1)
    prm_core = remote(prm_out, prm_in, prm_s.at[0], prm_r.at[0], core)
    prm_strip = remote(prm, prm_pair, prm_s.at[1], prm_r.at[1], peer(0, 1, 1))

    for c in loads:
        c.wait()

    def pack_send(i, carry):
        gather_rows(i, 1 - g, snd)
        snd_copy(i).start()
        return carry

    def pack_keep(i, carry):
        gather_rows(i, g, keep)
        return carry

    for i in (0, 4, 1):
        gather_rows(i, g, keep)
    pl.semaphore_wait(barrier, len(greet))
    a_copy(0).start()
    via_copy(1, 0, 0).start()
    a_copy(1).start()
    lax.fori_loop(0, 8, pack_send, 0)
    prm_core.start()
    prm_strip.start()
    lax.fori_loop(2, 4, pack_keep, 0)
    lax.fori_loop(5, 8, pack_keep, 0)
    for i in (0, 4, 1):
        snd_copy(i).wait_recv()
        if i == 4:
            via_copy(1, 0, 1).start()
        else:
            b_copy(i).start()

    for c in tables:
        c.wait()
    lane = lax.broadcasted_iota(jnp.int32, (512, 1), 0)
    wave = lax.broadcasted_iota(jnp.int32, (1, 512), 1)
    turn = lax.rem(lane, 128)
    for half in range(2):
        late = (turn >= 64).astype(jnp.int32)
        late = late if half == 0 else 1 - late
        target = 8 * lax.rem(turn, 64) + 2 * (lane // 128) + late
        perm[half] = jnp.where(target == wave, 1.0, 0.0).astype(BF)
        c_hi, c_lo = split(waves[half, 0])
        s_hi, s_lo = split(waves[half, 1])
        for k, (c, w) in enumerate(((c_hi, s_hi), (c_hi, s_hi), (c_lo, s_lo))):
            table[half, 512 * k : 512 * k + 256, 0:256] = c
            table[half, 512 * k : 512 * k + 256, 256:512] = -w
            table[half, 512 * k + 256 : 512 * k + 512, 0:256] = w
            table[half, 512 * k + 256 : 512 * k + 512, 256:512] = c

    lanes = lax.rem(lax.broadcasted_iota(jnp.int32, (1, 512), 1), 128)
    for half in range(2):
        late = lanes >= 64 if half == 0 else lanes < 64
        sign = 1.0 - 2.0 * jnp.where(late, h, 0).astype(F32)
        stack = []
        for b in (half, half + 2):
            sine, cosine = sincos(phi[:, 512 * b : 512 * b + 512])
            stack += [*split(cosine), *split(sine)]
        got = dot_t(jnp.concatenate(stack, axis=0), perm[half])
        for k, b in enumerate((half, half + 2)):
            for part in range(2):
                at = 128 * k + 64 * part
                e_own[part, :, 512 * b : 512 * b + 512] = (got[at : at + 32] + got[at + 32 : at + 64]) * sign
    e_copy = remote(e_own, e_other, prm_s.at[2], prm_r.at[2], core)
    e_copy.start()

    prm_core.wait()
    prm_strip.wait()
    both = prm[...] + prm_in[...]
    shift = both[0:1, :]
    col = lax.broadcasted_iota(jnp.int32, (NT, 128), 1)
    freq = lax.rem(lax.rem(col, 64) + 32 * g, NF)
    angle = (2.0 * math.pi / NF) * lax.rem(lax.broadcasted_iota(jnp.int32, (NT, 128), 0) * freq, NF).astype(F32)
    scale = 1.0 / math.sqrt(NF)
    real_in = col < 64

    def base(tile):
        phase = jnp.zeros((1, 128), F32)
        for t in range(4):
            phase = phase + jnp.where(tile == float(t), both[1 + t : 2 + t, :], 0.0)
        im, re = sincos(angle + phase)
        im, re = im * scale, re * scale
        return jnp.concatenate([jnp.where(real_in, re, -im), jnp.where(real_in, im, re)], axis=0)

    far = (4 * (1 - 2 * odd)).astype(F32)
    inside = jnp.where(odd == 1, (s > 1).astype(F32), (s < strips - 2).astype(F32))
    for nd in range(4):
        dest = block_of(nd)
        here, there = base(prm[8 + nd : 9 + nd, :]), base(prm_pair[pl.ds(8 + dest, 1), :])
        rows = slice(64 * nd, 64 * nd + 64)
        for n in range(4):
            source = block_of(n)
            own_hi, own_lo = split(jnp.where(shift == (nd - source).astype(F32), here, 0.0))
            step = (dest - source).astype(F32)
            pair_hi, pair_lo = split(jnp.where(shift == step + far, there, 0.0))
            halo_hi, halo_lo = split(jnp.where(shift == step - far, there * inside, 0.0))
            below = slice(256 + 64 * nd, 320 + 64 * nd)
            for k, (u, v, w) in enumerate(
                ((own_hi, pair_hi, halo_hi), (own_hi, pair_hi, halo_hi), (own_lo, pair_lo, halo_lo))
            ):
                at = 512 * k + 128 * n
                ww[rows, at : at + 128] = u
                ww[below, at : at + 128] = v
                wh[n, rows, 128 * k : 128 * k + 128] = w
    for i in (2, 3, 5, 6, 7):
        snd_copy(i).wait_recv()
    e_copy.wait()

    def spectrum(a, b, i, at, depth):
        re = jnp.concatenate([a[i, 0], b[i, 0]], axis=0)
        im = jnp.concatenate([a[i, 1], b[i, 1]], axis=0)
        for half_p, parts in enumerate(butterflies(re, im, tw)):
            for j, pieces in enumerate(parts):
                for half, w in enumerate(pieces):
                    hi, lo = split(w)
                    for k, x in enumerate((hi, lo, hi)):
                        at_k = 512 * k + 256 * half
                        spread[half_p, 64 * j : 64 * j + 64, at_k : at_k + 256] = x
        even, uneven = (dot(spread[k], table[k]) for k in range(2))
        early = lax.broadcasted_iota(jnp.int32, (64, 128), 1) < 64
        for j in range(4):
            for b4 in range(4):
                first, second = (even, uneven) if b4 % 2 == 0 else (uneven, even)
                rows = slice(64 * j, 64 * j + 64)
                c0 = 128 * (b4 // 2)
                u = jnp.where(early, first[rows, c0 : c0 + 128], second[rows, c0 : c0 + 128])
                v = jnp.where(early, first[rows, 256 + c0 : 384 + c0], second[rows, 256 + c0 : 384 + c0])
                e0 = 512 * b4 + 128 * j
                c, w = (
                    jnp.concatenate([e_own[part, :, e0 : e0 + 128], e_other[part, :, e0 : e0 + 128]], axis=0)
                    for part in range(2)
                )
                for half, value in enumerate((u * c - v * w, u * w + v * c)):
                    hi, lo = split(value)
                    for k, x in enumerate((hi, lo, hi)):
                        spec[b4, pl.ds(k * depth + at + 64 * half, 64), 128 * j : 128 * j + 128] = x

    def block_at(dg, dh):
        return 2 * lax.rem(g + dg, 2) + lax.rem(h + dh, 2)

    def near_copy(ii):
        return remote(near.at[1, ii], near_in.at[ii], near_s.at[ii], near_r.at[ii], core)

    def dest_rows(n):
        return pl.ds(pl.multiple_of(64 * (3 - block_of(n)), 64), 64)

    def row_copy(dg, i):
        at, ii = dest_rows(lax.rem(i, 4)), i // 4
        return remote(side.at[dg, ii, at], side_in.at[dg, ii, at], row_s.at[dg, i], row_r.at[dg, i], peer(dg, 0, 1))

    def opp_cross(i):
        return remote(opp.at[i], relay_in.at[i], rel_s.at[i], rel_r.at[i], peer(0, 1, 1))

    def opp_direct(i):
        return remote(opp.at[i], relay_in.at[i], rel_s.at[i], rel_r.at[i], peer(0, 0, 1))

    def cross_copy(dg, i):
        return remote(cross.at[dg, i], cross_in.at[dg, i], crs_s.at[dg, i], crs_r.at[dg, i], peer(dg, 1, 1))

    def own_rows(ii):
        def one(n, carry):
            @pl.when(jnp.logical_and(ii == 0, n == 1))
            def _():
                a_copy(2).start()
                b_copy(2).start()

            @pl.when(jnp.logical_and(ii == 0, n == 3))
            def _():
                pass_on(2, 0)
                for which in range(2):
                    via_copy(1, 1, which).start()
                a_copy(3).start()
                b_copy(3).start()

            spectrum(keep, other, 4 * ii + n, pl.multiple_of(128 * n, 128), 512)
            return carry

        lax.fori_loop(0, 4, one, 0)
        for dh in (1, 0):
            for dg in range(2):
                total = dot(ww[...], spec[block_at(dg, dh)])
                if dh == 0:
                    near[dg, ii] = total[0:256]
                else:
                    side[dg, ii] = total[0:256]
                    for n in (1, 3):
                        row_copy(dg, 4 * ii + n).start()
                pp[2 * dg + dh, ii] = total[256:512]
        near_copy(ii).start()

    def collect(i):
        n, ii = lax.rem(i, 4), i // 4
        at = dest_rows(n)
        for dg in range(2):
            cross_copy(dg, i).wait()
        parts = [
            near[0, ii, at, :] + side_in[0, ii, at, :] + cross_in[0, i],
            near_in[ii, at, :] + side_in[1, ii, at, :] + cross_in[1, i],
        ]
        got = dot(jnp.concatenate(split(jnp.concatenate(parts, axis=0)), axis=0), perm[h])
        rows = got[0:128] + got[128:256]
        for dg in range(2):
            row = 4 * (3 - block_of(n)) + 2 * lax.rem(g + dg, 2) + ii
            for c in range(4):
                for part in range(2):
                    at = 64 * dg + 32 * part
                    flat[c, part, pl.ds(row, 32, stride=16), :] = rows[at : at + 32, 128 * c : 128 * c + 128]

    def relay(i):
        n, ii = lax.rem(i, 4), i // 4

        @pl.when(lax.rem(i, 2) == 0)
        def _():
            opp_cross(i).wait()
            at = dest_rows(n)
            for dg in range(2):
                side[dg, ii, at, :] = side[dg, ii, at, :] + relay_in[i, dg]
                row_copy(dg, i).start()

        @pl.when(lax.rem(i, 2) == 1)
        def _():
            opp_direct(i).wait()
            for dg in range(2):
                cross[dg, i] = cross[dg, i] + relay_in[i, dg]
                cross_copy(dg, i).start()

    def step(i, carry):
        n, ii = lax.rem(i, 4), i // 4

        @pl.when(i == 1)
        def _():
            a_copy(5).start()
            b_copy(5).start()

        @pl.when(i == 2)
        def _():
            pass_on(3, 0)
            a_copy(6).start()
            b_copy(6).start()

        @pl.when(i == 3)
        def _():
            pass_on(2, 1)

        @pl.when(i == 5)
        def _():
            pass_on(3, 1)

        @pl.when(jnp.logical_or(i == 0, i == 3))
        def _():
            own_rows(i // 3)

        a_copy(i).wait_recv()
        b_copy(i).wait_recv()

        spectrum(halo_a, halo_b, i, 0, 128)
        mine = pl.ds(pl.multiple_of(64 * n, 64), 64)
        for dh in range(2):
            for dg in range(2):
                total = dot(wh[n], spec[block_at(dg, dh), 0:384, :])
                pp[2 * dg + dh, ii] = pp[2 * dg + dh, ii] + total
                if dh == 0:
                    opp[i, dg] = pp[2 * dg, ii, mine, :]
                else:
                    cross[dg, i] = pp[2 * dg + 1, ii, mine, :]
            if dh == 0:

                @pl.when(lax.rem(i, 2) == 0)
                def _():
                    opp_cross(i).start()

                @pl.when(lax.rem(i, 2) == 1)
                def _():
                    opp_direct(i).start()

        @pl.when(lax.rem(i, 2) == 0)
        def _():
            for dg in range(2):
                cross_copy(dg, i).start()

        @pl.when(i >= 1)
        def _():
            relay(i - 1)

        @pl.when(i >= 4)
        def _():
            @pl.when(i == 4)
            def _():
                near_copy(0).wait()

            for dg in range(2):
                row_copy(dg, i - 4).wait()
            collect(i - 4)

        return carry

    lax.fori_loop(0, 8, step, 0)
    relay(7)
    near_copy(1).wait()

    def last(i, carry):
        for dg in range(2):
            row_copy(dg, i).wait()
        collect(i)
        return carry

    lax.fori_loop(4, 8, last, 0)
    results = [
        pltpu.make_async_copy(flat.at[c], out.at[:, :, pl.ds(128 * c, 128)], load_sem.at[c]) for c in range(4)
    ]
    for c in results:
        c.start()
    for i in range(8):
        snd_copy(i).wait_send()
        if i not in (4, 7):
            a_copy(i).wait_send()
            b_copy(i).wait_send()
    for hops in range(1, 4):
        for k in range(2):
            for which in range(2):
                via_copy(hops, k, which).wait_send()
    for c in results:
        c.wait()


def local(strips, field, spectral_phase, chirp_shift, tile_map, tile_phase):
    waves, tw = dft_tables()
    vmem = pl.BlockSpec(memory_space=pltpu.VMEM)
    hbm = pl.BlockSpec(memory_space=pl.ANY)
    rows = pltpu.VMEM((8, 2, 32, 1024), F32)
    small = pltpu.VMEM((16, 128), F32)
    phase = pltpu.VMEM((2, 32, NY), F32)
    sums = pltpu.VMEM((2, 2, 256, 512), F32)
    dma = pltpu.SemaphoreType.DMA
    out = pl.pallas_call(
        functools.partial(kernel, strips),
        in_specs=[hbm, hbm, hbm, hbm, vmem, vmem, pl.BlockSpec(memory_space=pltpu.SMEM)],
        out_specs=pl.BlockSpec(memory_space=pl.ANY),
        out_shape=jax.ShapeDtypeStruct((2, 512, 512), F32),
        scratch_shapes=[
            pltpu.VMEM((8, 2, 512, 128), F32),
            rows, rows, rows, rows, rows,
            small, small, small, small,
            pltpu.VMEM((32, NY), F32),
            pltpu.VMEM(waves.shape, F32),
            pltpu.VMEM(tw.shape, F32),
            phase, phase,
            pltpu.VMEM((2, 1536, 512), BF),
            pltpu.VMEM((2, 512, 512), BF),
            pltpu.VMEM((512, 1536), BF),
            pltpu.VMEM((4, 256, 384), BF),
            pltpu.VMEM((2, 256, 1536), BF),
            pltpu.VMEM((4, 1536, 512), BF),
            sums,
            pltpu.VMEM((2, 256, 512), F32),
            sums, sums,
            pltpu.VMEM((4, 2, 256, 512), F32),
            pltpu.VMEM((8, 2, 64, 512), F32),
            pltpu.VMEM((8, 2, 64, 512), F32),
            pltpu.VMEM((2, 8, 64, 512), F32),
            pltpu.VMEM((2, 8, 64, 512), F32),
            pltpu.VMEM((2, 2, 2, 32, 1024), F32),
            pltpu.VMEM((2, 2, 2, 32, 1024), F32),
            dma((11,)),
            *[dma((8,))] * 6,
            dma((3,)), dma((3,)),
            dma((2,)), dma((2,)),
            dma((2, 8)), dma((2, 8)),
            dma((8,)), dma((8,)),
            dma((2, 8)), dma((2, 8)),
            *[dma((2, 2))] * 4,
        ],
        compiler_params=pltpu.CompilerParams(
            collective_id=0, has_side_effects=True, vmem_limit_bytes=VMEM * 2**20
        ),
        cost_estimate=pl.CostEstimate(flops=40 * 10**9, bytes_accessed=10 * 2**20, transcendentals=0),
    )(
        field.reshape(2, 512, 1024), spectral_phase, jnp.asarray(waves), jnp.asarray(tw),
        chirp_shift.reshape(1, 32), tile_phase, tile_map,
    )
    return out.reshape(2, NT, 16, 512)


def solution(mesh):
    placed = (P(None, "freq", "xs", "yh"), P("freq", None), P("freq"), P("xs"), P(None, "freq"))
    return jax.shard_map(
        functools.partial(local, mesh.shape["xs"]),
        mesh=mesh,
        in_specs=placed,
        out_specs=P(None, None, "xs", ("freq", "yh")),
        check_vma=False,
    )
```

```python
import functools
import math

import jax
import jax.numpy as jnp
import numpy as np
from jax import lax
from jax.experimental import pallas as pl
from jax.experimental.pallas import tpu as pltpu
from jax.sharding import PartitionSpec as P

NF = 64
NY = 2048
NT = 32
VMEM = 60
BF = jnp.bfloat16
F32 = jnp.float32
AXES = ("freq", "xs", "yh")
MESH = pl.DeviceIdType.MESH


def dft_tables():
    m = np.arange(256)
    angle = 2.0 * np.pi * (np.outer(m, m) % 256) / 256
    waves = np.stack([np.cos(angle), np.sin(angle)]) / math.sqrt(NY)
    odd_order = np.concatenate([np.arange(64) + 64 * b for b in (1, 0, 3, 2)])
    turn = 2.0 * np.pi * np.outer(np.arange(8), m) / NY
    twiddle = np.stack([np.cos(turn), np.sin(turn)])
    return np.stack([waves, waves[:, :, odd_order]]).astype(np.float32), twiddle.astype(np.float32)


def split(value):
    high = value.astype(BF)
    return high, (value - high.astype(F32)).astype(BF)


def dot(a, b):
    return jnp.dot(a, b, preferred_element_type=F32)


def dot_t(a, b):
    return lax.dot_general(a, b, (((1,), (1,)), ((), ())), preferred_element_type=F32)


def sincos(x):
    k = jnp.floor(x * (2.0 / math.pi) + 0.5)
    r = ((x - k * 1.5703125) - k * 4.837512969970703125e-4) - k * 7.54978995489188216e-8
    z = r * r
    sine = r + r * z * (-1.6666654611e-1 + z * (8.3321608736e-3 - z * 1.9515295891e-4))
    cosine = (1.0 - 0.5 * z) + z * z * (4.166664568298827e-2 + z * (-1.388731625493765e-3 + z * 2.443315711809948e-5))
    half = jnp.floor(k * 0.5)
    swap = (k - 2.0 * half) > 0.5
    sign = 1.0 - 2.0 * (half - 2.0 * jnp.floor(half * 0.5))
    return sign * jnp.where(swap, cosine, sine), sign * jnp.where(swap, -sine, cosine)


def butterflies(re, im, tw):
    a = [(re[:, 256 * c : 256 * c + 256], im[:, 256 * c : 256 * c + 256]) for c in range(4)]
    r = math.sqrt(0.5)

    def add(u, v):
        return u[0] + v[0], u[1] + v[1]

    def sub(u, v):
        return u[0] - v[0], u[1] - v[1]

    def mi(u):
        return u[1], -u[0]

    def four(b):
        e0, e1 = add(b[0], b[2]), sub(b[0], b[2])
        e2, e3 = add(b[1], b[3]), mi(sub(b[1], b[3]))
        return add(e0, e2), add(e1, e3), sub(e0, e2), sub(e1, e3)

    even = four(a)
    b1 = ((a[1][0] + a[1][1]) * r, (a[1][1] - a[1][0]) * r)
    b3 = ((a[3][1] - a[3][0]) * r, (-a[3][0] - a[3][1]) * r)
    odd = four((a[0], b1, mi(a[2]), b3))
    both = []
    for side, parts in enumerate((even, odd)):
        row = []
        for j in range(4):
            p = 2 * j + side
            u = parts[j]
            if p:
                c, s = tw[0, p : p + 1, :], tw[1, p : p + 1, :]
                u = u[0] * c + u[1] * s, u[1] * c - u[0] * s
            row.append(u)
        both.append(row)
    return both


def kernel(
    strips, field, phi_hbm, waves_hbm, tw_hbm, shift_row, tile_phase, tile_ids, out,
    flat, snd, keep, other, halo_a, halo_b, prm, prm_out, prm_in, prm_pair,
    phi, waves, tw, e_own, e_other, table, perm, ww, wh,
    spread, spec, near, near_in, side, side_in, pp, opp, relay_in, cross, cross_in, via_1, via_2, *rest,
):
    (load_sem, snd_s, snd_r, ha_s, ha_r, hb_s, hb_r, prm_s, prm_r,
     near_s, near_r, row_s, row_r, rel_s, rel_r, crs_s, crs_r, v1_s, v1_r, v2_s, v2_r) = rest
    g, s, h = (lax.axis_index(a) for a in AXES)
    odd = lax.rem(s, 2)
    pair = s + 1 - 2 * odd
    onward = lax.rem(s + strips + 4 * odd - 2, strips)
    back = lax.rem(s + strips + 2 - 4 * odd, strips)
    core = (1 - g, s, h)

    z, y, turns = s // 8, lax.rem(s // 2, 4), strips // 8
    hop = 1 - 2 * odd
    across = 8 * z + 2 * lax.rem(y + 4 + hop, 4) + odd
    across_from = 8 * z + 2 * lax.rem(y + 4 - hop, 4) + odd
    z_on = 8 * lax.rem(z + turns - hop, turns) + odd
    z_back = 8 * lax.rem(z + turns + hop, turns) + odd
    leaves = (y == 2 - odd).astype(jnp.int32)
    third = across + leaves * (z_on + 2 * (3 - 3 * odd) - across)
    enters = (y == 3 - 3 * odd).astype(jnp.int32)
    third_from = across_from + enters * (z_back + 2 * (2 - odd) - across_from)

    def peer(dg, ds, dh):
        return (lax.rem(g + dg, 2), pair if ds else s, lax.rem(h + dh, 2))

    def remote(src, dst, a, b, to):
        return pltpu.make_async_remote_copy(
            src_ref=src, dst_ref=dst, send_sem=a, recv_sem=b, device_id=to, device_id_type=MESH
        )

    def block_of(n):
        return n + odd * (3 - 2 * n)

    loads = [
        pltpu.make_async_copy(field.at[:, :, pl.ds(128 * y, 128)], flat.at[y], load_sem.at[y]) for y in range(8)
    ]
    tables = [
        pltpu.make_async_copy(src, dst, load_sem.at[8 + k])
        for k, (src, dst) in enumerate(((waves_hbm, waves), (tw_hbm, tw), (phi_hbm, phi)))
    ]
    for c in loads + tables:
        c.start()
    barrier = pltpu.get_barrier_semaphore()
    greet = [core, peer(0, 0, 1), peer(1, 0, 1), peer(0, 1, 1), peer(1, 1, 1), (g, onward, h), (g, back, h)]
    greet += [(g, across, h), (g, across_from, h), (g, third, h), (g, third_from, h)]
    for to in greet:
        pl.semaphore_signal(barrier, inc=1, device_id=to, device_id_type=MESH)

    def snd_copy(i):
        return remote(snd.at[i], other.at[i], snd_s.at[i], snd_r.at[i], core)

    def a_copy(i):
        return remote(keep.at[i], halo_a.at[i], ha_s.at[i], ha_r.at[i], (g, onward, h))

    def b_copy(i):
        return remote(other.at[i], halo_b.at[i], hb_s.at[i], hb_r.at[i], (g, onward, h))

    def via_copy(hops, k, which):
        i = 4 + 3 * k
        if hops == 1:
            src = (keep, other)[which].at[i]
            return remote(src, via_1.at[k, which], v1_s.at[k, which], v1_r.at[k, which], (g, across, h))
        if hops == 2:
            return remote(
                via_1.at[k, which], via_2.at[k, which], v2_s.at[k, which], v2_r.at[k, which], (g, across, h)
            )
        dst, sems = ((halo_a, (ha_s, ha_r)), (halo_b, (hb_s, hb_r)))[which]
        return remote(via_2.at[k, which], dst.at[i], sems[0].at[i], sems[1].at[i], (g, third, h))

    def pass_on(hops, k):
        for which in range(2):
            via_copy(hops - 1, k, which).wait_recv()
            via_copy(hops, k, which).start()

    def gather_rows(i, whose, into):
        row = 4 * block_of(lax.rem(i, 4)) + 2 * whose + i // 4
        for c in range(2):
            for y in range(8):
                into[i, c, :, 128 * y : 128 * y + 128] = flat[y, c, pl.ds(row, 32, stride=16), :]

    gap = jnp.zeros((8, 32), F32)
    rows = jnp.concatenate([shift_row[...].astype(F32), tile_phase[...], jnp.zeros((3, 32), F32)], axis=0)
    prm[0:8, :] = jnp.concatenate([rows, gap, rows, gap], axis=1)
    for rb in range(4):
        prm[8 + rb : 9 + rb, :] = jnp.full((1, 128), tile_ids[rb], jnp.int32).astype(F32)
    prm[12:16, :] = jnp.zeros((4, 128), F32)
    prm_out[...] = pltpu.roll(prm[...], 32, 1)
    prm_core = remote(prm_out, prm_in, prm_s.at[0], prm_r.at[0], core)
    prm_strip = remote(prm, prm_pair, prm_s.at[1], prm_r.at[1], peer(0, 1, 1))

    for c in loads:
        c.wait()

    def pack_send(i, carry):
        gather_rows(i, 1 - g, snd)
        snd_copy(i).start()
        return carry

    def pack_keep(i, carry):
        gather_rows(i, g, keep)
        return carry

    for i in (0, 4, 1):
        gather_rows(i, g, keep)
    pl.semaphore_wait(barrier, len(greet))
    a_copy(0).start()
    via_copy(1, 0, 0).start()
    a_copy(1).start()
    lax.fori_loop(0, 8, pack_send, 0)
    prm_core.start()
    prm_strip.start()
    lax.fori_loop(2, 4, pack_keep, 0)
    lax.fori_loop(5, 8, pack_keep, 0)
    for i in (0, 4, 1):
        snd_copy(i).wait_recv()
        if i == 4:
            via_copy(1, 0, 1).start()
        else:
            b_copy(i).start()

    for c in tables:
        c.wait()
    lane = lax.broadcasted_iota(jnp.int32, (512, 1), 0)
    wave = lax.broadcasted_iota(jnp.int32, (1, 512), 1)
    turn = lax.rem(lane, 128)
    for half in range(2):
        late = (turn >= 64).astype(jnp.int32)
        late = late if half == 0 else 1 - late
        target = 8 * lax.rem(turn, 64) + 2 * (lane // 128) + late
        perm[half] = jnp.where(target == wave, 1.0, 0.0).astype(BF)
        c_hi, c_lo = split(waves[half, 0])
        s_hi, s_lo = split(waves[half, 1])
        for k, (c, w) in enumerate(((c_hi, s_hi), (c_hi, s_hi), (c_lo, s_lo))):
            table[half, 512 * k : 512 * k + 256, 0:256] = c
            table[half, 512 * k : 512 * k + 256, 256:512] = -w
            table[half, 512 * k + 256 : 512 * k + 512, 0:256] = w
            table[half, 512 * k + 256 : 512 * k + 512, 256:512] = c

    lanes = lax.rem(lax.broadcasted_iota(jnp.int32, (1, 512), 1), 128)
    for half in range(2):
        late = lanes >= 64 if half == 0 else lanes < 64
        sign = 1.0 - 2.0 * jnp.where(late, h, 0).astype(F32)
        stack = []
        for b in (half, half + 2):
            sine, cosine = sincos(phi[:, 512 * b : 512 * b + 512])
            stack += [*split(cosine), *split(sine)]
        got = dot_t(jnp.concatenate(stack, axis=0), perm[half])
        for k, b in enumerate((half, half + 2)):
            for part in range(2):
                at = 128 * k + 64 * part
                e_own[part, :, 512 * b : 512 * b + 512] = (got[at : at + 32] + got[at + 32 : at + 64]) * sign
    e_copy = remote(e_own, e_other, prm_s.at[2], prm_r.at[2], core)
    e_copy.start()

    prm_core.wait()
    prm_strip.wait()
    both = prm[...] + prm_in[...]
    shift = both[0:1, :]
    col = lax.broadcasted_iota(jnp.int32, (NT, 128), 1)
    freq = lax.rem(lax.rem(col, 64) + 32 * g, NF)
    angle = (2.0 * math.pi / NF) * lax.rem(lax.broadcasted_iota(jnp.int32, (NT, 128), 0) * freq, NF).astype(F32)
    scale = 1.0 / math.sqrt(NF)
    real_in = col < 64

    def base(tile):
        phase = jnp.zeros((1, 128), F32)
        for t in range(4):
            phase = phase + jnp.where(tile == float(t), both[1 + t : 2 + t, :], 0.0)
        im, re = sincos(angle + phase)
        im, re = im * scale, re * scale
        return jnp.concatenate([jnp.where(real_in, re, -im), jnp.where(real_in, im, re)], axis=0)

    far = (4 * (1 - 2 * odd)).astype(F32)
    inside = jnp.where(odd == 1, (s > 1).astype(F32), (s < strips - 2).astype(F32))
    for nd in range(4):
        dest = block_of(nd)
        here, there = base(prm[8 + nd : 9 + nd, :]), base(prm_pair[pl.ds(8 + dest, 1), :])
        rows = slice(64 * nd, 64 * nd + 64)
        for n in range(4):
            source = block_of(n)
            own_hi, own_lo = split(jnp.where(shift == (nd - source).astype(F32), here, 0.0))
            step = (dest - source).astype(F32)
            pair_hi, pair_lo = split(jnp.where(shift == step + far, there, 0.0))
            halo_hi, halo_lo = split(jnp.where(shift == step - far, there * inside, 0.0))
            below = slice(256 + 64 * nd, 320 + 64 * nd)
            for k, (u, v, w) in enumerate(
                ((own_hi, pair_hi, halo_hi), (own_hi, pair_hi, halo_hi), (own_lo, pair_lo, halo_lo))
            ):
                at = 512 * k + 128 * n
                ww[rows, at : at + 128] = u
                ww[below, at : at + 128] = v
                wh[n, rows, 128 * k : 128 * k + 128] = w
    for i in (2, 3, 5, 6, 7):
        snd_copy(i).wait_recv()
    e_copy.wait()

    def spectrum(a, b, i, at, depth):
        re = jnp.concatenate([a[i, 0], b[i, 0]], axis=0)
        im = jnp.concatenate([a[i, 1], b[i, 1]], axis=0)
        for half_p, parts in enumerate(butterflies(re, im, tw)):
            for j, pieces in enumerate(parts):
                for half, w in enumerate(pieces):
                    hi, lo = split(w)
                    for k, x in enumerate((hi, lo, hi)):
                        at_k = 512 * k + 256 * half
                        spread[half_p, 64 * j : 64 * j + 64, at_k : at_k + 256] = x
        even, uneven = (dot(spread[k], table[k]) for k in range(2))
        early = lax.broadcasted_iota(jnp.int32, (64, 128), 1) < 64
        for j in range(4):
            for b4 in range(4):
                first, second = (even, uneven) if b4 % 2 == 0 else (uneven, even)
                rows = slice(64 * j, 64 * j + 64)
                c0 = 128 * (b4 // 2)
                u = jnp.where(early, first[rows, c0 : c0 + 128], second[rows, c0 : c0 + 128])
                v = jnp.where(early, first[rows, 256 + c0 : 384 + c0], second[rows, 256 + c0 : 384 + c0])
                e0 = 512 * b4 + 128 * j
                c, w = (
                    jnp.concatenate([e_own[part, :, e0 : e0 + 128], e_other[part, :, e0 : e0 + 128]], axis=0)
                    for part in range(2)
                )
                for half, value in enumerate((u * c - v * w, u * w + v * c)):
                    hi, lo = split(value)
                    for k, x in enumerate((hi, lo, hi)):
                        spec[b4, pl.ds(k * depth + at + 64 * half, 64), 128 * j : 128 * j + 128] = x

    def block_at(dg, dh):
        return 2 * lax.rem(g + dg, 2) + lax.rem(h + dh, 2)

    def near_copy(ii):
        return remote(near.at[1, ii], near_in.at[ii], near_s.at[ii], near_r.at[ii], core)

    def dest_rows(n):
        return pl.ds(pl.multiple_of(64 * (3 - block_of(n)), 64), 64)

    def row_copy(dg, i):
        at, ii = dest_rows(lax.rem(i, 4)), i // 4
        return remote(side.at[dg, ii, at], side_in.at[dg, ii, at], row_s.at[dg, i], row_r.at[dg, i], peer(dg, 0, 1))

    def opp_cross(i):
        return remote(opp.at[i], relay_in.at[i], rel_s.at[i], rel_r.at[i], peer(0, 1, 1))

    def opp_direct(i):
        return remote(opp.at[i], relay_in.at[i], rel_s.at[i], rel_r.at[i], peer(0, 0, 1))

    def cross_copy(dg, i):
        return remote(cross.at[dg, i], cross_in.at[dg, i], crs_s.at[dg, i], crs_r.at[dg, i], peer(dg, 1, 1))

    def own_rows(ii):
        def one(n, carry):
            @pl.when(jnp.logical_and(ii == 0, n == 1))
            def _():
                a_copy(2).start()
                b_copy(2).start()

            @pl.when(jnp.logical_and(ii == 0, n == 3))
            def _():
                pass_on(2, 0)
                for which in range(2):
                    via_copy(1, 1, which).start()
                a_copy(3).start()
                b_copy(3).start()

            spectrum(keep, other, 4 * ii + n, pl.multiple_of(128 * n, 128), 512)
            return carry

        lax.fori_loop(0, 4, one, 0)
        for dh in (1, 0):
            for dg in range(2):
                total = dot(ww[...], spec[block_at(dg, dh)])
                if dh == 0:
                    near[dg, ii] = total[0:256]
                else:
                    side[dg, ii] = total[0:256]
                    for n in (1, 3):
                        row_copy(dg, 4 * ii + n).start()
                pp[2 * dg + dh, ii] = total[256:512]
        near_copy(ii).start()

    def collect(i):
        n, ii = lax.rem(i, 4), i // 4
        at = dest_rows(n)
        for dg in range(2):
            cross_copy(dg, i).wait()
        parts = [
            near[0, ii, at, :] + side_in[0, ii, at, :] + cross_in[0, i],
            near_in[ii, at, :] + side_in[1, ii, at, :] + cross_in[1, i],
        ]
        got = dot(jnp.concatenate(split(jnp.concatenate(parts, axis=0)), axis=0), perm[h])
        rows = got[0:128] + got[128:256]
        for dg in range(2):
            row = 4 * (3 - block_of(n)) + 2 * lax.rem(g + dg, 2) + ii
            for c in range(4):
                for part in range(2):
                    at = 64 * dg + 32 * part
                    flat[c, part, pl.ds(row, 32, stride=16), :] = rows[at : at + 32, 128 * c : 128 * c + 128]

    def relay(i):
        n, ii = lax.rem(i, 4), i // 4

        @pl.when(lax.rem(i, 2) == 0)
        def _():
            opp_cross(i).wait()
            at = dest_rows(n)
            for dg in range(2):
                side[dg, ii, at, :] = side[dg, ii, at, :] + relay_in[i, dg]
                row_copy(dg, i).start()

        @pl.when(lax.rem(i, 2) == 1)
        def _():
            opp_direct(i).wait()
            for dg in range(2):
                cross[dg, i] = cross[dg, i] + relay_in[i, dg]
                cross_copy(dg, i).start()

    def step(i, carry):
        n, ii = lax.rem(i, 4), i // 4

        @pl.when(i == 1)
        def _():
            a_copy(5).start()
            b_copy(5).start()

        @pl.when(i == 2)
        def _():
            pass_on(3, 0)
            a_copy(6).start()
            b_copy(6).start()

        @pl.when(i == 3)
        def _():
            pass_on(2, 1)

        @pl.when(i == 5)
        def _():
            pass_on(3, 1)

        @pl.when(jnp.logical_or(i == 0, i == 3))
        def _():
            own_rows(i // 3)

        a_copy(i).wait_recv()
        b_copy(i).wait_recv()

        spectrum(halo_a, halo_b, i, 0, 128)
        mine = pl.ds(pl.multiple_of(64 * n, 64), 64)
        for dh in range(2):
            for dg in range(2):
                total = dot(wh[n], spec[block_at(dg, dh), 0:384, :])
                pp[2 * dg + dh, ii] = pp[2 * dg + dh, ii] + total
                if dh == 0:
                    opp[i, dg] = pp[2 * dg, ii, mine, :]
                else:
                    cross[dg, i] = pp[2 * dg + 1, ii, mine, :]
            if dh == 0:

                @pl.when(lax.rem(i, 2) == 0)
                def _():
                    opp_cross(i).start()

                @pl.when(lax.rem(i, 2) == 1)
                def _():
                    opp_direct(i).start()

        @pl.when(lax.rem(i, 2) == 0)
        def _():
            for dg in range(2):
                cross_copy(dg, i).start()

        @pl.when(i >= 1)
        def _():
            relay(i - 1)

        @pl.when(i >= 4)
        def _():
            @pl.when(i == 4)
            def _():
                near_copy(0).wait()

            for dg in range(2):
                row_copy(dg, i - 4).wait()
            collect(i - 4)

        return carry

    lax.fori_loop(0, 8, step, 0)
    relay(7)
    near_copy(1).wait()

    def last(i, carry):
        for dg in range(2):
            row_copy(dg, i).wait()
        collect(i)
        return carry

    lax.fori_loop(4, 8, last, 0)
    results = [
        pltpu.make_async_copy(flat.at[c], out.at[:, :, pl.ds(128 * c, 128)], load_sem.at[c]) for c in range(4)
    ]
    for c in results:
        c.start()
    for i in range(8):
        snd_copy(i).wait_send()
        if i not in (4, 7):
            a_copy(i).wait_send()
            b_copy(i).wait_send()
    for hops in range(1, 4):
        for k in range(2):
            for which in range(2):
                via_copy(hops, k, which).wait_send()
    for c in results:
        c.wait()


def local(strips, field, spectral_phase, chirp_shift, tile_map, tile_phase):
    waves, tw = dft_tables()
    vmem = pl.BlockSpec(memory_space=pltpu.VMEM)
    hbm = pl.BlockSpec(memory_space=pl.ANY)
    rows = pltpu.VMEM((8, 2, 32, 1024), F32)
    small = pltpu.VMEM((16, 128), F32)
    phase = pltpu.VMEM((2, 32, NY), F32)
    sums = pltpu.VMEM((2, 2, 256, 512), F32)
    dma = pltpu.SemaphoreType.DMA
    out = pl.pallas_call(
        functools.partial(kernel, strips),
        in_specs=[hbm, hbm, hbm, hbm, vmem, vmem, pl.BlockSpec(memory_space=pltpu.SMEM)],
        out_specs=pl.BlockSpec(memory_space=pl.ANY),
        out_shape=jax.ShapeDtypeStruct((2, 512, 512), F32),
        scratch_shapes=[
            pltpu.VMEM((8, 2, 512, 128), F32),
            rows, rows, rows, rows, rows,
            small, small, small, small,
            pltpu.VMEM((32, NY), F32),
            pltpu.VMEM(waves.shape, F32),
            pltpu.VMEM(tw.shape, F32),
            phase, phase,
            pltpu.VMEM((2, 1536, 512), BF),
            pltpu.VMEM((2, 512, 512), BF),
            pltpu.VMEM((512, 1536), BF),
            pltpu.VMEM((4, 256, 384), BF),
            pltpu.VMEM((2, 256, 1536), BF),
            pltpu.VMEM((4, 1536, 512), BF),
            sums,
            pltpu.VMEM((2, 256, 512), F32),
            sums, sums,
            pltpu.VMEM((4, 2, 256, 512), F32),
            pltpu.VMEM((8, 2, 64, 512), F32),
            pltpu.VMEM((8, 2, 64, 512), F32),
            pltpu.VMEM((2, 8, 64, 512), F32),
            pltpu.VMEM((2, 8, 64, 512), F32),
            pltpu.VMEM((2, 2, 2, 32, 1024), F32),
            pltpu.VMEM((2, 2, 2, 32, 1024), F32),
            dma((11,)),
            *[dma((8,))] * 6,
            dma((3,)), dma((3,)),
            dma((2,)), dma((2,)),
            dma((2, 8)), dma((2, 8)),
            dma((8,)), dma((8,)),
            dma((2, 8)), dma((2, 8)),
            *[dma((2, 2))] * 4,
        ],
        compiler_params=pltpu.CompilerParams(
            collective_id=0, has_side_effects=True, vmem_limit_bytes=VMEM * 2**20
        ),
        cost_estimate=pl.CostEstimate(flops=40 * 10**9, bytes_accessed=10 * 2**20, transcendentals=0),
    )(
        field.reshape(2, 512, 1024), spectral_phase, jnp.asarray(waves), jnp.asarray(tw),
        chirp_shift.reshape(1, 32), tile_phase, tile_map,
    )
    return out.reshape(2, NT, 16, 512)


def solution(mesh):
    placed = (P(None, "freq", "xs", "yh"), P("freq", None), P("freq"), P("xs"), P(None, "freq"))
    return jax.shard_map(
        functools.partial(local, mesh.shape["xs"]),
        mesh=mesh,
        in_specs=placed,
        out_specs=P(None, None, "xs", ("freq", "yh")),
        check_vma=False,
    )
```

```python
import functools
import math

import jax
import jax.numpy as jnp
import numpy as np
from jax import lax
from jax.experimental import pallas as pl
from jax.experimental.pallas import tpu as pltpu
from jax.sharding import PartitionSpec as P

NF = 64
NY = 2048
NT = 32
VMEM = 60
BF = jnp.bfloat16
F32 = jnp.float32
AXES = ("freq", "xs", "yh")
MESH = pl.DeviceIdType.MESH


def dft_tables():
    m = np.arange(256)
    angle = 2.0 * np.pi * (np.outer(m, m) % 256) / 256
    waves = np.stack([np.cos(angle), np.sin(angle)]) / math.sqrt(NY)
    odd_order = np.concatenate([np.arange(64) + 64 * b for b in (1, 0, 3, 2)])
    turn = 2.0 * np.pi * np.outer(np.arange(8), m) / NY
    twiddle = np.stack([np.cos(turn), np.sin(turn)])
    return np.stack([waves, waves[:, :, odd_order]]).astype(np.float32), twiddle.astype(np.float32)


def split(value):
    high = value.astype(BF)
    return high, (value - high.astype(F32)).astype(BF)


def dot(a, b):
    return jnp.dot(a, b, preferred_element_type=F32)


def dot_t(a, b):
    return lax.dot_general(a, b, (((1,), (1,)), ((), ())), preferred_element_type=F32)


def sincos(x):
    k = jnp.floor(x * (2.0 / math.pi) + 0.5)
    r = ((x - k * 1.5703125) - k * 4.837512969970703125e-4) - k * 7.54978995489188216e-8
    z = r * r
    sine = r + r * z * (-1.6666654611e-1 + z * (8.3321608736e-3 - z * 1.9515295891e-4))
    cosine = (1.0 - 0.5 * z) + z * z * (4.166664568298827e-2 + z * (-1.388731625493765e-3 + z * 2.443315711809948e-5))
    half = jnp.floor(k * 0.5)
    swap = (k - 2.0 * half) > 0.5
    sign = 1.0 - 2.0 * (half - 2.0 * jnp.floor(half * 0.5))
    return sign * jnp.where(swap, cosine, sine), sign * jnp.where(swap, -sine, cosine)


def butterflies(re, im, tw):
    a = [(re[:, 256 * c : 256 * c + 256], im[:, 256 * c : 256 * c + 256]) for c in range(4)]
    r = math.sqrt(0.5)

    def add(u, v):
        return u[0] + v[0], u[1] + v[1]

    def sub(u, v):
        return u[0] - v[0], u[1] - v[1]

    def mi(u):
        return u[1], -u[0]

    def four(b):
        e0, e1 = add(b[0], b[2]), sub(b[0], b[2])
        e2, e3 = add(b[1], b[3]), mi(sub(b[1], b[3]))
        return add(e0, e2), add(e1, e3), sub(e0, e2), sub(e1, e3)

    even = four(a)
    b1 = ((a[1][0] + a[1][1]) * r, (a[1][1] - a[1][0]) * r)
    b3 = ((a[3][1] - a[3][0]) * r, (-a[3][0] - a[3][1]) * r)
    odd = four((a[0], b1, mi(a[2]), b3))
    both = []
    for side, parts in enumerate((even, odd)):
        row = []
        for j in range(4):
            p = 2 * j + side
            u = parts[j]
            if p:
                c, s = tw[0, p : p + 1, :], tw[1, p : p + 1, :]
                u = u[0] * c + u[1] * s, u[1] * c - u[0] * s
            row.append(u)
        both.append(row)
    return both


def kernel(
    strips, field, phi_hbm, waves_hbm, tw_hbm, shift_row, tile_phase, tile_ids, out,
    flat, snd, keep, other, halo_a, halo_b, prm, prm_out, prm_in, prm_pair,
    phi, waves, tw, e_own, e_other, table, perm, ww, wh,
    spread, spec, near, near_in, side, side_in, pp, opp, relay_in, cross, cross_in, via_1, via_2, *rest,
):
    (load_sem, snd_s, snd_r, ha_s, ha_r, hb_s, hb_r, prm_s, prm_r,
     near_s, near_r, row_s, row_r, rel_s, rel_r, crs_s, crs_r, v1_s, v1_r, v2_s, v2_r) = rest
    g, s, h = (lax.axis_index(a) for a in AXES)
    odd = lax.rem(s, 2)
    pair = s + 1 - 2 * odd
    onward = lax.rem(s + strips + 4 * odd - 2, strips)
    back = lax.rem(s + strips + 2 - 4 * odd, strips)
    core = (1 - g, s, h)

    z, y, turns = s // 8, lax.rem(s // 2, 4), strips // 8
    hop = 1 - 2 * odd
    across = 8 * z + 2 * lax.rem(y + 4 + hop, 4) + odd
    across_from = 8 * z + 2 * lax.rem(y + 4 - hop, 4) + odd
    z_on = 8 * lax.rem(z + turns - hop, turns) + odd
    z_back = 8 * lax.rem(z + turns + hop, turns) + odd
    leaves = (y == 2 - odd).astype(jnp.int32)
    third = across + leaves * (z_on + 2 * (3 - 3 * odd) - across)
    enters = (y == 3 - 3 * odd).astype(jnp.int32)
    third_from = across_from + enters * (z_back + 2 * (2 - odd) - across_from)

    def peer(dg, ds, dh):
        return (lax.rem(g + dg, 2), pair if ds else s, lax.rem(h + dh, 2))

    def remote(src, dst, a, b, to):
        return pltpu.make_async_remote_copy(
            src_ref=src, dst_ref=dst, send_sem=a, recv_sem=b, device_id=to, device_id_type=MESH
        )

    def block_of(n):
        return n + odd * (3 - 2 * n)

    loads = [
        pltpu.make_async_copy(field.at[:, :, pl.ds(128 * y, 128)], flat.at[y], load_sem.at[y]) for y in range(8)
    ]
    tables = [
        pltpu.make_async_copy(src, dst, load_sem.at[8 + k])
        for k, (src, dst) in enumerate(((waves_hbm, waves), (tw_hbm, tw), (phi_hbm, phi)))
    ]
    for c in loads + tables:
        c.start()
    barrier = pltpu.get_barrier_semaphore()
    greet = [core, peer(0, 0, 1), peer(1, 0, 1), peer(0, 1, 1), peer(1, 1, 1), (g, onward, h), (g, back, h)]
    greet += [(g, across, h), (g, across_from, h), (g, third, h), (g, third_from, h)]
    for to in greet:
        pl.semaphore_signal(barrier, inc=1, device_id=to, device_id_type=MESH)

    def snd_copy(i):
        return remote(snd.at[i], other.at[i], snd_s.at[i], snd_r.at[i], core)

    def a_copy(i):
        return remote(keep.at[i], halo_a.at[i], ha_s.at[i], ha_r.at[i], (g, onward, h))

    def b_copy(i):
        return remote(other.at[i], halo_b.at[i], hb_s.at[i], hb_r.at[i], (g, onward, h))

    def via_copy(hops, k, which):
        i = 4 + 2 * k
        if hops == 1:
            src = (keep, other)[which].at[i]
            return remote(src, via_1.at[k, which], v1_s.at[k, which], v1_r.at[k, which], (g, across, h))
        if hops == 2:
            return remote(
                via_1.at[k, which], via_2.at[k, which], v2_s.at[k, which], v2_r.at[k, which], (g, across, h)
            )
        dst, sems = ((halo_a, (ha_s, ha_r)), (halo_b, (hb_s, hb_r)))[which]
        return remote(via_2.at[k, which], dst.at[i], sems[0].at[i], sems[1].at[i], (g, third, h))

    def pass_on(hops, k):
        for which in range(2):
            via_copy(hops - 1, k, which).wait_recv()
            via_copy(hops, k, which).start()

    def gather_rows(i, whose, into):
        row = 4 * block_of(lax.rem(i, 4)) + 2 * whose + i // 4
        for c in range(2):
            for y in range(8):
                into[i, c, :, 128 * y : 128 * y + 128] = flat[y, c, pl.ds(row, 32, stride=16), :]

    gap = jnp.zeros((8, 32), F32)
    rows = jnp.concatenate([shift_row[...].astype(F32), tile_phase[...], jnp.zeros((3, 32), F32)], axis=0)
    prm[0:8, :] = jnp.concatenate([rows, gap, rows, gap], axis=1)
    for rb in range(4):
        prm[8 + rb : 9 + rb, :] = jnp.full((1, 128), tile_ids[rb], jnp.int32).astype(F32)
    prm[12:16, :] = jnp.zeros((4, 128), F32)
    prm_out[...] = pltpu.roll(prm[...], 32, 1)
    prm_core = remote(prm_out, prm_in, prm_s.at[0], prm_r.at[0], core)
    prm_strip = remote(prm, prm_pair, prm_s.at[1], prm_r.at[1], peer(0, 1, 1))

    for c in loads:
        c.wait()

    def pack_send(i, carry):
        gather_rows(i, 1 - g, snd)
        snd_copy(i).start()
        return carry

    def pack_keep(i, carry):
        gather_rows(i, g, keep)
        return carry

    for i in (0, 4):
        gather_rows(i, g, keep)
    pl.semaphore_wait(barrier, len(greet))
    a_copy(0).start()
    via_copy(1, 0, 0).start()
    lax.fori_loop(0, 8, pack_send, 0)
    prm_core.start()
    prm_strip.start()
    lax.fori_loop(1, 4, pack_keep, 0)
    lax.fori_loop(5, 8, pack_keep, 0)
    snd_copy(0).wait_recv()
    b_copy(0).start()
    snd_copy(4).wait_recv()
    via_copy(1, 0, 1).start()

    for c in tables:
        c.wait()
    lane = lax.broadcasted_iota(jnp.int32, (512, 1), 0)
    wave = lax.broadcasted_iota(jnp.int32, (1, 512), 1)
    turn = lax.rem(lane, 128)
    for half in range(2):
        late = (turn >= 64).astype(jnp.int32)
        late = late if half == 0 else 1 - late
        target = 8 * lax.rem(turn, 64) + 2 * (lane // 128) + late
        perm[half] = jnp.where(target == wave, 1.0, 0.0).astype(BF)
        c_hi, c_lo = split(waves[half, 0])
        s_hi, s_lo = split(waves[half, 1])
        for k, (c, w) in enumerate(((c_hi, s_hi), (c_hi, s_hi), (c_lo, s_lo))):
            table[half, 512 * k : 512 * k + 256, 0:256] = c
            table[half, 512 * k : 512 * k + 256, 256:512] = -w
            table[half, 512 * k + 256 : 512 * k + 512, 0:256] = w
            table[half, 512 * k + 256 : 512 * k + 512, 256:512] = c

    lanes = lax.rem(lax.broadcasted_iota(jnp.int32, (1, 512), 1), 128)
    for half in range(2):
        late = lanes >= 64 if half == 0 else lanes < 64
        sign = 1.0 - 2.0 * jnp.where(late, h, 0).astype(F32)
        stack = []
        for b in (half, half + 2):
            sine, cosine = sincos(phi[:, 512 * b : 512 * b + 512])
            stack += [*split(cosine), *split(sine)]
        got = dot_t(jnp.concatenate(stack, axis=0), perm[half])
        for k, b in enumerate((half, half + 2)):
            for part in range(2):
                at = 128 * k + 64 * part
                e_own[part, :, 512 * b : 512 * b + 512] = (got[at : at + 32] + got[at + 32 : at + 64]) * sign
    e_copy = remote(e_own, e_other, prm_s.at[2], prm_r.at[2], core)
    e_copy.start()

    prm_core.wait()
    prm_strip.wait()
    both = prm[...] + prm_in[...]
    shift = both[0:1, :]
    col = lax.broadcasted_iota(jnp.int32, (NT, 128), 1)
    freq = lax.rem(lax.rem(col, 64) + 32 * g, NF)
    angle = (2.0 * math.pi / NF) * lax.rem(lax.broadcasted_iota(jnp.int32, (NT, 128), 0) * freq, NF).astype(F32)
    scale = 1.0 / math.sqrt(NF)
    real_in = col < 64

    def base(tile):
        phase = jnp.zeros((1, 128), F32)
        for t in range(4):
            phase = phase + jnp.where(tile == float(t), both[1 + t : 2 + t, :], 0.0)
        im, re = sincos(angle + phase)
        im, re = im * scale, re * scale
        return jnp.concatenate([jnp.where(real_in, re, -im), jnp.where(real_in, im, re)], axis=0)

    far = (4 * (1 - 2 * odd)).astype(F32)
    inside = jnp.where(odd == 1, (s > 1).astype(F32), (s < strips - 2).astype(F32))
    for nd in range(4):
        dest = block_of(nd)
        here, there = base(prm[8 + nd : 9 + nd, :]), base(prm_pair[pl.ds(8 + dest, 1), :])
        rows = slice(64 * nd, 64 * nd + 64)
        for n in range(4):
            source = block_of(n)
            own_hi, own_lo = split(jnp.where(shift == (nd - source).astype(F32), here, 0.0))
            step = (dest - source).astype(F32)
            pair_hi, pair_lo = split(jnp.where(shift == step + far, there, 0.0))
            halo_hi, halo_lo = split(jnp.where(shift == step - far, there * inside, 0.0))
            below = slice(256 + 64 * nd, 320 + 64 * nd)
            for k, (u, v, w) in enumerate(
                ((own_hi, pair_hi, halo_hi), (own_hi, pair_hi, halo_hi), (own_lo, pair_lo, halo_lo))
            ):
                at = 512 * k + 128 * n
                ww[rows, at : at + 128] = u
                ww[below, at : at + 128] = v
                wh[n, rows, 128 * k : 128 * k + 128] = w
    for i in (1, 2, 3, 5, 6, 7):
        snd_copy(i).wait_recv()
    e_copy.wait()
    a_copy(1).start()
    b_copy(1).start()
    for which in range(2):
        via_copy(1, 1, which).start()

    def spectrum(a, b, i, at, depth):
        re = jnp.concatenate([a[i, 0], b[i, 0]], axis=0)
        im = jnp.concatenate([a[i, 1], b[i, 1]], axis=0)
        for half_p, parts in enumerate(butterflies(re, im, tw)):
            for j, pieces in enumerate(parts):
                for half, w in enumerate(pieces):
                    hi, lo = split(w)
                    for k, x in enumerate((hi, lo, hi)):
                        at_k = 512 * k + 256 * half
                        spread[half_p, 64 * j : 64 * j + 64, at_k : at_k + 256] = x
        even, uneven = (dot(spread[k], table[k]) for k in range(2))
        early = lax.broadcasted_iota(jnp.int32, (64, 128), 1) < 64
        for j in range(4):
            for b4 in range(4):
                first, second = (even, uneven) if b4 % 2 == 0 else (uneven, even)
                rows = slice(64 * j, 64 * j + 64)
                c0 = 128 * (b4 // 2)
                u = jnp.where(early, first[rows, c0 : c0 + 128], second[rows, c0 : c0 + 128])
                v = jnp.where(early, first[rows, 256 + c0 : 384 + c0], second[rows, 256 + c0 : 384 + c0])
                e0 = 512 * b4 + 128 * j
                c, w = (
                    jnp.concatenate([e_own[part, :, e0 : e0 + 128], e_other[part, :, e0 : e0 + 128]], axis=0)
                    for part in range(2)
                )
                for half, value in enumerate((u * c - v * w, u * w + v * c)):
                    hi, lo = split(value)
                    for k, x in enumerate((hi, lo, hi)):
                        spec[b4, pl.ds(k * depth + at + 64 * half, 64), 128 * j : 128 * j + 128] = x

    def block_at(dg, dh):
        return 2 * lax.rem(g + dg, 2) + lax.rem(h + dh, 2)

    def near_copy(ii):
        return remote(near.at[1, ii], near_in.at[ii], near_s.at[ii], near_r.at[ii], core)

    def dest_rows(n):
        return pl.ds(pl.multiple_of(64 * (3 - block_of(n)), 64), 64)

    def row_copy(dg, i):
        at, ii = dest_rows(lax.rem(i, 4)), i // 4
        return remote(side.at[dg, ii, at], side_in.at[dg, ii, at], row_s.at[dg, i], row_r.at[dg, i], peer(dg, 0, 1))

    def opp_cross(i):
        return remote(opp.at[i], relay_in.at[i], rel_s.at[i], rel_r.at[i], peer(0, 1, 1))

    def opp_direct(i):
        return remote(opp.at[i], relay_in.at[i], rel_s.at[i], rel_r.at[i], peer(0, 0, 1))

    def cross_copy(dg, i):
        return remote(cross.at[dg, i], cross_in.at[dg, i], crs_s.at[dg, i], crs_r.at[dg, i], peer(dg, 1, 1))

    def own_rows(ii):
        def one(n, carry):
            @pl.when(jnp.logical_and(ii == 0, n == 3))
            def _():
                pass_on(2, 0)
                a_copy(2).start()
                b_copy(2).start()

            spectrum(keep, other, 4 * ii + n, pl.multiple_of(128 * n, 128), 512)
            return carry

        lax.fori_loop(0, 4, one, 0)
        for dh in (1, 0):
            for dg in range(2):
                total = dot(ww[...], spec[block_at(dg, dh)])
                if dh == 0:
                    near[dg, ii] = total[0:256]
                else:
                    side[dg, ii] = total[0:256]
                    for n in (1, 3):
                        row_copy(dg, 4 * ii + n).start()
                pp[2 * dg + dh, ii] = total[256:512]
        near_copy(ii).start()

    def collect(i):
        n, ii = lax.rem(i, 4), i // 4
        at = dest_rows(n)
        for dg in range(2):
            cross_copy(dg, i).wait()
        parts = [
            near[0, ii, at, :] + side_in[0, ii, at, :] + cross_in[0, i],
            near_in[ii, at, :] + side_in[1, ii, at, :] + cross_in[1, i],
        ]
        got = dot(jnp.concatenate(split(jnp.concatenate(parts, axis=0)), axis=0), perm[h])
        rows = got[0:128] + got[128:256]
        for dg in range(2):
            row = 4 * (3 - block_of(n)) + 2 * lax.rem(g + dg, 2) + ii
            for c in range(4):
                for part in range(2):
                    at = 64 * dg + 32 * part
                    flat[c, part, pl.ds(row, 32, stride=16), :] = rows[at : at + 32, 128 * c : 128 * c + 128]

    def relay(i):
        n, ii = lax.rem(i, 4), i // 4

        @pl.when(lax.rem(i, 2) == 0)
        def _():
            opp_cross(i).wait()
            at = dest_rows(n)
            for dg in range(2):
                side[dg, ii, at, :] = side[dg, ii, at, :] + relay_in[i, dg]
                row_copy(dg, i).start()

        @pl.when(lax.rem(i, 2) == 1)
        def _():
            opp_direct(i).wait()
            for dg in range(2):
                cross[dg, i] = cross[dg, i] + relay_in[i, dg]
                cross_copy(dg, i).start()

    def step(i, carry):
        n, ii = lax.rem(i, 4), i // 4

        for now, start in ((2, 3), (3, 5), (4, 7)):

            @pl.when(i == now)
            def _():
                a_copy(start).start()
                b_copy(start).start()

        @pl.when(i == 2)
        def _():
            pass_on(2, 1)
            pass_on(3, 0)

        @pl.when(i == 5)
        def _():
            pass_on(3, 1)

        @pl.when(jnp.logical_or(i == 0, i == 3))
        def _():
            own_rows(i // 3)

        a_copy(i).wait_recv()
        b_copy(i).wait_recv()

        spectrum(halo_a, halo_b, i, 0, 128)
        mine = pl.ds(pl.multiple_of(64 * n, 64), 64)
        for dh in range(2):
            for dg in range(2):
                total = dot(wh[n], spec[block_at(dg, dh), 0:384, :])
                pp[2 * dg + dh, ii] = pp[2 * dg + dh, ii] + total
                if dh == 0:
                    opp[i, dg] = pp[2 * dg, ii, mine, :]
                else:
                    cross[dg, i] = pp[2 * dg + 1, ii, mine, :]
            if dh == 0:

                @pl.when(lax.rem(i, 2) == 0)
                def _():
                    opp_cross(i).start()

                @pl.when(lax.rem(i, 2) == 1)
                def _():
                    opp_direct(i).start()

        @pl.when(lax.rem(i, 2) == 0)
        def _():
            for dg in range(2):
                cross_copy(dg, i).start()

        @pl.when(i >= 1)
        def _():
            relay(i - 1)

        @pl.when(i >= 4)
        def _():
            @pl.when(i == 4)
            def _():
                near_copy(0).wait()

            for dg in range(2):
                row_copy(dg, i - 4).wait()
            collect(i - 4)

        return carry

    lax.fori_loop(0, 8, step, 0)
    near_copy(1).wait()

    def last(i, carry):
        for dg in range(2):
            row_copy(dg, i).wait()
        collect(i)
        return carry

    lax.fori_loop(4, 6, last, 0)
    relay(7)
    lax.fori_loop(6, 8, last, 0)
    results = [
        pltpu.make_async_copy(flat.at[c], out.at[:, :, pl.ds(128 * c, 128)], load_sem.at[c]) for c in range(4)
    ]
    for c in results:
        c.start()
    for i in range(8):
        snd_copy(i).wait_send()
        if i not in (4, 6):
            a_copy(i).wait_send()
            b_copy(i).wait_send()
    for hops in range(1, 4):
        for k in range(2):
            for which in range(2):
                via_copy(hops, k, which).wait_send()
    for c in results:
        c.wait()


def local(strips, field, spectral_phase, chirp_shift, tile_map, tile_phase):
    waves, tw = dft_tables()
    vmem = pl.BlockSpec(memory_space=pltpu.VMEM)
    hbm = pl.BlockSpec(memory_space=pl.ANY)
    rows = pltpu.VMEM((8, 2, 32, 1024), F32)
    small = pltpu.VMEM((16, 128), F32)
    phase = pltpu.VMEM((2, 32, NY), F32)
    sums = pltpu.VMEM((2, 2, 256, 512), F32)
    dma = pltpu.SemaphoreType.DMA
    out = pl.pallas_call(
        functools.partial(kernel, strips),
        in_specs=[hbm, hbm, hbm, hbm, vmem, vmem, pl.BlockSpec(memory_space=pltpu.SMEM)],
        out_specs=pl.BlockSpec(memory_space=pl.ANY),
        out_shape=jax.ShapeDtypeStruct((2, 512, 512), F32),
        scratch_shapes=[
            pltpu.VMEM((8, 2, 512, 128), F32),
            rows, rows, rows, rows, rows,
            small, small, small, small,
            pltpu.VMEM((32, NY), F32),
            pltpu.VMEM(waves.shape, F32),
            pltpu.VMEM(tw.shape, F32),
            phase, phase,
            pltpu.VMEM((2, 1536, 512), BF),
            pltpu.VMEM((2, 512, 512), BF),
            pltpu.VMEM((512, 1536), BF),
            pltpu.VMEM((4, 256, 384), BF),
            pltpu.VMEM((2, 256, 1536), BF),
            pltpu.VMEM((4, 1536, 512), BF),
            sums,
            pltpu.VMEM((2, 256, 512), F32),
            sums, sums,
            pltpu.VMEM((4, 2, 256, 512), F32),
            pltpu.VMEM((8, 2, 64, 512), F32),
            pltpu.VMEM((8, 2, 64, 512), F32),
            pltpu.VMEM((2, 8, 64, 512), F32),
            pltpu.VMEM((2, 8, 64, 512), F32),
            pltpu.VMEM((2, 2, 2, 32, 1024), F32),
            pltpu.VMEM((2, 2, 2, 32, 1024), F32),
            dma((11,)),
            *[dma((8,))] * 6,
            dma((3,)), dma((3,)),
            dma((2,)), dma((2,)),
            dma((2, 8)), dma((2, 8)),
            dma((8,)), dma((8,)),
            dma((2, 8)), dma((2, 8)),
            *[dma((2, 2))] * 4,
        ],
        compiler_params=pltpu.CompilerParams(
            collective_id=0, has_side_effects=True, vmem_limit_bytes=VMEM * 2**20
        ),
        cost_estimate=pl.CostEstimate(flops=40 * 10**9, bytes_accessed=10 * 2**20, transcendentals=0),
    )(
        field.reshape(2, 512, 1024), spectral_phase, jnp.asarray(waves), jnp.asarray(tw),
        chirp_shift.reshape(1, 32), tile_phase, tile_map,
    )
    return out.reshape(2, NT, 16, 512)


def solution(mesh):
    placed = (P(None, "freq", "xs", "yh"), P("freq", None), P("freq"), P("xs"), P(None, "freq"))
    return jax.shard_map(
        functools.partial(local, mesh.shape["xs"]),
        mesh=mesh,
        in_specs=placed,
        out_specs=P(None, None, "xs", ("freq", "yh")),
        check_vma=False,
    )
```

```python
import functools
import math

import jax
import jax.numpy as jnp
import numpy as np
from jax import lax
from jax.experimental import pallas as pl
from jax.experimental.pallas import tpu as pltpu
from jax.sharding import PartitionSpec as P

NF = 64
NY = 2048
NT = 32
VMEM = 60
BF = jnp.bfloat16
F32 = jnp.float32
AXES = ("freq", "xs", "yh")
MESH = pl.DeviceIdType.MESH


def dft_tables():
    m = np.arange(256)
    angle = 2.0 * np.pi * (np.outer(m, m) % 256) / 256
    waves = np.stack([np.cos(angle), np.sin(angle)]) / math.sqrt(NY)
    odd_order = np.concatenate([np.arange(64) + 64 * b for b in (1, 0, 3, 2)])
    turn = 2.0 * np.pi * np.outer(np.arange(8), m) / NY
    twiddle = np.stack([np.cos(turn), np.sin(turn)])
    return np.stack([waves, waves[:, :, odd_order]]).astype(np.float32), twiddle.astype(np.float32)


def split(value):
    high = value.astype(BF)
    return high, (value - high.astype(F32)).astype(BF)


def dot(a, b):
    return jnp.dot(a, b, preferred_element_type=F32)


def dot_t(a, b):
    return lax.dot_general(a, b, (((1,), (1,)), ((), ())), preferred_element_type=F32)


class Copies:
    def __init__(self, copies):
        self.copies = copies

    def start(self):
        for c in self.copies:
            c.start()

    def wait_send(self):
        for c in self.copies:
            c.wait_send()

    def wait_recv(self):
        for c in self.copies:
            c.wait_recv()

    def wait(self):
        self.wait_send()
        self.wait_recv()


def sincos(x):
    k = jnp.floor(x * (2.0 / math.pi) + 0.5)
    r = ((x - k * 1.5703125) - k * 4.837512969970703125e-4) - k * 7.54978995489188216e-8
    z = r * r
    sine = r + r * z * (-1.6666654611e-1 + z * (8.3321608736e-3 - z * 1.9515295891e-4))
    cosine = (1.0 - 0.5 * z) + z * z * (4.166664568298827e-2 + z * (-1.388731625493765e-3 + z * 2.443315711809948e-5))
    half = jnp.floor(k * 0.5)
    swap = (k - 2.0 * half) > 0.5
    sign = 1.0 - 2.0 * (half - 2.0 * jnp.floor(half * 0.5))
    return sign * jnp.where(swap, cosine, sine), sign * jnp.where(swap, -sine, cosine)


def butterflies(re, im, tw):
    a = [(re[:, 256 * c : 256 * c + 256], im[:, 256 * c : 256 * c + 256]) for c in range(4)]
    r = math.sqrt(0.5)

    def add(u, v):
        return u[0] + v[0], u[1] + v[1]

    def sub(u, v):
        return u[0] - v[0], u[1] - v[1]

    def mi(u):
        return u[1], -u[0]

    def four(b):
        e0, e1 = add(b[0], b[2]), sub(b[0], b[2])
        e2, e3 = add(b[1], b[3]), mi(sub(b[1], b[3]))
        return add(e0, e2), add(e1, e3), sub(e0, e2), sub(e1, e3)

    even = four(a)
    b1 = ((a[1][0] + a[1][1]) * r, (a[1][1] - a[1][0]) * r)
    b3 = ((a[3][1] - a[3][0]) * r, (-a[3][0] - a[3][1]) * r)
    odd = four((a[0], b1, mi(a[2]), b3))
    both = []
    for side, parts in enumerate((even, odd)):
        row = []
        for j in range(4):
            p = 2 * j + side
            u = parts[j]
            if p:
                c, s = tw[0, p : p + 1, :], tw[1, p : p + 1, :]
                u = u[0] * c + u[1] * s, u[1] * c - u[0] * s
            row.append(u)
        both.append(row)
    return both


def kernel(
    strips, field, phi_hbm, waves_hbm, tw_hbm, shift_row, tile_phase, tile_ids, out,
    flat, snd, keep, other, halo_a, halo_b, prm, prm_out, prm_in, prm_pair,
    phi, waves, tw, e_own, e_other, table, perm, ww, wh,
    spread, spec, near, near_in, side, side_in, pp, opp, relay_in, cross, cross_in, via_1, via_2, *rest,
):
    (load_sem, snd_s, snd_r, ha_s, ha_r, hb_s, hb_r, prm_s, prm_r,
     near_s, near_r, row_s, row_r, rel_s, rel_r, crs_s, crs_r, v1_s, v1_r, v2_s, v2_r) = rest
    g, s, h = (lax.axis_index(a) for a in AXES)
    odd = lax.rem(s, 2)
    pair = s + 1 - 2 * odd
    onward = lax.rem(s + strips + 4 * odd - 2, strips)
    back = lax.rem(s + strips + 2 - 4 * odd, strips)
    core = (1 - g, s, h)

    z, y, turns = s // 8, lax.rem(s // 2, 4), strips // 8
    hop = 1 - 2 * odd
    across = 8 * z + 2 * lax.rem(y + 4 + hop, 4) + odd
    across_from = 8 * z + 2 * lax.rem(y + 4 - hop, 4) + odd
    z_on = 8 * lax.rem(z + turns - hop, turns) + odd
    z_back = 8 * lax.rem(z + turns + hop, turns) + odd
    leaves = (y == 2 - odd).astype(jnp.int32)
    third = across + leaves * (z_on + 2 * (3 - 3 * odd) - across)
    enters = (y == 3 - 3 * odd).astype(jnp.int32)
    third_from = across_from + enters * (z_back + 2 * (2 - odd) - across_from)

    def peer(dg, ds, dh):
        return (lax.rem(g + dg, 2), pair if ds else s, lax.rem(h + dh, 2))

    def remote(src, dst, a, b, to):
        return pltpu.make_async_remote_copy(
            src_ref=src, dst_ref=dst, send_sem=a, recv_sem=b, device_id=to, device_id_type=MESH
        )

    def block_of(n):
        return n + odd * (3 - 2 * n)

    loads = [
        pltpu.make_async_copy(field.at[:, :, pl.ds(128 * y, 128)], flat.at[y], load_sem.at[y]) for y in range(8)
    ]
    tables = [
        pltpu.make_async_copy(src, dst, load_sem.at[8 + k])
        for k, (src, dst) in enumerate(((waves_hbm, waves), (tw_hbm, tw), (phi_hbm, phi)))
    ]
    for c in loads + tables:
        c.start()
    barrier = pltpu.get_barrier_semaphore()
    greet = [core, peer(0, 0, 1), peer(1, 0, 1), peer(0, 1, 1), peer(1, 1, 1), (g, onward, h), (g, back, h)]
    greet += [(g, across, h), (g, across_from, h), (g, third, h), (g, third_from, h)]
    for to in greet:
        pl.semaphore_signal(barrier, inc=1, device_id=to, device_id_type=MESH)

    def snd_copy(i):
        return remote(snd.at[i], other.at[i], snd_s.at[i], snd_r.at[i], core)

    def halves(src, dst, a, b, to):
        return Copies([remote(src.at[c], dst.at[c], a.at[c], b.at[c], to) for c in range(2)])

    def a_copy(i):
        return halves(keep.at[i], halo_a.at[i], ha_s.at[i], ha_r.at[i], (g, onward, h))

    def b_copy(i):
        return halves(other.at[i], halo_b.at[i], hb_s.at[i], hb_r.at[i], (g, onward, h))

    def via_copy(hops, k, which):
        i = 4 + 2 * k
        if hops == 1:
            src = (keep, other)[which].at[i]
            return halves(src, via_1.at[k, which], v1_s.at[k, which], v1_r.at[k, which], (g, across, h))
        if hops == 2:
            return halves(
                via_1.at[k, which], via_2.at[k, which], v2_s.at[k, which], v2_r.at[k, which], (g, across, h)
            )
        dst, sems = ((halo_a, (ha_s, ha_r)), (halo_b, (hb_s, hb_r)))[which]
        return halves(via_2.at[k, which], dst.at[i], sems[0].at[i], sems[1].at[i], (g, third, h))

    def pass_on(hops, k):
        for which in range(2):
            via_copy(hops - 1, k, which).wait_recv()
            via_copy(hops, k, which).start()

    def gather_rows(i, whose, into):
        row = 4 * block_of(lax.rem(i, 4)) + 2 * whose + i // 4
        for c in range(2):
            for y in range(8):
                into[i, c, :, 128 * y : 128 * y + 128] = flat[y, c, pl.ds(row, 32, stride=16), :]

    gap = jnp.zeros((8, 32), F32)
    rows = jnp.concatenate([shift_row[...].astype(F32), tile_phase[...], jnp.zeros((3, 32), F32)], axis=0)
    prm[0:8, :] = jnp.concatenate([rows, gap, rows, gap], axis=1)
    for rb in range(4):
        prm[8 + rb : 9 + rb, :] = jnp.full((1, 128), tile_ids[rb], jnp.int32).astype(F32)
    prm[12:16, :] = jnp.zeros((4, 128), F32)
    prm_out[...] = pltpu.roll(prm[...], 32, 1)
    prm_core = remote(prm_out, prm_in, prm_s.at[0], prm_r.at[0], core)
    prm_strip = remote(prm, prm_pair, prm_s.at[1], prm_r.at[1], peer(0, 1, 1))

    for c in loads:
        c.wait()

    def pack_send(i, carry):
        gather_rows(i, 1 - g, snd)
        snd_copy(i).start()
        return carry

    def pack_keep(i, carry):
        gather_rows(i, g, keep)
        return carry

    for i in (0, 4, 1):
        gather_rows(i, g, keep)
    pl.semaphore_wait(barrier, len(greet))
    a_copy(0).start()
    via_copy(1, 0, 0).start()
    a_copy(1).start()
    lax.fori_loop(0, 8, pack_send, 0)
    prm_core.start()
    prm_strip.start()
    lax.fori_loop(2, 4, pack_keep, 0)
    lax.fori_loop(5, 8, pack_keep, 0)
    snd_copy(0).wait_recv()
    b_copy(0).start()
    snd_copy(4).wait_recv()
    via_copy(1, 0, 1).start()
    snd_copy(1).wait_recv()
    b_copy(1).start()

    for c in tables:
        c.wait()
    lane = lax.broadcasted_iota(jnp.int32, (512, 1), 0)
    wave = lax.broadcasted_iota(jnp.int32, (1, 512), 1)
    turn = lax.rem(lane, 128)
    for half in range(2):
        late = (turn >= 64).astype(jnp.int32)
        late = late if half == 0 else 1 - late
        target = 8 * lax.rem(turn, 64) + 2 * (lane // 128) + late
        perm[half] = jnp.where(target == wave, 1.0, 0.0).astype(BF)
        c_hi, c_lo = split(waves[half, 0])
        s_hi, s_lo = split(waves[half, 1])
        for k, (c, w) in enumerate(((c_hi, s_hi), (c_hi, s_hi), (c_lo, s_lo))):
            table[half, 512 * k : 512 * k + 256, 0:256] = c
            table[half, 512 * k : 512 * k + 256, 256:512] = -w
            table[half, 512 * k + 256 : 512 * k + 512, 0:256] = w
            table[half, 512 * k + 256 : 512 * k + 512, 256:512] = c

    lanes = lax.rem(lax.broadcasted_iota(jnp.int32, (1, 512), 1), 128)
    for half in range(2):
        late = lanes >= 64 if half == 0 else lanes < 64
        sign = 1.0 - 2.0 * jnp.where(late, h, 0).astype(F32)
        stack = []
        for b in (half, half + 2):
            sine, cosine = sincos(phi[:, 512 * b : 512 * b + 512])
            stack += [*split(cosine), *split(sine)]
        got = dot_t(jnp.concatenate(stack, axis=0), perm[half])
        for k, b in enumerate((half, half + 2)):
            for part in range(2):
                at = 128 * k + 64 * part
                e_own[part, :, 512 * b : 512 * b + 512] = (got[at : at + 32] + got[at + 32 : at + 64]) * sign
    e_copy = remote(e_own, e_other, prm_s.at[2], prm_r.at[2], core)
    e_copy.start()

    prm_core.wait()
    prm_strip.wait()
    both = prm[...] + prm_in[...]
    shift = both[0:1, :]
    col = lax.broadcasted_iota(jnp.int32, (NT, 128), 1)
    freq = lax.rem(lax.rem(col, 64) + 32 * g, NF)
    angle = (2.0 * math.pi / NF) * lax.rem(lax.broadcasted_iota(jnp.int32, (NT, 128), 0) * freq, NF).astype(F32)
    scale = 1.0 / math.sqrt(NF)
    real_in = col < 64

    def base(tile):
        phase = jnp.zeros((1, 128), F32)
        for t in range(4):
            phase = phase + jnp.where(tile == float(t), both[1 + t : 2 + t, :], 0.0)
        im, re = sincos(angle + phase)
        im, re = im * scale, re * scale
        return jnp.concatenate([jnp.where(real_in, re, -im), jnp.where(real_in, im, re)], axis=0)

    far = (4 * (1 - 2 * odd)).astype(F32)
    inside = jnp.where(odd == 1, (s > 1).astype(F32), (s < strips - 2).astype(F32))
    for nd in range(4):
        dest = block_of(nd)
        here, there = base(prm[8 + nd : 9 + nd, :]), base(prm_pair[pl.ds(8 + dest, 1), :])
        rows = slice(64 * nd, 64 * nd + 64)
        for n in range(4):
            source = block_of(n)
            own_hi, own_lo = split(jnp.where(shift == (nd - source).astype(F32), here, 0.0))
            step = (dest - source).astype(F32)
            pair_hi, pair_lo = split(jnp.where(shift == step + far, there, 0.0))
            halo_hi, halo_lo = split(jnp.where(shift == step - far, there * inside, 0.0))
            below = slice(256 + 64 * nd, 320 + 64 * nd)
            for k, (u, v, w) in enumerate(
                ((own_hi, pair_hi, halo_hi), (own_hi, pair_hi, halo_hi), (own_lo, pair_lo, halo_lo))
            ):
                at = 512 * k + 128 * n
                ww[rows, at : at + 128] = u
                ww[below, at : at + 128] = v
                wh[n, rows, 128 * k : 128 * k + 128] = w
    for i in (2, 3, 5, 6, 7):
        snd_copy(i).wait_recv()
    e_copy.wait()
    a_copy(2).start()
    b_copy(2).start()
    for which in range(2):
        via_copy(1, 1, which).start()

    def spectrum(a, b, i, at, depth):
        re = jnp.concatenate([a[i, 0], b[i, 0]], axis=0)
        im = jnp.concatenate([a[i, 1], b[i, 1]], axis=0)
        for half_p, parts in enumerate(butterflies(re, im, tw)):
            for j, pieces in enumerate(parts):
                for half, w in enumerate(pieces):
                    hi, lo = split(w)
                    for k, x in enumerate((hi, lo, hi)):
                        at_k = 512 * k + 256 * half
                        spread[half_p, 64 * j : 64 * j + 64, at_k : at_k + 256] = x
        even, uneven = (dot(spread[k], table[k]) for k in range(2))
        early = lax.broadcasted_iota(jnp.int32, (64, 128), 1) < 64
        for j in range(4):
            for b4 in range(4):
                first, second = (even, uneven) if b4 % 2 == 0 else (uneven, even)
                rows = slice(64 * j, 64 * j + 64)
                c0 = 128 * (b4 // 2)
                u = jnp.where(early, first[rows, c0 : c0 + 128], second[rows, c0 : c0 + 128])
                v = jnp.where(early, first[rows, 256 + c0 : 384 + c0], second[rows, 256 + c0 : 384 + c0])
                e0 = 512 * b4 + 128 * j
                c, w = (
                    jnp.concatenate([e_own[part, :, e0 : e0 + 128], e_other[part, :, e0 : e0 + 128]], axis=0)
                    for part in range(2)
                )
                for half, value in enumerate((u * c - v * w, u * w + v * c)):
                    hi, lo = split(value)
                    for k, x in enumerate((hi, lo, hi)):
                        spec[b4, pl.ds(k * depth + at + 64 * half, 64), 128 * j : 128 * j + 128] = x

    def block_at(dg, dh):
        return 2 * lax.rem(g + dg, 2) + lax.rem(h + dh, 2)

    def near_copy(ii):
        return remote(near.at[1, ii], near_in.at[ii], near_s.at[ii], near_r.at[ii], core)

    def dest_rows(n):
        return pl.ds(pl.multiple_of(64 * (3 - block_of(n)), 64), 64)

    def row_copy(dg, i):
        at, ii = dest_rows(lax.rem(i, 4)), i // 4
        return remote(side.at[dg, ii, at], side_in.at[dg, ii, at], row_s.at[dg, i], row_r.at[dg, i], peer(dg, 0, 1))

    def opp_cross(i):
        return halves(opp.at[i], relay_in.at[i], rel_s.at[i], rel_r.at[i], peer(0, 1, 1))

    def opp_direct(i):
        return halves(opp.at[i], relay_in.at[i], rel_s.at[i], rel_r.at[i], peer(0, 0, 1))

    def cross_copy(dg, i):
        return remote(cross.at[dg, i], cross_in.at[dg, i], crs_s.at[dg, i], crs_r.at[dg, i], peer(dg, 1, 1))

    def own_rows(ii):
        def one(n, carry):
            @pl.when(jnp.logical_and(ii == 0, n == 1))
            def _():
                a_copy(3).start()
                b_copy(3).start()

            @pl.when(jnp.logical_and(ii == 0, n == 3))
            def _():
                pass_on(2, 0)
                a_copy(5).start()
                b_copy(5).start()

            spectrum(keep, other, 4 * ii + n, pl.multiple_of(128 * n, 128), 512)
            return carry

        lax.fori_loop(0, 4, one, 0)
        for dh in (1, 0):
            for dg in range(2):
                total = dot(ww[...], spec[block_at(dg, dh)])
                if dh == 0:
                    near[dg, ii] = total[0:256]
                else:
                    side[dg, ii] = total[0:256]
                    for n in (1, 3):
                        row_copy(dg, 4 * ii + n).start()
                pp[2 * dg + dh, ii] = total[256:512]
        near_copy(ii).start()

    def collect(i):
        n, ii = lax.rem(i, 4), i // 4
        at = dest_rows(n)
        for dg in range(2):
            cross_copy(dg, i).wait()
        parts = [
            near[0, ii, at, :] + side_in[0, ii, at, :] + cross_in[0, i],
            near_in[ii, at, :] + side_in[1, ii, at, :] + cross_in[1, i],
        ]
        got = dot(jnp.concatenate(split(jnp.concatenate(parts, axis=0)), axis=0), perm[h])
        rows = got[0:128] + got[128:256]
        for dg in range(2):
            row = 4 * (3 - block_of(n)) + 2 * lax.rem(g + dg, 2) + ii
            for c in range(4):
                for part in range(2):
                    at = 64 * dg + 32 * part
                    flat[c, part, pl.ds(row, 32, stride=16), :] = rows[at : at + 32, 128 * c : 128 * c + 128]

    def relay(i):
        n, ii = lax.rem(i, 4), i // 4

        @pl.when(lax.rem(i, 2) == 0)
        def _():
            opp_cross(i).wait()
            at = dest_rows(n)
            for dg in range(2):
                side[dg, ii, at, :] = side[dg, ii, at, :] + relay_in[i, dg]
                row_copy(dg, i).start()

        @pl.when(lax.rem(i, 2) == 1)
        def _():
            opp_direct(i).wait()
            for dg in range(2):
                cross[dg, i] = cross[dg, i] + relay_in[i, dg]
                cross_copy(dg, i).start()

    def step(i, carry):
        n, ii = lax.rem(i, 4), i // 4

        @pl.when(i == 1)
        def _():
            a_copy(7).start()
            b_copy(7).start()

        @pl.when(i == 2)
        def _():
            pass_on(3, 0)
            pass_on(2, 1)

        @pl.when(i == 4)
        def _():
            pass_on(3, 1)

        @pl.when(jnp.logical_or(i == 0, i == 3))
        def _():
            own_rows(i // 3)

        a_copy(i).wait_recv()
        b_copy(i).wait_recv()

        spectrum(halo_a, halo_b, i, 0, 128)
        mine = pl.ds(pl.multiple_of(64 * n, 64), 64)
        for dh in range(2):
            for dg in range(2):
                total = dot(wh[n], spec[block_at(dg, dh), 0:384, :])
                pp[2 * dg + dh, ii] = pp[2 * dg + dh, ii] + total
                if dh == 0:
                    opp[i, dg] = pp[2 * dg, ii, mine, :]
                else:
                    cross[dg, i] = pp[2 * dg + 1, ii, mine, :]
            if dh == 0:

                @pl.when(lax.rem(i, 2) == 0)
                def _():
                    opp_cross(i).start()

                @pl.when(lax.rem(i, 2) == 1)
                def _():
                    opp_direct(i).start()

        @pl.when(lax.rem(i, 2) == 0)
        def _():
            for dg in range(2):
                cross_copy(dg, i).start()

        @pl.when(i >= 1)
        def _():
            relay(i - 1)

        @pl.when(i >= 4)
        def _():
            @pl.when(i == 4)
            def _():
                near_copy(0).wait()

            for dg in range(2):
                row_copy(dg, i - 4).wait()
            collect(i - 4)

        return carry

    lax.fori_loop(0, 8, step, 0)
    near_copy(1).wait()

    def last(i, carry):
        for dg in range(2):
            row_copy(dg, i).wait()
        collect(i)
        return carry

    lax.fori_loop(4, 6, last, 0)
    relay(7)
    lax.fori_loop(6, 8, last, 0)
    results = [
        pltpu.make_async_copy(flat.at[c], out.at[:, :, pl.ds(128 * c, 128)], load_sem.at[c]) for c in range(4)
    ]
    for c in results:
        c.start()
    for i in range(8):
        snd_copy(i).wait_send()
        if i not in (4, 6):
            a_copy(i).wait_send()
            b_copy(i).wait_send()
    for hops in range(1, 4):
        for k in range(2):
            for which in range(2):
                via_copy(hops, k, which).wait_send()
    for c in results:
        c.wait()


def local(strips, field, spectral_phase, chirp_shift, tile_map, tile_phase):
    waves, tw = dft_tables()
    vmem = pl.BlockSpec(memory_space=pltpu.VMEM)
    hbm = pl.BlockSpec(memory_space=pl.ANY)
    rows = pltpu.VMEM((8, 2, 32, 1024), F32)
    small = pltpu.VMEM((16, 128), F32)
    phase = pltpu.VMEM((2, 32, NY), F32)
    sums = pltpu.VMEM((2, 2, 256, 512), F32)
    dma = pltpu.SemaphoreType.DMA
    out = pl.pallas_call(
        functools.partial(kernel, strips),
        in_specs=[hbm, hbm, hbm, hbm, vmem, vmem, pl.BlockSpec(memory_space=pltpu.SMEM)],
        out_specs=pl.BlockSpec(memory_space=pl.ANY),
        out_shape=jax.ShapeDtypeStruct((2, 512, 512), F32),
        scratch_shapes=[
            pltpu.VMEM((8, 2, 512, 128), F32),
            rows, rows, rows, rows, rows,
            small, small, small, small,
            pltpu.VMEM((32, NY), F32),
            pltpu.VMEM(waves.shape, F32),
            pltpu.VMEM(tw.shape, F32),
            phase, phase,
            pltpu.VMEM((2, 1536, 512), BF),
            pltpu.VMEM((2, 512, 512), BF),
            pltpu.VMEM((512, 1536), BF),
            pltpu.VMEM((4, 256, 384), BF),
            pltpu.VMEM((2, 256, 1536), BF),
            pltpu.VMEM((4, 1536, 512), BF),
            sums,
            pltpu.VMEM((2, 256, 512), F32),
            sums, sums,
            pltpu.VMEM((4, 2, 256, 512), F32),
            pltpu.VMEM((8, 2, 64, 512), F32),
            pltpu.VMEM((8, 2, 64, 512), F32),
            pltpu.VMEM((2, 8, 64, 512), F32),
            pltpu.VMEM((2, 8, 64, 512), F32),
            pltpu.VMEM((2, 2, 2, 32, 1024), F32),
            pltpu.VMEM((2, 2, 2, 32, 1024), F32),
            dma((11,)),
            dma((8,)), dma((8,)),
            *[dma((8, 2))] * 4,
            dma((3,)), dma((3,)),
            dma((2,)), dma((2,)),
            dma((2, 8)), dma((2, 8)),
            dma((8, 2)), dma((8, 2)),
            dma((2, 8)), dma((2, 8)),
            *[dma((2, 2, 2))] * 4,
        ],
        compiler_params=pltpu.CompilerParams(
            collective_id=0, has_side_effects=True, vmem_limit_bytes=VMEM * 2**20
        ),
        cost_estimate=pl.CostEstimate(flops=40 * 10**9, bytes_accessed=10 * 2**20, transcendentals=0),
    )(
        field.reshape(2, 512, 1024), spectral_phase, jnp.asarray(waves), jnp.asarray(tw),
        chirp_shift.reshape(1, 32), tile_phase, tile_map,
    )
    return out.reshape(2, NT, 16, 512)


def solution(mesh):
    placed = (P(None, "freq", "xs", "yh"), P("freq", None), P("freq"), P("xs"), P(None, "freq"))
    return jax.shard_map(
        functools.partial(local, mesh.shape["xs"]),
        mesh=mesh,
        in_specs=placed,
        out_specs=P(None, None, "xs", ("freq", "yh")),
        check_vma=False,
    )
```

```python
import functools
import math

import jax
import jax.numpy as jnp
import numpy as np
from jax import lax
from jax.experimental import pallas as pl
from jax.experimental.pallas import tpu as pltpu
from jax.sharding import PartitionSpec as P

NF = 64
NY = 2048
NT = 32
VMEM = 60
BF = jnp.bfloat16
F32 = jnp.float32
AXES = ("freq", "xs", "yh")
MESH = pl.DeviceIdType.MESH


def dft_tables():
    m = np.arange(256)
    angle = 2.0 * np.pi * (np.outer(m, m) % 256) / 256
    waves = np.stack([np.cos(angle), np.sin(angle)]) / math.sqrt(NY)
    odd_order = np.concatenate([np.arange(64) + 64 * b for b in (1, 0, 3, 2)])
    turn = 2.0 * np.pi * np.outer(np.arange(8), m) / NY
    twiddle = np.stack([np.cos(turn), np.sin(turn)])
    return np.stack([waves, waves[:, :, odd_order]]).astype(np.float32), twiddle.astype(np.float32)


def split(value):
    high = value.astype(BF)
    return high, (value - high.astype(F32)).astype(BF)


def dot(a, b):
    return jnp.dot(a, b, preferred_element_type=F32)


def dot_t(a, b):
    return lax.dot_general(a, b, (((1,), (1,)), ((), ())), preferred_element_type=F32)


def sincos(x):
    k = jnp.floor(x * (2.0 / math.pi) + 0.5)
    r = ((x - k * 1.5703125) - k * 4.837512969970703125e-4) - k * 7.54978995489188216e-8
    z = r * r
    sine = r + r * z * (-1.6666654611e-1 + z * (8.3321608736e-3 - z * 1.9515295891e-4))
    cosine = (1.0 - 0.5 * z) + z * z * (4.166664568298827e-2 + z * (-1.388731625493765e-3 + z * 2.443315711809948e-5))
    half = jnp.floor(k * 0.5)
    swap = (k - 2.0 * half) > 0.5
    sign = 1.0 - 2.0 * (half - 2.0 * jnp.floor(half * 0.5))
    return sign * jnp.where(swap, cosine, sine), sign * jnp.where(swap, -sine, cosine)


def butterflies(re, im, tw):
    a = [(re[:, 256 * c : 256 * c + 256], im[:, 256 * c : 256 * c + 256]) for c in range(4)]
    r = math.sqrt(0.5)

    def add(u, v):
        return u[0] + v[0], u[1] + v[1]

    def sub(u, v):
        return u[0] - v[0], u[1] - v[1]

    def mi(u):
        return u[1], -u[0]

    def four(b):
        e0, e1 = add(b[0], b[2]), sub(b[0], b[2])
        e2, e3 = add(b[1], b[3]), mi(sub(b[1], b[3]))
        return add(e0, e2), add(e1, e3), sub(e0, e2), sub(e1, e3)

    even = four(a)
    b1 = ((a[1][0] + a[1][1]) * r, (a[1][1] - a[1][0]) * r)
    b3 = ((a[3][1] - a[3][0]) * r, (-a[3][0] - a[3][1]) * r)
    odd = four((a[0], b1, mi(a[2]), b3))
    both = []
    for side, parts in enumerate((even, odd)):
        row = []
        for j in range(4):
            p = 2 * j + side
            u = parts[j]
            if p:
                c, s = tw[0, p : p + 1, :], tw[1, p : p + 1, :]
                u = u[0] * c + u[1] * s, u[1] * c - u[0] * s
            row.append(u)
        both.append(row)
    return both


def kernel(
    strips, field, phi_hbm, waves_hbm, tw_hbm, shift_row, tile_phase, tile_ids, out,
    flat, snd, keep, other, halo_a, halo_b, prm, prm_out, prm_in, prm_pair,
    phi, waves, tw, e_own, e_other, table, perm, ww, wh,
    spread, spec, near, near_in, side, side_in, pp, opp, relay_in, cross, cross_in, via_1, via_2, *rest,
):
    (load_sem, snd_s, snd_r, ha_s, ha_r, hb_s, hb_r, prm_s, prm_r,
     near_s, near_r, row_s, row_r, rel_s, rel_r, crs_s, crs_r, v1_s, v1_r, v2_s, v2_r) = rest
    g, s, h = (lax.axis_index(a) for a in AXES)
    odd = lax.rem(s, 2)
    pair = s + 1 - 2 * odd
    onward = lax.rem(s + strips + 4 * odd - 2, strips)
    back = lax.rem(s + strips + 2 - 4 * odd, strips)
    core = (1 - g, s, h)

    z, y, turns = s // 8, lax.rem(s // 2, 4), strips // 8
    hop = 1 - 2 * odd
    across = 8 * z + 2 * lax.rem(y + 4 + hop, 4) + odd
    across_from = 8 * z + 2 * lax.rem(y + 4 - hop, 4) + odd
    z_on = 8 * lax.rem(z + turns - hop, turns) + odd
    z_back = 8 * lax.rem(z + turns + hop, turns) + odd
    leaves = (y == 2 - odd).astype(jnp.int32)
    third = across + leaves * (z_on + 2 * (3 - 3 * odd) - across)
    enters = (y == 3 - 3 * odd).astype(jnp.int32)
    third_from = across_from + enters * (z_back + 2 * (2 - odd) - across_from)

    def peer(dg, ds, dh):
        return (lax.rem(g + dg, 2), pair if ds else s, lax.rem(h + dh, 2))

    def remote(src, dst, a, b, to):
        return pltpu.make_async_remote_copy(
            src_ref=src, dst_ref=dst, send_sem=a, recv_sem=b, device_id=to, device_id_type=MESH
        )

    def block_of(n):
        return n + odd * (3 - 2 * n)

    loads = [
        pltpu.make_async_copy(field.at[:, :, pl.ds(128 * y, 128)], flat.at[y], load_sem.at[y]) for y in range(8)
    ]
    tables = [
        pltpu.make_async_copy(src, dst, load_sem.at[8 + k])
        for k, (src, dst) in enumerate(((waves_hbm, waves), (tw_hbm, tw), (phi_hbm, phi)))
    ]
    for c in loads + tables:
        c.start()
    barrier = pltpu.get_barrier_semaphore()
    greet = [core, peer(0, 0, 1), peer(1, 0, 1), peer(0, 1, 1), peer(1, 1, 1), (g, onward, h), (g, back, h)]
    greet += [(g, across, h), (g, across_from, h), (g, third, h), (g, third_from, h)]
    for to in greet:
        pl.semaphore_signal(barrier, inc=1, device_id=to, device_id_type=MESH)

    def snd_copy(i):
        return remote(snd.at[i], other.at[i], snd_s.at[i], snd_r.at[i], core)

    def a_copy(i):
        return remote(keep.at[i], halo_a.at[i], ha_s.at[i], ha_r.at[i], (g, onward, h))

    def b_copy(i):
        return remote(other.at[i], halo_b.at[i], hb_s.at[i], hb_r.at[i], (g, onward, h))

    def via_copy(hops, which):
        i = 4
        if hops == 1:
            src = (keep, other)[which].at[i]
            return remote(src, via_1.at[which], v1_s.at[which], v1_r.at[which], (g, across, h))
        if hops == 2:
            return remote(
                via_1.at[which], via_2.at[which], v2_s.at[which], v2_r.at[which], (g, across, h)
            )
        dst, sems = ((halo_a, (ha_s, ha_r)), (halo_b, (hb_s, hb_r)))[which]
        return remote(via_2.at[which], dst.at[i], sems[0].at[i], sems[1].at[i], (g, third, h))

    def pass_on(hops):
        for which in range(2):
            via_copy(hops - 1, which).wait_recv()
            via_copy(hops, which).start()

    def gather_rows(i, whose, into):
        row = 4 * block_of(lax.rem(i, 4)) + 2 * whose + i // 4
        for c in range(2):
            for y in range(8):
                into[i, c, :, 128 * y : 128 * y + 128] = flat[y, c, pl.ds(row, 32, stride=16), :]

    gap = jnp.zeros((8, 32), F32)
    rows = jnp.concatenate([shift_row[...].astype(F32), tile_phase[...], jnp.zeros((3, 32), F32)], axis=0)
    prm[0:8, :] = jnp.concatenate([rows, gap, rows, gap], axis=1)
    for rb in range(4):
        prm[8 + rb : 9 + rb, :] = jnp.full((1, 128), tile_ids[rb], jnp.int32).astype(F32)
    prm[12:16, :] = jnp.zeros((4, 128), F32)
    prm_out[...] = pltpu.roll(prm[...], 32, 1)
    prm_core = remote(prm_out, prm_in, prm_s.at[0], prm_r.at[0], core)
    prm_strip = remote(prm, prm_pair, prm_s.at[1], prm_r.at[1], peer(0, 1, 1))

    for c in loads:
        c.wait()

    def pack_send(i, carry):
        gather_rows(i, 1 - g, snd)
        snd_copy(i).start()
        return carry

    def pack_keep(i, carry):
        gather_rows(i, g, keep)
        return carry

    for i in (0, 4, 1):
        gather_rows(i, g, keep)
    pl.semaphore_wait(barrier, len(greet))
    a_copy(0).start()
    via_copy(1, 0).start()
    a_copy(1).start()
    lax.fori_loop(0, 8, pack_send, 0)
    prm_core.start()
    prm_strip.start()
    lax.fori_loop(2, 4, pack_keep, 0)
    lax.fori_loop(5, 8, pack_keep, 0)
    for i in (0, 4, 1):
        snd_copy(i).wait_recv()
        if i == 4:
            via_copy(1, 1).start()
        else:
            b_copy(i).start()

    for c in tables:
        c.wait()
    lane = lax.broadcasted_iota(jnp.int32, (512, 1), 0)
    wave = lax.broadcasted_iota(jnp.int32, (1, 512), 1)
    turn = lax.rem(lane, 128)
    for half in range(2):
        late = (turn >= 64).astype(jnp.int32)
        late = late if half == 0 else 1 - late
        target = 8 * lax.rem(turn, 64) + 2 * (lane // 128) + late
        perm[half] = jnp.where(target == wave, 1.0, 0.0).astype(BF)
        c_hi, c_lo = split(waves[half, 0])
        s_hi, s_lo = split(waves[half, 1])
        for k, (c, w) in enumerate(((c_hi, s_hi), (c_hi, s_hi), (c_lo, s_lo))):
            table[half, 512 * k : 512 * k + 256, 0:256] = c
            table[half, 512 * k : 512 * k + 256, 256:512] = -w
            table[half, 512 * k + 256 : 512 * k + 512, 0:256] = w
            table[half, 512 * k + 256 : 512 * k + 512, 256:512] = c

    lanes = lax.rem(lax.broadcasted_iota(jnp.int32, (1, 512), 1), 128)
    for half in range(2):
        late = lanes >= 64 if half == 0 else lanes < 64
        sign = 1.0 - 2.0 * jnp.where(late, h, 0).astype(F32)
        stack = []
        for b in (half, half + 2):
            sine, cosine = sincos(phi[:, 512 * b : 512 * b + 512])
            stack += [*split(cosine), *split(sine)]
        got = dot_t(jnp.concatenate(stack, axis=0), perm[half])
        for k, b in enumerate((half, half + 2)):
            for part in range(2):
                at = 128 * k + 64 * part
                e_own[part, :, 512 * b : 512 * b + 512] = (got[at : at + 32] + got[at + 32 : at + 64]) * sign
    e_copy = remote(e_own, e_other, prm_s.at[2], prm_r.at[2], core)
    e_copy.start()

    prm_core.wait()
    prm_strip.wait()
    both = prm[...] + prm_in[...]
    shift = both[0:1, :]
    col = lax.broadcasted_iota(jnp.int32, (NT, 128), 1)
    freq = lax.rem(lax.rem(col, 64) + 32 * g, NF)
    angle = (2.0 * math.pi / NF) * lax.rem(lax.broadcasted_iota(jnp.int32, (NT, 128), 0) * freq, NF).astype(F32)
    scale = 1.0 / math.sqrt(NF)
    real_in = col < 64

    def base(tile):
        phase = jnp.zeros((1, 128), F32)
        for t in range(4):
            phase = phase + jnp.where(tile == float(t), both[1 + t : 2 + t, :], 0.0)
        im, re = sincos(angle + phase)
        im, re = im * scale, re * scale
        return jnp.concatenate([jnp.where(real_in, re, -im), jnp.where(real_in, im, re)], axis=0)

    far = (4 * (1 - 2 * odd)).astype(F32)
    inside = jnp.where(odd == 1, (s > 1).astype(F32), (s < strips - 2).astype(F32))
    for nd in range(4):
        dest = block_of(nd)
        here, there = base(prm[8 + nd : 9 + nd, :]), base(prm_pair[pl.ds(8 + dest, 1), :])
        rows = slice(64 * nd, 64 * nd + 64)
        for n in range(4):
            source = block_of(n)
            own_hi, own_lo = split(jnp.where(shift == (nd - source).astype(F32), here, 0.0))
            step = (dest - source).astype(F32)
            pair_hi, pair_lo = split(jnp.where(shift == step + far, there, 0.0))
            halo_hi, halo_lo = split(jnp.where(shift == step - far, there * inside, 0.0))
            below = slice(256 + 64 * nd, 320 + 64 * nd)
            for k, (u, v, w) in enumerate(
                ((own_hi, pair_hi, halo_hi), (own_hi, pair_hi, halo_hi), (own_lo, pair_lo, halo_lo))
            ):
                at = 512 * k + 128 * n
                ww[rows, at : at + 128] = u
                ww[below, at : at + 128] = v
                wh[n, rows, 128 * k : 128 * k + 128] = w
    for i in (2, 3, 5, 6, 7):
        snd_copy(i).wait_recv()
    e_copy.wait()

    def spectrum(a, b, i, at, depth):
        re = jnp.concatenate([a[i, 0], b[i, 0]], axis=0)
        im = jnp.concatenate([a[i, 1], b[i, 1]], axis=0)
        for half_p, parts in enumerate(butterflies(re, im, tw)):
            for j, pieces in enumerate(parts):
                for half, w in enumerate(pieces):
                    hi, lo = split(w)
                    for k, x in enumerate((hi, lo, hi)):
                        at_k = 512 * k + 256 * half
                        spread[half_p, 64 * j : 64 * j + 64, at_k : at_k + 256] = x
        even, uneven = (dot(spread[k], table[k]) for k in range(2))
        early = lax.broadcasted_iota(jnp.int32, (64, 128), 1) < 64
        for j in range(4):
            for b4 in range(4):
                first, second = (even, uneven) if b4 % 2 == 0 else (uneven, even)
                rows = slice(64 * j, 64 * j + 64)
                c0 = 128 * (b4 // 2)
                u = jnp.where(early, first[rows, c0 : c0 + 128], second[rows, c0 : c0 + 128])
                v = jnp.where(early, first[rows, 256 + c0 : 384 + c0], second[rows, 256 + c0 : 384 + c0])
                e0 = 512 * b4 + 128 * j
                c, w = (
                    jnp.concatenate([e_own[part, :, e0 : e0 + 128], e_other[part, :, e0 : e0 + 128]], axis=0)
                    for part in range(2)
                )
                for half, value in enumerate((u * c - v * w, u * w + v * c)):
                    hi, lo = split(value)
                    for k, x in enumerate((hi, lo, hi)):
                        spec[b4, pl.ds(k * depth + at + 64 * half, 64), 128 * j : 128 * j + 128] = x

    def block_at(dg, dh):
        return 2 * lax.rem(g + dg, 2) + lax.rem(h + dh, 2)

    def near_copy(ii):
        return remote(near.at[1, ii], near_in.at[ii], near_s.at[ii], near_r.at[ii], core)

    def dest_rows(n):
        return pl.ds(pl.multiple_of(64 * (3 - block_of(n)), 64), 64)

    def row_copy(dg, i):
        at, ii = dest_rows(lax.rem(i, 4)), i // 4
        return remote(side.at[dg, ii, at], side_in.at[dg, ii, at], row_s.at[dg, i], row_r.at[dg, i], peer(dg, 0, 1))

    def opp_cross(i):
        return remote(opp.at[i], relay_in.at[i], rel_s.at[i], rel_r.at[i], peer(0, 1, 1))

    def opp_direct(i):
        return remote(opp.at[i], relay_in.at[i], rel_s.at[i], rel_r.at[i], peer(0, 0, 1))

    def cross_copy(dg, i):
        return remote(cross.at[dg, i], cross_in.at[dg, i], crs_s.at[dg, i], crs_r.at[dg, i], peer(dg, 1, 1))

    def own_rows(ii):
        def one(n, carry):
            @pl.when(jnp.logical_and(ii == 0, n == 1))
            def _():
                a_copy(2).start()
                b_copy(2).start()

            @pl.when(jnp.logical_and(ii == 0, n == 3))
            def _():
                pass_on(2)
                a_copy(3).start()
                b_copy(3).start()

            spectrum(keep, other, 4 * ii + n, pl.multiple_of(128 * n, 128), 512)
            return carry

        lax.fori_loop(0, 4, one, 0)
        for dh in (1, 0):
            for dg in range(2):
                total = dot(ww[...], spec[block_at(dg, dh)])
                if dh == 0:
                    near[dg, ii] = total[0:256]
                else:
                    side[dg, ii] = total[0:256]
                    for n in (1, 3):
                        row_copy(dg, 4 * ii + n).start()
                pp[2 * dg + dh, ii] = total[256:512]
        near_copy(ii).start()

    def collect(i):
        n, ii = lax.rem(i, 4), i // 4
        at = dest_rows(n)
        for dg in range(2):
            cross_copy(dg, i).wait()
        parts = [
            near[0, ii, at, :] + side_in[0, ii, at, :] + cross_in[0, i],
            near_in[ii, at, :] + side_in[1, ii, at, :] + cross_in[1, i],
        ]
        got = dot(jnp.concatenate(split(jnp.concatenate(parts, axis=0)), axis=0), perm[h])
        rows = got[0:128] + got[128:256]
        for dg in range(2):
            row = 4 * (3 - block_of(n)) + 2 * lax.rem(g + dg, 2) + ii
            for c in range(4):
                for part in range(2):
                    at = 64 * dg + 32 * part
                    flat[c, part, pl.ds(row, 32, stride=16), :] = rows[at : at + 32, 128 * c : 128 * c + 128]

    def relay(i):
        n, ii = lax.rem(i, 4), i // 4

        @pl.when(lax.rem(i, 2) == 0)
        def _():
            opp_cross(i).wait()
            at = dest_rows(n)
            for dg in range(2):
                side[dg, ii, at, :] = side[dg, ii, at, :] + relay_in[i, dg]
                row_copy(dg, i).start()

        @pl.when(lax.rem(i, 2) == 1)
        def _():
            opp_direct(i).wait()
            for dg in range(2):
                cross[dg, i] = cross[dg, i] + relay_in[i, dg]
                cross_copy(dg, i).start()

    def step(i, carry):
        n, ii = lax.rem(i, 4), i // 4

        @pl.when(i == 1)
        def _():
            a_copy(5).start()
            b_copy(5).start()

        @pl.when(i == 2)
        def _():
            pass_on(3)
            a_copy(6).start()
            b_copy(6).start()

        @pl.when(i == 3)
        def _():
            a_copy(7).start()
            b_copy(7).start()

        @pl.when(jnp.logical_or(i == 0, i == 3))
        def _():
            own_rows(i // 3)

        a_copy(i).wait_recv()
        b_copy(i).wait_recv()

        spectrum(halo_a, halo_b, i, 0, 128)
        mine = pl.ds(pl.multiple_of(64 * n, 64), 64)
        for dh in range(2):
            for dg in range(2):
                total = dot(wh[n], spec[block_at(dg, dh), 0:384, :])
                pp[2 * dg + dh, ii] = pp[2 * dg + dh, ii] + total
                if dh == 0:
                    opp[i, dg] = pp[2 * dg, ii, mine, :]
                else:
                    cross[dg, i] = pp[2 * dg + 1, ii, mine, :]
            if dh == 0:

                @pl.when(lax.rem(i, 2) == 0)
                def _():
                    opp_cross(i).start()

                @pl.when(lax.rem(i, 2) == 1)
                def _():
                    opp_direct(i).start()

        @pl.when(lax.rem(i, 2) == 0)
        def _():
            for dg in range(2):
                cross_copy(dg, i).start()

        @pl.when(i >= 1)
        def _():
            relay(i - 1)

        @pl.when(i >= 4)
        def _():
            @pl.when(i == 4)
            def _():
                near_copy(0).wait()

            for dg in range(2):
                row_copy(dg, i - 4).wait()
            collect(i - 4)

        return carry

    lax.fori_loop(0, 8, step, 0)
    near_copy(1).wait()

    def last(i, carry):
        for dg in range(2):
            row_copy(dg, i).wait()
        collect(i)
        return carry

    lax.fori_loop(4, 6, last, 0)
    relay(7)
    lax.fori_loop(6, 8, last, 0)
    results = [
        pltpu.make_async_copy(flat.at[c], out.at[:, :, pl.ds(128 * c, 128)], load_sem.at[c]) for c in range(4)
    ]
    for c in results:
        c.start()
    for i in range(8):
        snd_copy(i).wait_send()
        if i != 4:
            a_copy(i).wait_send()
            b_copy(i).wait_send()
    for hops in range(1, 4):
        for which in range(2):
            via_copy(hops, which).wait_send()
    for c in results:
        c.wait()


def local(strips, field, spectral_phase, chirp_shift, tile_map, tile_phase):
    waves, tw = dft_tables()
    vmem = pl.BlockSpec(memory_space=pltpu.VMEM)
    hbm = pl.BlockSpec(memory_space=pl.ANY)
    rows = pltpu.VMEM((8, 2, 32, 1024), F32)
    small = pltpu.VMEM((16, 128), F32)
    phase = pltpu.VMEM((2, 32, NY), F32)
    sums = pltpu.VMEM((2, 2, 256, 512), F32)
    dma = pltpu.SemaphoreType.DMA
    out = pl.pallas_call(
        functools.partial(kernel, strips),
        in_specs=[hbm, hbm, hbm, hbm, vmem, vmem, pl.BlockSpec(memory_space=pltpu.SMEM)],
        out_specs=pl.BlockSpec(memory_space=pl.ANY),
        out_shape=jax.ShapeDtypeStruct((2, 512, 512), F32),
        scratch_shapes=[
            pltpu.VMEM((8, 2, 512, 128), F32),
            rows, rows, rows, rows, rows,
            small, small, small, small,
            pltpu.VMEM((32, NY), F32),
            pltpu.VMEM(waves.shape, F32),
            pltpu.VMEM(tw.shape, F32),
            phase, phase,
            pltpu.VMEM((2, 1536, 512), BF),
            pltpu.VMEM((2, 512, 512), BF),
            pltpu.VMEM((512, 1536), BF),
            pltpu.VMEM((4, 256, 384), BF),
            pltpu.VMEM((2, 256, 1536), BF),
            pltpu.VMEM((4, 1536, 512), BF),
            sums,
            pltpu.VMEM((2, 256, 512), F32),
            sums, sums,
            pltpu.VMEM((4, 2, 256, 512), F32),
            pltpu.VMEM((8, 2, 64, 512), F32),
            pltpu.VMEM((8, 2, 64, 512), F32),
            pltpu.VMEM((2, 8, 64, 512), F32),
            pltpu.VMEM((2, 8, 64, 512), F32),
            pltpu.VMEM((2, 2, 32, 1024), F32),
            pltpu.VMEM((2, 2, 32, 1024), F32),
            dma((11,)),
            *[dma((8,))] * 6,
            dma((3,)), dma((3,)),
            dma((2,)), dma((2,)),
            dma((2, 8)), dma((2, 8)),
            dma((8,)), dma((8,)),
            dma((2, 8)), dma((2, 8)),
            *[dma((2,))] * 4,
        ],
        compiler_params=pltpu.CompilerParams(
            collective_id=0, has_side_effects=True, vmem_limit_bytes=VMEM * 2**20
        ),
        cost_estimate=pl.CostEstimate(flops=40 * 10**9, bytes_accessed=10 * 2**20, transcendentals=0),
    )(
        field.reshape(2, 512, 1024), spectral_phase, jnp.asarray(waves), jnp.asarray(tw),
        chirp_shift.reshape(1, 32), tile_phase, tile_map,
    )
    return out.reshape(2, NT, 16, 512)


def solution(mesh):
    placed = (P(None, "freq", "xs", "yh"), P("freq", None), P("freq"), P("xs"), P(None, "freq"))
    return jax.shard_map(
        functools.partial(local, mesh.shape["xs"]),
        mesh=mesh,
        in_specs=placed,
        out_specs=P(None, None, "xs", ("freq", "yh")),
        check_vma=False,
    )
```

```python
import functools
import math

import jax
import jax.numpy as jnp
import numpy as np
from jax import lax
from jax.experimental import pallas as pl
from jax.experimental.pallas import tpu as pltpu
from jax.sharding import PartitionSpec as P

NF = 64
NY = 2048
NT = 32
VMEM = 60
BF = jnp.bfloat16
F32 = jnp.float32
AXES = ("freq", "xs", "yh")
MESH = pl.DeviceIdType.MESH


def dft_tables():
    m = np.arange(256)
    angle = 2.0 * np.pi * (np.outer(m, m) % 256) / 256
    waves = np.stack([np.cos(angle), np.sin(angle)]) / math.sqrt(NY)
    odd_order = np.concatenate([np.arange(64) + 64 * b for b in (1, 0, 3, 2)])
    turn = 2.0 * np.pi * np.outer(np.arange(8), m) / NY
    twiddle = np.stack([np.cos(turn), np.sin(turn)])
    return np.stack([waves, waves[:, :, odd_order]]).astype(np.float32), twiddle.astype(np.float32)


def split(value):
    high = value.astype(BF)
    return high, (value - high.astype(F32)).astype(BF)


def dot(a, b):
    return jnp.dot(a, b, preferred_element_type=F32)


def dot_t(a, b):
    return lax.dot_general(a, b, (((1,), (1,)), ((), ())), preferred_element_type=F32)


def sincos(x):
    k = jnp.floor(x * (2.0 / math.pi) + 0.5)
    r = ((x - k * 1.5703125) - k * 4.837512969970703125e-4) - k * 7.54978995489188216e-8
    z = r * r
    sine = r + r * z * (-1.6666654611e-1 + z * (8.3321608736e-3 - z * 1.9515295891e-4))
    cosine = (1.0 - 0.5 * z) + z * z * (4.166664568298827e-2 + z * (-1.388731625493765e-3 + z * 2.443315711809948e-5))
    half = jnp.floor(k * 0.5)
    swap = (k - 2.0 * half) > 0.5
    sign = 1.0 - 2.0 * (half - 2.0 * jnp.floor(half * 0.5))
    return sign * jnp.where(swap, cosine, sine), sign * jnp.where(swap, -sine, cosine)


def butterflies(re, im, tw):
    a = [(re[:, 256 * c : 256 * c + 256], im[:, 256 * c : 256 * c + 256]) for c in range(4)]
    r = math.sqrt(0.5)

    def add(u, v):
        return u[0] + v[0], u[1] + v[1]

    def sub(u, v):
        return u[0] - v[0], u[1] - v[1]

    def mi(u):
        return u[1], -u[0]

    def four(b):
        e0, e1 = add(b[0], b[2]), sub(b[0], b[2])
        e2, e3 = add(b[1], b[3]), mi(sub(b[1], b[3]))
        return add(e0, e2), add(e1, e3), sub(e0, e2), sub(e1, e3)

    even = four(a)
    b1 = ((a[1][0] + a[1][1]) * r, (a[1][1] - a[1][0]) * r)
    b3 = ((a[3][1] - a[3][0]) * r, (-a[3][0] - a[3][1]) * r)
    odd = four((a[0], b1, mi(a[2]), b3))
    both = []
    for side, parts in enumerate((even, odd)):
        row = []
        for j in range(4):
            p = 2 * j + side
            u = parts[j]
            if p:
                c, s = tw[0, p : p + 1, :], tw[1, p : p + 1, :]
                u = u[0] * c + u[1] * s, u[1] * c - u[0] * s
            row.append(u)
        both.append(row)
    return both


def kernel(
    strips, field, phi_hbm, waves_hbm, tw_hbm, shift_row, tile_phase, tile_ids, out,
    flat, snd, keep, other, halo_a, halo_b, prm, prm_out, prm_in, prm_pair,
    phi, waves, tw, e_own, e_other, table, perm, ww, wh,
    spread, spec, near, near_in, side, side_in, pp, opp, relay_in, cross, cross_in, via_1, via_2, *rest,
):
    (load_sem, snd_s, snd_r, ha_s, ha_r, hb_s, hb_r, prm_s, prm_r,
     near_s, near_r, row_s, row_r, rel_s, rel_r, crs_s, crs_r, v1_s, v1_r, v2_s, v2_r) = rest
    g, s, h = (lax.axis_index(a) for a in AXES)
    odd = lax.rem(s, 2)
    pair = s + 1 - 2 * odd
    onward = lax.rem(s + strips + 4 * odd - 2, strips)
    back = lax.rem(s + strips + 2 - 4 * odd, strips)
    core = (1 - g, s, h)

    z, y, turns = s // 8, lax.rem(s // 2, 4), strips // 8
    hop = 1 - 2 * odd
    across = 8 * z + 2 * lax.rem(y + 4 + hop, 4) + odd
    across_from = 8 * z + 2 * lax.rem(y + 4 - hop, 4) + odd
    z_on = 8 * lax.rem(z + turns - hop, turns) + odd
    z_back = 8 * lax.rem(z + turns + hop, turns) + odd
    leaves = (y == 2 - odd).astype(jnp.int32)
    third = across + leaves * (z_on + 2 * (3 - 3 * odd) - across)
    enters = (y == 3 - 3 * odd).astype(jnp.int32)
    third_from = across_from + enters * (z_back + 2 * (2 - odd) - across_from)

    def peer(dg, ds, dh):
        return (lax.rem(g + dg, 2), pair if ds else s, lax.rem(h + dh, 2))

    def remote(src, dst, a, b, to):
        return pltpu.make_async_remote_copy(
            src_ref=src, dst_ref=dst, send_sem=a, recv_sem=b, device_id=to, device_id_type=MESH
        )

    def block_of(n):
        return n + odd * (3 - 2 * n)

    loads = [
        pltpu.make_async_copy(field.at[:, :, pl.ds(128 * y, 128)], flat.at[y], load_sem.at[y]) for y in range(8)
    ]
    tables = [
        pltpu.make_async_copy(src, dst, load_sem.at[8 + k])
        for k, (src, dst) in enumerate(((waves_hbm, waves), (tw_hbm, tw), (phi_hbm, phi)))
    ]
    for c in loads + tables:
        c.start()
    barrier = pltpu.get_barrier_semaphore()
    greet = [core, peer(0, 0, 1), peer(1, 0, 1), peer(0, 1, 1), peer(1, 1, 1), (g, onward, h), (g, back, h)]
    greet += [(g, across, h), (g, across_from, h), (g, third, h), (g, third_from, h)]
    for to in greet:
        pl.semaphore_signal(barrier, inc=1, device_id=to, device_id_type=MESH)

    def snd_copy(i):
        return remote(snd.at[i], other.at[i], snd_s.at[i], snd_r.at[i], core)

    def a_copy(i):
        return remote(keep.at[i], halo_a.at[i], ha_s.at[i], ha_r.at[i], (g, onward, h))

    def b_copy(i):
        return remote(other.at[i], halo_b.at[i], hb_s.at[i], hb_r.at[i], (g, onward, h))

    def via_copy(hops, slot):
        which, i = ((0, 4), (1, 4), (1, 6))[slot]
        if hops == 1:
            src = (keep, other)[which].at[i]
            return remote(src, via_1.at[slot], v1_s.at[slot], v1_r.at[slot], (g, across, h))
        if hops == 2:
            return remote(via_1.at[slot], via_2.at[slot], v2_s.at[slot], v2_r.at[slot], (g, across, h))
        dst, sems = ((halo_a, (ha_s, ha_r)), (halo_b, (hb_s, hb_r)))[which]
        return remote(via_2.at[slot], dst.at[i], sems[0].at[i], sems[1].at[i], (g, third, h))

    def pass_on(hops, slots):
        for slot in slots:
            via_copy(hops - 1, slot).wait_recv()
            via_copy(hops, slot).start()

    def gather_rows(i, whose, into):
        row = 4 * block_of(lax.rem(i, 4)) + 2 * whose + i // 4
        for c in range(2):
            for y in range(8):
                into[i, c, :, 128 * y : 128 * y + 128] = flat[y, c, pl.ds(row, 32, stride=16), :]

    gap = jnp.zeros((8, 32), F32)
    rows = jnp.concatenate([shift_row[...].astype(F32), tile_phase[...], jnp.zeros((3, 32), F32)], axis=0)
    prm[0:8, :] = jnp.concatenate([rows, gap, rows, gap], axis=1)
    for rb in range(4):
        prm[8 + rb : 9 + rb, :] = jnp.full((1, 128), tile_ids[rb], jnp.int32).astype(F32)
    prm[12:16, :] = jnp.zeros((4, 128), F32)
    prm_out[...] = pltpu.roll(prm[...], 32, 1)
    prm_core = remote(prm_out, prm_in, prm_s.at[0], prm_r.at[0], core)
    prm_strip = remote(prm, prm_pair, prm_s.at[1], prm_r.at[1], peer(0, 1, 1))

    for c in loads:
        c.wait()

    def pack_send(i, carry):
        gather_rows(i, 1 - g, snd)
        snd_copy(i).start()
        return carry

    def pack_keep(i, carry):
        gather_rows(i, g, keep)
        return carry

    for i in (0, 4, 1):
        gather_rows(i, g, keep)
    pl.semaphore_wait(barrier, len(greet))
    a_copy(0).start()
    via_copy(1, 0).start()
    a_copy(1).start()
    lax.fori_loop(0, 8, pack_send, 0)
    prm_core.start()
    prm_strip.start()
    lax.fori_loop(2, 4, pack_keep, 0)
    lax.fori_loop(5, 8, pack_keep, 0)
    for i in (0, 4, 1):
        snd_copy(i).wait_recv()
        if i == 4:
            via_copy(1, 1).start()
        else:
            b_copy(i).start()

    for c in tables:
        c.wait()
    lane = lax.broadcasted_iota(jnp.int32, (512, 1), 0)
    wave = lax.broadcasted_iota(jnp.int32, (1, 512), 1)
    turn = lax.rem(lane, 128)
    for half in range(2):
        late = (turn >= 64).astype(jnp.int32)
        late = late if half == 0 else 1 - late
        target = 8 * lax.rem(turn, 64) + 2 * (lane // 128) + late
        perm[half] = jnp.where(target == wave, 1.0, 0.0).astype(BF)
        c_hi, c_lo = split(waves[half, 0])
        s_hi, s_lo = split(waves[half, 1])
        for k, (c, w) in enumerate(((c_hi, s_hi), (c_hi, s_hi), (c_lo, s_lo))):
            table[half, 512 * k : 512 * k + 256, 0:256] = c
            table[half, 512 * k : 512 * k + 256, 256:512] = -w
            table[half, 512 * k + 256 : 512 * k + 512, 0:256] = w
            table[half, 512 * k + 256 : 512 * k + 512, 256:512] = c

    lanes = lax.rem(lax.broadcasted_iota(jnp.int32, (1, 512), 1), 128)
    for half in range(2):
        late = lanes >= 64 if half == 0 else lanes < 64
        sign = 1.0 - 2.0 * jnp.where(late, h, 0).astype(F32)
        stack = []
        for b in (half, half + 2):
            sine, cosine = sincos(phi[:, 512 * b : 512 * b + 512])
            stack += [*split(cosine), *split(sine)]
        got = dot_t(jnp.concatenate(stack, axis=0), perm[half])
        for k, b in enumerate((half, half + 2)):
            for part in range(2):
                at = 128 * k + 64 * part
                e_own[part, :, 512 * b : 512 * b + 512] = (got[at : at + 32] + got[at + 32 : at + 64]) * sign
    e_copy = remote(e_own, e_other, prm_s.at[2], prm_r.at[2], core)
    e_copy.start()

    prm_core.wait()
    prm_strip.wait()
    both = prm[...] + prm_in[...]
    shift = both[0:1, :]
    col = lax.broadcasted_iota(jnp.int32, (NT, 128), 1)
    freq = lax.rem(lax.rem(col, 64) + 32 * g, NF)
    angle = (2.0 * math.pi / NF) * lax.rem(lax.broadcasted_iota(jnp.int32, (NT, 128), 0) * freq, NF).astype(F32)
    scale = 1.0 / math.sqrt(NF)
    real_in = col < 64

    def base(tile):
        phase = jnp.zeros((1, 128), F32)
        for t in range(4):
            phase = phase + jnp.where(tile == float(t), both[1 + t : 2 + t, :], 0.0)
        im, re = sincos(angle + phase)
        im, re = im * scale, re * scale
        return jnp.concatenate([jnp.where(real_in, re, -im), jnp.where(real_in, im, re)], axis=0)

    far = (4 * (1 - 2 * odd)).astype(F32)
    inside = jnp.where(odd == 1, (s > 1).astype(F32), (s < strips - 2).astype(F32))
    for nd in range(4):
        dest = block_of(nd)
        here, there = base(prm[8 + nd : 9 + nd, :]), base(prm_pair[pl.ds(8 + dest, 1), :])
        rows = slice(64 * nd, 64 * nd + 64)
        for n in range(4):
            source = block_of(n)
            own_hi, own_lo = split(jnp.where(shift == (nd - source).astype(F32), here, 0.0))
            step = (dest - source).astype(F32)
            pair_hi, pair_lo = split(jnp.where(shift == step + far, there, 0.0))
            halo_hi, halo_lo = split(jnp.where(shift == step - far, there * inside, 0.0))
            below = slice(256 + 64 * nd, 320 + 64 * nd)
            for k, (u, v, w) in enumerate(
                ((own_hi, pair_hi, halo_hi), (own_hi, pair_hi, halo_hi), (own_lo, pair_lo, halo_lo))
            ):
                at = 512 * k + 128 * n
                ww[rows, at : at + 128] = u
                ww[below, at : at + 128] = v
                wh[n, rows, 128 * k : 128 * k + 128] = w
    for i in (2, 3, 5, 6, 7):
        snd_copy(i).wait_recv()
    e_copy.wait()
    via_copy(1, 2).start()

    def spectrum(a, b, i, at, depth):
        re = jnp.concatenate([a[i, 0], b[i, 0]], axis=0)
        im = jnp.concatenate([a[i, 1], b[i, 1]], axis=0)
        for half_p, parts in enumerate(butterflies(re, im, tw)):
            for j, pieces in enumerate(parts):
                for half, w in enumerate(pieces):
                    hi, lo = split(w)
                    for k, x in enumerate((hi, lo, hi)):
                        at_k = 512 * k + 256 * half
                        spread[half_p, 64 * j : 64 * j + 64, at_k : at_k + 256] = x
        even, uneven = (dot(spread[k], table[k]) for k in range(2))
        early = lax.broadcasted_iota(jnp.int32, (64, 128), 1) < 64
        for j in range(4):
            for b4 in range(4):
                first, second = (even, uneven) if b4 % 2 == 0 else (uneven, even)
                rows = slice(64 * j, 64 * j + 64)
                c0 = 128 * (b4 // 2)
                u = jnp.where(early, first[rows, c0 : c0 + 128], second[rows, c0 : c0 + 128])
                v = jnp.where(early, first[rows, 256 + c0 : 384 + c0], second[rows, 256 + c0 : 384 + c0])
                e0 = 512 * b4 + 128 * j
                c, w = (
                    jnp.concatenate([e_own[part, :, e0 : e0 + 128], e_other[part, :, e0 : e0 + 128]], axis=0)
                    for part in range(2)
                )
                for half, value in enumerate((u * c - v * w, u * w + v * c)):
                    hi, lo = split(value)
                    for k, x in enumerate((hi, lo, hi)):
                        spec[b4, pl.ds(k * depth + at + 64 * half, 64), 128 * j : 128 * j + 128] = x

    def block_at(dg, dh):
        return 2 * lax.rem(g + dg, 2) + lax.rem(h + dh, 2)

    def near_copy(ii):
        return remote(near.at[1, ii], near_in.at[ii], near_s.at[ii], near_r.at[ii], core)

    def dest_rows(n):
        return pl.ds(pl.multiple_of(64 * (3 - block_of(n)), 64), 64)

    def row_copy(dg, i):
        at, ii = dest_rows(lax.rem(i, 4)), i // 4
        return remote(side.at[dg, ii, at], side_in.at[dg, ii, at], row_s.at[dg, i], row_r.at[dg, i], peer(dg, 0, 1))

    def opp_copy(dg, i, to):
        return remote(opp.at[i, dg], relay_in.at[i, dg], rel_s.at[i, dg], rel_r.at[i, dg], to)

    def opp_cross(dg, i):
        return opp_copy(dg, i, peer(0, 1, 1))

    def opp_direct(dg, i):
        return opp_copy(dg, i, peer(0, 0, 1))

    def cross_copy(dg, i):
        return remote(cross.at[dg, i], cross_in.at[dg, i], crs_s.at[dg, i], crs_r.at[dg, i], peer(dg, 1, 1))

    def own_rows(ii):
        def one(n, carry):
            @pl.when(jnp.logical_and(ii == 0, n == 1))
            def _():
                a_copy(2).start()
                b_copy(2).start()

            @pl.when(jnp.logical_and(ii == 0, n == 3))
            def _():
                pass_on(2, (0, 1))
                a_copy(3).start()
                b_copy(3).start()

            spectrum(keep, other, 4 * ii + n, pl.multiple_of(128 * n, 128), 512)
            return carry

        lax.fori_loop(0, 4, one, 0)
        for dh in (1, 0):
            for dg in range(2):
                total = dot(ww[...], spec[block_at(dg, dh)])
                if dh == 0:
                    near[dg, ii] = total[0:256]
                else:
                    side[dg, ii] = total[0:256]
                    for n in (1, 3):
                        row_copy(dg, 4 * ii + n).start()
                pp[2 * dg + dh, ii] = total[256:512]
        near_copy(ii).start()

    def collect(i):
        n, ii = lax.rem(i, 4), i // 4
        at = dest_rows(n)
        for dg in range(2):
            cross_copy(dg, i).wait()
        parts = [
            near[0, ii, at, :] + side_in[0, ii, at, :] + cross_in[0, i],
            near_in[ii, at, :] + side_in[1, ii, at, :] + cross_in[1, i],
        ]
        got = dot(jnp.concatenate(split(jnp.concatenate(parts, axis=0)), axis=0), perm[h])
        rows = got[0:128] + got[128:256]
        for dg in range(2):
            row = 4 * (3 - block_of(n)) + 2 * lax.rem(g + dg, 2) + ii
            for c in range(4):
                for part in range(2):
                    at = 64 * dg + 32 * part
                    flat[c, part, pl.ds(row, 32, stride=16), :] = rows[at : at + 32, 128 * c : 128 * c + 128]

    def relay(i):
        n, ii = lax.rem(i, 4), i // 4

        @pl.when(lax.rem(i, 2) == 0)
        def _():
            at = dest_rows(n)
            for dg in range(2):
                opp_cross(dg, i).wait()
                side[dg, ii, at, :] = side[dg, ii, at, :] + relay_in[i, dg]
                row_copy(dg, i).start()

        @pl.when(lax.rem(i, 2) == 1)
        def _():
            for dg in range(2):
                opp_direct(dg, i).wait()
                cross[dg, i] = cross[dg, i] + relay_in[i, dg]
                cross_copy(dg, i).start()

    def step(i, carry):
        n, ii = lax.rem(i, 4), i // 4

        @pl.when(i == 1)
        def _():
            a_copy(5).start()
            b_copy(5).start()

        @pl.when(i == 2)
        def _():
            pass_on(3, (0, 1))
            a_copy(6).start()

        @pl.when(i == 3)
        def _():
            a_copy(7).start()
            b_copy(7).start()
            pass_on(2, (2,))

        @pl.when(i == 4)
        def _():
            pass_on(3, (2,))

        @pl.when(jnp.logical_or(i == 0, i == 3))
        def _():
            own_rows(i // 3)

        a_copy(i).wait_recv()
        b_copy(i).wait_recv()

        spectrum(halo_a, halo_b, i, 0, 128)
        mine = pl.ds(pl.multiple_of(64 * n, 64), 64)
        for dh in range(2):
            for dg in range(2):
                total = dot(wh[n], spec[block_at(dg, dh), 0:384, :])
                pp[2 * dg + dh, ii] = pp[2 * dg + dh, ii] + total
                if dh == 1:
                    cross[dg, i] = pp[2 * dg + 1, ii, mine, :]
                    continue
                opp[i, dg] = pp[2 * dg, ii, mine, :]

                @pl.when(lax.rem(i, 2) == 0)
                def _():
                    opp_cross(dg, i).start()

                @pl.when(lax.rem(i, 2) == 1)
                def _():
                    opp_direct(dg, i).start()

        @pl.when(lax.rem(i, 2) == 0)
        def _():
            for dg in range(2):
                cross_copy(dg, i).start()

        @pl.when(i >= 1)
        def _():
            relay(i - 1)

        @pl.when(i >= 4)
        def _():
            @pl.when(i == 4)
            def _():
                near_copy(0).wait()

            for dg in range(2):
                row_copy(dg, i - 4).wait()
            collect(i - 4)

        return carry

    lax.fori_loop(0, 8, step, 0)
    near_copy(1).wait()

    def last(i, carry):
        for dg in range(2):
            row_copy(dg, i).wait()
        collect(i)
        return carry

    lax.fori_loop(4, 6, last, 0)
    relay(7)
    lax.fori_loop(6, 8, last, 0)
    results = [
        pltpu.make_async_copy(flat.at[c], out.at[:, :, pl.ds(128 * c, 128)], load_sem.at[c]) for c in range(4)
    ]
    for c in results:
        c.start()
    for i in range(8):
        snd_copy(i).wait_send()
        if i != 4:
            a_copy(i).wait_send()
        if i not in (4, 6):
            b_copy(i).wait_send()
    for hops in range(1, 4):
        for slot in range(3):
            via_copy(hops, slot).wait_send()
    for c in results:
        c.wait()


def local(strips, field, spectral_phase, chirp_shift, tile_map, tile_phase):
    waves, tw = dft_tables()
    vmem = pl.BlockSpec(memory_space=pltpu.VMEM)
    hbm = pl.BlockSpec(memory_space=pl.ANY)
    rows = pltpu.VMEM((8, 2, 32, 1024), F32)
    small = pltpu.VMEM((16, 128), F32)
    phase = pltpu.VMEM((2, 32, NY), F32)
    sums = pltpu.VMEM((2, 2, 256, 512), F32)
    dma = pltpu.SemaphoreType.DMA
    out = pl.pallas_call(
        functools.partial(kernel, strips),
        in_specs=[hbm, hbm, hbm, hbm, vmem, vmem, pl.BlockSpec(memory_space=pltpu.SMEM)],
        out_specs=pl.BlockSpec(memory_space=pl.ANY),
        out_shape=jax.ShapeDtypeStruct((2, 512, 512), F32),
        scratch_shapes=[
            pltpu.VMEM((8, 2, 512, 128), F32),
            rows, rows, rows, rows, rows,
            small, small, small, small,
            pltpu.VMEM((32, NY), F32),
            pltpu.VMEM(waves.shape, F32),
            pltpu.VMEM(tw.shape, F32),
            phase, phase,
            pltpu.VMEM((2, 1536, 512), BF),
            pltpu.VMEM((2, 512, 512), BF),
            pltpu.VMEM((512, 1536), BF),
            pltpu.VMEM((4, 256, 384), BF),
            pltpu.VMEM((2, 256, 1536), BF),
            pltpu.VMEM((4, 1536, 512), BF),
            sums,
            pltpu.VMEM((2, 256, 512), F32),
            sums, sums,
            pltpu.VMEM((4, 2, 256, 512), F32),
            pltpu.VMEM((8, 2, 64, 512), F32),
            pltpu.VMEM((8, 2, 64, 512), F32),
            pltpu.VMEM((2, 8, 64, 512), F32),
            pltpu.VMEM((2, 8, 64, 512), F32),
            pltpu.VMEM((3, 2, 32, 1024), F32),
            pltpu.VMEM((3, 2, 32, 1024), F32),
            dma((11,)),
            *[dma((8,))] * 6,
            dma((3,)), dma((3,)),
            dma((2,)), dma((2,)),
            dma((2, 8)), dma((2, 8)),
            dma((8, 2)), dma((8, 2)),
            dma((2, 8)), dma((2, 8)),
            *[dma((3,))] * 4,
        ],
        compiler_params=pltpu.CompilerParams(
            collective_id=0, has_side_effects=True, vmem_limit_bytes=VMEM * 2**20
        ),
        cost_estimate=pl.CostEstimate(flops=40 * 10**9, bytes_accessed=10 * 2**20, transcendentals=0),
    )(
        field.reshape(2, 512, 1024), spectral_phase, jnp.asarray(waves), jnp.asarray(tw),
        chirp_shift.reshape(1, 32), tile_phase, tile_map,
    )
    return out.reshape(2, NT, 16, 512)


def solution(mesh):
    placed = (P(None, "freq", "xs", "yh"), P("freq", None), P("freq"), P("xs"), P(None, "freq"))
    return jax.shard_map(
        functools.partial(local, mesh.shape["xs"]),
        mesh=mesh,
        in_specs=placed,
        out_specs=P(None, None, "xs", ("freq", "yh")),
        check_vma=False,
    )
```

```python
import functools
import math

import jax
import jax.numpy as jnp
import numpy as np
from jax import lax
from jax.experimental import pallas as pl
from jax.experimental.pallas import tpu as pltpu
from jax.sharding import PartitionSpec as P

NF = 64
NY = 2048
NT = 32
VMEM = 60
BF = jnp.bfloat16
F32 = jnp.float32
AXES = ("freq", "xs", "yh")
MESH = pl.DeviceIdType.MESH


def dft_tables():
    m = np.arange(256)
    angle = 2.0 * np.pi * (np.outer(m, m) % 256) / 256
    waves = np.stack([np.cos(angle), np.sin(angle)]) / math.sqrt(NY)
    odd_order = np.concatenate([np.arange(64) + 64 * b for b in (1, 0, 3, 2)])
    turn = 2.0 * np.pi * np.outer(np.arange(8), m) / NY
    twiddle = np.stack([np.cos(turn), np.sin(turn)])
    return np.stack([waves, waves[:, :, odd_order]]).astype(np.float32), twiddle.astype(np.float32)


def split(value):
    high = value.astype(BF)
    return high, (value - high.astype(F32)).astype(BF)


def dot(a, b):
    return jnp.dot(a, b, preferred_element_type=F32)


def dot_t(a, b):
    return lax.dot_general(a, b, (((1,), (1,)), ((), ())), preferred_element_type=F32)


def sincos(x):
    k = jnp.floor(x * (2.0 / math.pi) + 0.5)
    r = ((x - k * 1.5703125) - k * 4.837512969970703125e-4) - k * 7.54978995489188216e-8
    z = r * r
    sine = r + r * z * (-1.6666654611e-1 + z * (8.3321608736e-3 - z * 1.9515295891e-4))
    cosine = (1.0 - 0.5 * z) + z * z * (4.166664568298827e-2 + z * (-1.388731625493765e-3 + z * 2.443315711809948e-5))
    half = jnp.floor(k * 0.5)
    swap = (k - 2.0 * half) > 0.5
    sign = 1.0 - 2.0 * (half - 2.0 * jnp.floor(half * 0.5))
    return sign * jnp.where(swap, cosine, sine), sign * jnp.where(swap, -sine, cosine)


def butterflies(re, im, tw):
    a = [(re[:, 256 * c : 256 * c + 256], im[:, 256 * c : 256 * c + 256]) for c in range(4)]
    r = math.sqrt(0.5)

    def add(u, v):
        return u[0] + v[0], u[1] + v[1]

    def sub(u, v):
        return u[0] - v[0], u[1] - v[1]

    def mi(u):
        return u[1], -u[0]

    def four(b):
        e0, e1 = add(b[0], b[2]), sub(b[0], b[2])
        e2, e3 = add(b[1], b[3]), mi(sub(b[1], b[3]))
        return add(e0, e2), add(e1, e3), sub(e0, e2), sub(e1, e3)

    even = four(a)
    b1 = ((a[1][0] + a[1][1]) * r, (a[1][1] - a[1][0]) * r)
    b3 = ((a[3][1] - a[3][0]) * r, (-a[3][0] - a[3][1]) * r)
    odd = four((a[0], b1, mi(a[2]), b3))
    both = []
    for side, parts in enumerate((even, odd)):
        row = []
        for j in range(4):
            p = 2 * j + side
            u = parts[j]
            if p:
                c, s = tw[0, p : p + 1, :], tw[1, p : p + 1, :]
                u = u[0] * c + u[1] * s, u[1] * c - u[0] * s
            row.append(u)
        both.append(row)
    return both


def kernel(
    strips, field, phi_hbm, waves_hbm, tw_hbm, shift_row, tile_phase, tile_ids, out,
    flat, snd, keep, other, halo_a, halo_b, prm, prm_out, prm_in, prm_pair,
    phi, waves, tw, e_own, e_other, table, perm, ww, wh,
    spread, spec, near, near_in, side, side_in, pp, opp, relay_in, cross, cross_in, via_1, via_2, *rest,
):
    (load_sem, snd_s, snd_r, ha_s, ha_r, hb_s, hb_r, prm_s, prm_r,
     near_s, near_r, row_s, row_r, rel_s, rel_r, crs_s, crs_r, v1_s, v1_r, v2_s, v2_r) = rest
    g, s, h = (lax.axis_index(a) for a in AXES)
    odd = lax.rem(s, 2)
    pair = s + 1 - 2 * odd
    onward = lax.rem(s + strips + 4 * odd - 2, strips)
    back = lax.rem(s + strips + 2 - 4 * odd, strips)
    core = (1 - g, s, h)

    z, y, turns = s // 8, lax.rem(s // 2, 4), strips // 8
    hop = 1 - 2 * odd
    across = 8 * z + 2 * lax.rem(y + 4 + hop, 4) + odd
    across_from = 8 * z + 2 * lax.rem(y + 4 - hop, 4) + odd
    z_on = 8 * lax.rem(z + turns - hop, turns) + odd
    z_back = 8 * lax.rem(z + turns + hop, turns) + odd
    leaves = (y == 2 - odd).astype(jnp.int32)
    third = across + leaves * (z_on + 2 * (3 - 3 * odd) - across)
    enters = (y == 3 - 3 * odd).astype(jnp.int32)
    third_from = across_from + enters * (z_back + 2 * (2 - odd) - across_from)

    def peer(dg, ds, dh):
        return (lax.rem(g + dg, 2), pair if ds else s, lax.rem(h + dh, 2))

    def remote(src, dst, a, b, to):
        return pltpu.make_async_remote_copy(
            src_ref=src, dst_ref=dst, send_sem=a, recv_sem=b, device_id=to, device_id_type=MESH
        )

    def block_of(n):
        return n + odd * (3 - 2 * n)

    loads = [
        pltpu.make_async_copy(field.at[:, :, pl.ds(128 * y, 128)], flat.at[y], load_sem.at[y]) for y in range(8)
    ]
    tables = [
        pltpu.make_async_copy(src, dst, load_sem.at[8 + k])
        for k, (src, dst) in enumerate(((waves_hbm, waves), (tw_hbm, tw), (phi_hbm, phi)))
    ]
    for c in loads + tables:
        c.start()
    barrier = pltpu.get_barrier_semaphore()
    greet = [core, peer(0, 0, 1), peer(1, 0, 1), peer(0, 1, 1), peer(1, 1, 1), (g, onward, h), (g, back, h)]
    greet += [(g, across, h), (g, across_from, h), (g, third, h), (g, third_from, h)]
    for to in greet:
        pl.semaphore_signal(barrier, inc=1, device_id=to, device_id_type=MESH)

    def snd_copy(i):
        return remote(snd.at[i], other.at[i], snd_s.at[i], snd_r.at[i], core)

    def a_copy(i):
        return remote(keep.at[i], halo_a.at[i], ha_s.at[i], ha_r.at[i], (g, onward, h))

    def b_copy(i):
        return remote(other.at[i], halo_b.at[i], hb_s.at[i], hb_r.at[i], (g, onward, h))

    def via_copy(hops, slot):
        which, i = ((0, 4), (1, 4))[slot]
        if hops == 1:
            src = (keep, other)[which].at[i]
            return remote(src, via_1.at[slot], v1_s.at[slot], v1_r.at[slot], (g, across, h))
        if hops == 2:
            return remote(via_1.at[slot], via_2.at[slot], v2_s.at[slot], v2_r.at[slot], (g, across, h))
        dst, sems = ((halo_a, (ha_s, ha_r)), (halo_b, (hb_s, hb_r)))[which]
        return remote(via_2.at[slot], dst.at[i], sems[0].at[i], sems[1].at[i], (g, third, h))

    def pass_on(hops, slots):
        for slot in slots:
            via_copy(hops - 1, slot).wait_recv()
            via_copy(hops, slot).start()

    def gather_rows(i, whose, into):
        row = 4 * block_of(lax.rem(i, 4)) + 2 * whose + i // 4
        for c in range(2):
            for y in range(8):
                into[i, c, :, 128 * y : 128 * y + 128] = flat[y, c, pl.ds(row, 32, stride=16), :]

    gap = jnp.zeros((8, 32), F32)
    rows = jnp.concatenate([shift_row[...].astype(F32), tile_phase[...], jnp.zeros((3, 32), F32)], axis=0)
    prm[0:8, :] = jnp.concatenate([rows, gap, rows, gap], axis=1)
    for rb in range(4):
        prm[8 + rb : 9 + rb, :] = jnp.full((1, 128), tile_ids[rb], jnp.int32).astype(F32)
    prm[12:16, :] = jnp.zeros((4, 128), F32)
    prm_out[...] = pltpu.roll(prm[...], 32, 1)
    prm_core = remote(prm_out, prm_in, prm_s.at[0], prm_r.at[0], core)
    prm_strip = remote(prm, prm_pair, prm_s.at[1], prm_r.at[1], peer(0, 1, 1))

    for c in loads:
        c.wait()

    def pack_send(i, carry):
        gather_rows(i, 1 - g, snd)
        snd_copy(i).start()
        return carry

    def pack_keep(i, carry):
        gather_rows(i, g, keep)
        return carry

    for i in (0, 4, 1):
        gather_rows(i, g, keep)
    pl.semaphore_wait(barrier, len(greet))
    a_copy(0).start()
    via_copy(1, 0).start()
    a_copy(1).start()
    lax.fori_loop(0, 8, pack_send, 0)
    prm_core.start()
    prm_strip.start()
    lax.fori_loop(2, 4, pack_keep, 0)
    lax.fori_loop(5, 8, pack_keep, 0)
    for i in (0, 4, 1):
        snd_copy(i).wait_recv()
        if i == 4:
            via_copy(1, 1).start()
        else:
            b_copy(i).start()

    for c in tables:
        c.wait()
    lane = lax.broadcasted_iota(jnp.int32, (512, 1), 0)
    wave = lax.broadcasted_iota(jnp.int32, (1, 512), 1)
    turn = lax.rem(lane, 128)
    for half in range(2):
        late = (turn >= 64).astype(jnp.int32)
        late = late if half == 0 else 1 - late
        target = 8 * lax.rem(turn, 64) + 2 * (lane // 128) + late
        perm[half] = jnp.where(target == wave, 1.0, 0.0).astype(BF)
        c_hi, c_lo = split(waves[half, 0])
        s_hi, s_lo = split(waves[half, 1])
        for k, (c, w) in enumerate(((c_hi, s_hi), (c_hi, s_hi), (c_lo, s_lo))):
            table[half, 512 * k : 512 * k + 256, 0:256] = c
            table[half, 512 * k : 512 * k + 256, 256:512] = -w
            table[half, 512 * k + 256 : 512 * k + 512, 0:256] = w
            table[half, 512 * k + 256 : 512 * k + 512, 256:512] = c

    lanes = lax.rem(lax.broadcasted_iota(jnp.int32, (1, 512), 1), 128)
    for half in range(2):
        late = lanes >= 64 if half == 0 else lanes < 64
        sign = 1.0 - 2.0 * jnp.where(late, h, 0).astype(F32)
        stack = []
        for b in (half, half + 2):
            sine, cosine = sincos(phi[:, 512 * b : 512 * b + 512])
            stack += [*split(cosine), *split(sine)]
        got = dot_t(jnp.concatenate(stack, axis=0), perm[half])
        for k, b in enumerate((half, half + 2)):
            for part in range(2):
                at = 128 * k + 64 * part
                e_own[part, :, 512 * b : 512 * b + 512] = (got[at : at + 32] + got[at + 32 : at + 64]) * sign
    e_copy = remote(e_own, e_other, prm_s.at[2], prm_r.at[2], core)
    e_copy.start()

    prm_core.wait()
    prm_strip.wait()
    both = prm[...] + prm_in[...]
    shift = both[0:1, :]
    col = lax.broadcasted_iota(jnp.int32, (NT, 128), 1)
    freq = lax.rem(lax.rem(col, 64) + 32 * g, NF)
    angle = (2.0 * math.pi / NF) * lax.rem(lax.broadcasted_iota(jnp.int32, (NT, 128), 0) * freq, NF).astype(F32)
    scale = 1.0 / math.sqrt(NF)
    real_in = col < 64

    def base(tile):
        phase = jnp.zeros((1, 128), F32)
        for t in range(4):
            phase = phase + jnp.where(tile == float(t), both[1 + t : 2 + t, :], 0.0)
        im, re = sincos(angle + phase)
        im, re = im * scale, re * scale
        return jnp.concatenate([jnp.where(real_in, re, -im), jnp.where(real_in, im, re)], axis=0)

    far = (4 * (1 - 2 * odd)).astype(F32)
    inside = jnp.where(odd == 1, (s > 1).astype(F32), (s < strips - 2).astype(F32))
    for nd in range(4):
        dest = block_of(nd)
        here, there = base(prm[8 + nd : 9 + nd, :]), base(prm_pair[pl.ds(8 + dest, 1), :])
        rows = slice(64 * nd, 64 * nd + 64)
        for n in range(4):
            source = block_of(n)
            own_hi, own_lo = split(jnp.where(shift == (nd - source).astype(F32), here, 0.0))
            step = (dest - source).astype(F32)
            pair_hi, pair_lo = split(jnp.where(shift == step + far, there, 0.0))
            halo_hi, halo_lo = split(jnp.where(shift == step - far, there * inside, 0.0))
            below = slice(256 + 64 * nd, 320 + 64 * nd)
            for k, (u, v, w) in enumerate(
                ((own_hi, pair_hi, halo_hi), (own_hi, pair_hi, halo_hi), (own_lo, pair_lo, halo_lo))
            ):
                at = 512 * k + 128 * n
                ww[rows, at : at + 128] = u
                ww[below, at : at + 128] = v
                wh[n, rows, 128 * k : 128 * k + 128] = w
    for i in (2, 3, 5, 6, 7):
        snd_copy(i).wait_recv()
    e_copy.wait()

    def spectrum(a, b, i, at, depth):
        re = jnp.concatenate([a[i, 0], b[i, 0]], axis=0)
        im = jnp.concatenate([a[i, 1], b[i, 1]], axis=0)
        for half_p, parts in enumerate(butterflies(re, im, tw)):
            for j, pieces in enumerate(parts):
                for half, w in enumerate(pieces):
                    hi, lo = split(w)
                    for k, x in enumerate((hi, lo, hi)):
                        at_k = 512 * k + 256 * half
                        spread[half_p, 64 * j : 64 * j + 64, at_k : at_k + 256] = x
        even, uneven = (dot(spread[k], table[k]) for k in range(2))
        early = lax.broadcasted_iota(jnp.int32, (64, 128), 1) < 64
        for j in range(4):
            for b4 in range(4):
                first, second = (even, uneven) if b4 % 2 == 0 else (uneven, even)
                rows = slice(64 * j, 64 * j + 64)
                c0 = 128 * (b4 // 2)
                u = jnp.where(early, first[rows, c0 : c0 + 128], second[rows, c0 : c0 + 128])
                v = jnp.where(early, first[rows, 256 + c0 : 384 + c0], second[rows, 256 + c0 : 384 + c0])
                e0 = 512 * b4 + 128 * j
                c, w = (
                    jnp.concatenate([e_own[part, :, e0 : e0 + 128], e_other[part, :, e0 : e0 + 128]], axis=0)
                    for part in range(2)
                )
                for half, value in enumerate((u * c - v * w, u * w + v * c)):
                    hi, lo = split(value)
                    for k, x in enumerate((hi, lo, hi)):
                        spec[b4, pl.ds(k * depth + at + 64 * half, 64), 128 * j : 128 * j + 128] = x

    def block_at(dg, dh):
        return 2 * lax.rem(g + dg, 2) + lax.rem(h + dh, 2)

    def near_copy(ii):
        return remote(near.at[1, ii], near_in.at[ii], near_s.at[ii], near_r.at[ii], core)

    def dest_rows(n):
        return pl.ds(pl.multiple_of(64 * (3 - block_of(n)), 64), 64)

    def row_copy(dg, i):
        at, ii = dest_rows(lax.rem(i, 4)), i // 4
        return remote(side.at[dg, ii, at], side_in.at[dg, ii, at], row_s.at[dg, i], row_r.at[dg, i], peer(dg, 0, 1))

    def opp_copy(dg, i, to):
        return remote(opp.at[i, dg], relay_in.at[i, dg], rel_s.at[i, dg], rel_r.at[i, dg], to)

    def opp_cross(dg, i):
        return opp_copy(dg, i, peer(0, 1, 1))

    def opp_direct(dg, i):
        return opp_copy(dg, i, peer(0, 0, 1))

    def cross_copy(dg, i):
        return remote(cross.at[dg, i], cross_in.at[dg, i], crs_s.at[dg, i], crs_r.at[dg, i], peer(dg, 1, 1))

    def own_rows(ii):
        def one(n, carry):
            @pl.when(jnp.logical_and(ii == 0, n == 1))
            def _():
                a_copy(2).start()
                b_copy(2).start()

            @pl.when(jnp.logical_and(ii == 0, n == 3))
            def _():
                pass_on(2, (0, 1))
                a_copy(3).start()
                b_copy(3).start()

            spectrum(keep, other, 4 * ii + n, pl.multiple_of(128 * n, 128), 512)
            return carry

        lax.fori_loop(0, 4, one, 0)
        for dh in (1, 0):
            for dg in range(2):
                total = dot(ww[...], spec[block_at(dg, dh)])
                if dh == 0:
                    near[dg, ii] = total[0:256]
                else:
                    side[dg, ii] = total[0:256]
                    row_copy(dg, 4 * ii + 1).start()

                    @pl.when(ii == 0)
                    def _():
                        row_copy(dg, 3).start()

                pp[2 * dg + dh, ii] = total[256:512]
        near_copy(ii).start()

    def collect(i):
        n, ii = lax.rem(i, 4), i // 4
        at = dest_rows(n)
        for dg in range(2):
            cross_copy(dg, i).wait()
        parts = [
            near[0, ii, at, :] + side_in[0, ii, at, :] + cross_in[0, i],
            near_in[ii, at, :] + side_in[1, ii, at, :] + cross_in[1, i],
        ]
        got = dot(jnp.concatenate(split(jnp.concatenate(parts, axis=0)), axis=0), perm[h])
        rows = got[0:128] + got[128:256]
        for dg in range(2):
            row = 4 * (3 - block_of(n)) + 2 * lax.rem(g + dg, 2) + ii
            for c in range(4):
                for part in range(2):
                    at = 64 * dg + 32 * part
                    flat[c, part, pl.ds(row, 32, stride=16), :] = rows[at : at + 32, 128 * c : 128 * c + 128]

    def relay(i):
        n, ii = lax.rem(i, 4), i // 4

        @pl.when(lax.rem(i, 2) == 0)
        def _():
            at = dest_rows(n)
            for dg in range(2):
                opp_cross(dg, i).wait()
                side[dg, ii, at, :] = side[dg, ii, at, :] + relay_in[i, dg]
                row_copy(dg, i).start()

        @pl.when(lax.rem(i, 2) == 1)
        def _():
            for dg in range(2):
                opp_direct(dg, i).wait()
                cross[dg, i] = cross[dg, i] + relay_in[i, dg]
                cross_copy(dg, i).start()

    def step(i, carry):
        n, ii = lax.rem(i, 4), i // 4

        @pl.when(i == 1)
        def _():
            a_copy(5).start()
            b_copy(5).start()

        @pl.when(i == 2)
        def _():
            pass_on(3, (0, 1))
            a_copy(6).start()
            b_copy(6).start()

        @pl.when(i == 3)
        def _():
            a_copy(7).start()
            b_copy(7).start()

        @pl.when(i < 2)
        def _():
            own_rows(i)

        a_copy(i).wait_recv()
        b_copy(i).wait_recv()

        spectrum(halo_a, halo_b, i, 0, 128)
        mine = pl.ds(pl.multiple_of(64 * n, 64), 64)
        for dh in range(2):
            for dg in range(2):
                total = dot(wh[n], spec[block_at(dg, dh), 0:384, :])
                pp[2 * dg + dh, ii] = pp[2 * dg + dh, ii] + total
                if dh == 1:
                    cross[dg, i] = pp[2 * dg + 1, ii, mine, :]
                    continue
                opp[i, dg] = pp[2 * dg, ii, mine, :]

                @pl.when(lax.rem(i, 2) == 0)
                def _():
                    opp_cross(dg, i).start()

                @pl.when(lax.rem(i, 2) == 1)
                def _():
                    opp_direct(dg, i).start()

        @pl.when(lax.rem(i, 2) == 0)
        def _():
            for dg in range(2):
                cross_copy(dg, i).start()

        @pl.when(i >= 1)
        def _():
            relay(i - 1)

        @pl.when(i == 3)
        def _():
            for dg in range(2):
                row_copy(dg, 7).start()

        @pl.when(i >= 4)
        def _():
            @pl.when(i == 4)
            def _():
                near_copy(0).wait()

            for dg in range(2):
                row_copy(dg, i - 4).wait()
            collect(i - 4)

        return carry

    lax.fori_loop(0, 8, step, 0)
    near_copy(1).wait()

    def last(i, carry):
        for dg in range(2):
            row_copy(dg, i).wait()
        collect(i)
        return carry

    lax.fori_loop(4, 6, last, 0)
    relay(7)
    lax.fori_loop(6, 8, last, 0)
    results = [
        pltpu.make_async_copy(flat.at[c], out.at[:, :, pl.ds(128 * c, 128)], load_sem.at[c]) for c in range(4)
    ]
    for c in results:
        c.start()
    for i in range(8):
        snd_copy(i).wait_send()
        if i != 4:
            a_copy(i).wait_send()
        if i != 4:
            b_copy(i).wait_send()
    for hops in range(1, 4):
        for slot in range(2):
            via_copy(hops, slot).wait_send()
    for c in results:
        c.wait()


def local(strips, field, spectral_phase, chirp_shift, tile_map, tile_phase):
    waves, tw = dft_tables()
    vmem = pl.BlockSpec(memory_space=pltpu.VMEM)
    hbm = pl.BlockSpec(memory_space=pl.ANY)
    rows = pltpu.VMEM((8, 2, 32, 1024), F32)
    small = pltpu.VMEM((16, 128), F32)
    phase = pltpu.VMEM((2, 32, NY), F32)
    sums = pltpu.VMEM((2, 2, 256, 512), F32)
    dma = pltpu.SemaphoreType.DMA
    out = pl.pallas_call(
        functools.partial(kernel, strips),
        in_specs=[hbm, hbm, hbm, hbm, vmem, vmem, pl.BlockSpec(memory_space=pltpu.SMEM)],
        out_specs=pl.BlockSpec(memory_space=pl.ANY),
        out_shape=jax.ShapeDtypeStruct((2, 512, 512), F32),
        scratch_shapes=[
            pltpu.VMEM((8, 2, 512, 128), F32),
            rows, rows, rows, rows, rows,
            small, small, small, small,
            pltpu.VMEM((32, NY), F32),
            pltpu.VMEM(waves.shape, F32),
            pltpu.VMEM(tw.shape, F32),
            phase, phase,
            pltpu.VMEM((2, 1536, 512), BF),
            pltpu.VMEM((2, 512, 512), BF),
            pltpu.VMEM((512, 1536), BF),
            pltpu.VMEM((4, 256, 384), BF),
            pltpu.VMEM((2, 256, 1536), BF),
            pltpu.VMEM((4, 1536, 512), BF),
            sums,
            pltpu.VMEM((2, 256, 512), F32),
            sums, sums,
            pltpu.VMEM((4, 2, 256, 512), F32),
            pltpu.VMEM((8, 2, 64, 512), F32),
            pltpu.VMEM((8, 2, 64, 512), F32),
            pltpu.VMEM((2, 8, 64, 512), F32),
            pltpu.VMEM((2, 8, 64, 512), F32),
            pltpu.VMEM((2, 2, 32, 1024), F32),
            pltpu.VMEM((2, 2, 32, 1024), F32),
            dma((11,)),
            *[dma((8,))] * 6,
            dma((3,)), dma((3,)),
            dma((2,)), dma((2,)),
            dma((2, 8)), dma((2, 8)),
            dma((8, 2)), dma((8, 2)),
            dma((2, 8)), dma((2, 8)),
            *[dma((2,))] * 4,
        ],
        compiler_params=pltpu.CompilerParams(
            collective_id=0, has_side_effects=True, vmem_limit_bytes=VMEM * 2**20
        ),
        cost_estimate=pl.CostEstimate(flops=40 * 10**9, bytes_accessed=10 * 2**20, transcendentals=0),
    )(
        field.reshape(2, 512, 1024), spectral_phase, jnp.asarray(waves), jnp.asarray(tw),
        chirp_shift.reshape(1, 32), tile_phase, tile_map,
    )
    return out.reshape(2, NT, 16, 512)


def solution(mesh):
    placed = (P(None, "freq", "xs", "yh"), P("freq", None), P("freq"), P("xs"), P(None, "freq"))
    return jax.shard_map(
        functools.partial(local, mesh.shape["xs"]),
        mesh=mesh,
        in_specs=placed,
        out_specs=P(None, None, "xs", ("freq", "yh")),
        check_vma=False,
    )
```

```python
import functools
import math

import jax
import jax.numpy as jnp
import numpy as np
from jax import lax
from jax.experimental import pallas as pl
from jax.experimental.pallas import tpu as pltpu
from jax.sharding import PartitionSpec as P

NF = 64
NY = 2048
NT = 32
VMEM = 60
BF = jnp.bfloat16
F32 = jnp.float32
AXES = ("freq", "xs", "yh")
MESH = pl.DeviceIdType.MESH


def dft_tables():
    m = np.arange(256)
    angle = 2.0 * np.pi * (np.outer(m, m) % 256) / 256
    waves = np.stack([np.cos(angle), np.sin(angle)]) / math.sqrt(NY)
    odd_order = np.concatenate([np.arange(64) + 64 * b for b in (1, 0, 3, 2)])
    turn = 2.0 * np.pi * np.outer(np.arange(8), m) / NY
    twiddle = np.stack([np.cos(turn), np.sin(turn)])
    return np.stack([waves, waves[:, :, odd_order]]).astype(np.float32), twiddle.astype(np.float32)


def split(value):
    high = value.astype(BF)
    return high, (value - high.astype(F32)).astype(BF)


def dot(a, b):
    return jnp.dot(a, b, preferred_element_type=F32)


def dot_t(a, b):
    return lax.dot_general(a, b, (((1,), (1,)), ((), ())), preferred_element_type=F32)


def sincos(x):
    k = jnp.floor(x * (2.0 / math.pi) + 0.5)
    r = ((x - k * 1.5703125) - k * 4.837512969970703125e-4) - k * 7.54978995489188216e-8
    z = r * r
    sine = r + r * z * (-1.6666654611e-1 + z * (8.3321608736e-3 - z * 1.9515295891e-4))
    cosine = (1.0 - 0.5 * z) + z * z * (4.166664568298827e-2 + z * (-1.388731625493765e-3 + z * 2.443315711809948e-5))
    half = jnp.floor(k * 0.5)
    swap = (k - 2.0 * half) > 0.5
    sign = 1.0 - 2.0 * (half - 2.0 * jnp.floor(half * 0.5))
    return sign * jnp.where(swap, cosine, sine), sign * jnp.where(swap, -sine, cosine)


def butterflies(re, im, tw):
    a = [(re[:, 256 * c : 256 * c + 256], im[:, 256 * c : 256 * c + 256]) for c in range(4)]
    r = math.sqrt(0.5)

    def add(u, v):
        return u[0] + v[0], u[1] + v[1]

    def sub(u, v):
        return u[0] - v[0], u[1] - v[1]

    def mi(u):
        return u[1], -u[0]

    def four(b):
        e0, e1 = add(b[0], b[2]), sub(b[0], b[2])
        e2, e3 = add(b[1], b[3]), mi(sub(b[1], b[3]))
        return add(e0, e2), add(e1, e3), sub(e0, e2), sub(e1, e3)

    even = four(a)
    b1 = ((a[1][0] + a[1][1]) * r, (a[1][1] - a[1][0]) * r)
    b3 = ((a[3][1] - a[3][0]) * r, (-a[3][0] - a[3][1]) * r)
    odd = four((a[0], b1, mi(a[2]), b3))
    both = []
    for side, parts in enumerate((even, odd)):
        row = []
        for j in range(4):
            p = 2 * j + side
            u = parts[j]
            if p:
                c, s = tw[0, p : p + 1, :], tw[1, p : p + 1, :]
                u = u[0] * c + u[1] * s, u[1] * c - u[0] * s
            row.append(u)
        both.append(row)
    return both


def kernel(
    strips, field, phi_hbm, waves_hbm, tw_hbm, shift_row, tile_phase, tile_ids, out,
    flat, snd, keep, other, halo_a, halo_b, prm, prm_out, prm_in, prm_pair,
    phi, waves, tw, e_own, e_other, table, perm, ww, wh,
    spread, spec, near, near_in, side, side_in, pp, opp, relay_in, cross, cross_in, via_1, via_2, *rest,
):
    (load_sem, snd_s, snd_r, ha_s, ha_r, hb_s, hb_r, prm_s, prm_r,
     near_s, near_r, row_s, row_r, rel_s, rel_r, crs_s, crs_r, v1_s, v1_r, v2_s, v2_r) = rest
    g, s, h = (lax.axis_index(a) for a in AXES)
    odd = lax.rem(s, 2)
    pair = s + 1 - 2 * odd
    onward = lax.rem(s + strips + 4 * odd - 2, strips)
    back = lax.rem(s + strips + 2 - 4 * odd, strips)
    core = (1 - g, s, h)

    z, y, turns = s // 8, lax.rem(s // 2, 4), strips // 8
    hop = 1 - 2 * odd
    across = 8 * z + 2 * lax.rem(y + 4 + hop, 4) + odd
    across_from = 8 * z + 2 * lax.rem(y + 4 - hop, 4) + odd
    z_on = 8 * lax.rem(z + turns - hop, turns) + odd
    z_back = 8 * lax.rem(z + turns + hop, turns) + odd
    leaves = (y == 2 - odd).astype(jnp.int32)
    third = across + leaves * (z_on + 2 * (3 - 3 * odd) - across)
    enters = (y == 3 - 3 * odd).astype(jnp.int32)
    third_from = across_from + enters * (z_back + 2 * (2 - odd) - across_from)

    def peer(dg, ds, dh):
        return (lax.rem(g + dg, 2), pair if ds else s, lax.rem(h + dh, 2))

    def remote(src, dst, a, b, to):
        return pltpu.make_async_remote_copy(
            src_ref=src, dst_ref=dst, send_sem=a, recv_sem=b, device_id=to, device_id_type=MESH
        )

    def block_of(n):
        return n + odd * (3 - 2 * n)

    loads = [
        pltpu.make_async_copy(field.at[:, :, pl.ds(128 * y, 128)], flat.at[y], load_sem.at[y]) for y in range(8)
    ]
    tables = [
        pltpu.make_async_copy(src, dst, load_sem.at[8 + k])
        for k, (src, dst) in enumerate(((waves_hbm, waves), (tw_hbm, tw), (phi_hbm, phi)))
    ]
    for c in loads + tables:
        c.start()
    barrier = pltpu.get_barrier_semaphore()
    greet = [core, peer(0, 0, 1), peer(1, 0, 1), peer(0, 1, 1), peer(1, 1, 1), (g, onward, h), (g, back, h)]
    greet += [(g, across, h), (g, across_from, h), (g, third, h), (g, third_from, h)]
    for to in greet:
        pl.semaphore_signal(barrier, inc=1, device_id=to, device_id_type=MESH)

    def snd_copy(i):
        return remote(snd.at[i], other.at[i], snd_s.at[i], snd_r.at[i], core)

    def a_copy(i):
        return remote(keep.at[i], halo_a.at[i], ha_s.at[i], ha_r.at[i], (g, onward, h))

    def b_copy(i):
        return remote(other.at[i], halo_b.at[i], hb_s.at[i], hb_r.at[i], (g, onward, h))

    def via_copy(hops, slot):
        which, i = ((0, 4), (1, 4))[slot]
        if hops == 1:
            src = (keep, other)[which].at[i]
            return remote(src, via_1.at[slot], v1_s.at[slot], v1_r.at[slot], (g, across, h))
        if hops == 2:
            return remote(via_1.at[slot], via_2.at[slot], v2_s.at[slot], v2_r.at[slot], (g, across, h))
        dst, sems = ((halo_a, (ha_s, ha_r)), (halo_b, (hb_s, hb_r)))[which]
        return remote(via_2.at[slot], dst.at[i], sems[0].at[i], sems[1].at[i], (g, third, h))

    def pass_on(hops, slots):
        for slot in slots:
            via_copy(hops - 1, slot).wait_recv()
            via_copy(hops, slot).start()

    def gather_rows(i, whose, into):
        row = 4 * block_of(lax.rem(i, 4)) + 2 * whose + i // 4
        for c in range(2):
            for y in range(8):
                into[i, c, :, 128 * y : 128 * y + 128] = flat[y, c, pl.ds(row, 32, stride=16), :]

    gap = jnp.zeros((8, 32), F32)
    rows = jnp.concatenate([shift_row[...].astype(F32), tile_phase[...], jnp.zeros((3, 32), F32)], axis=0)
    prm[0:8, :] = jnp.concatenate([rows, gap, rows, gap], axis=1)
    for rb in range(4):
        prm[8 + rb : 9 + rb, :] = jnp.full((1, 128), tile_ids[rb], jnp.int32).astype(F32)
    prm[12:16, :] = jnp.zeros((4, 128), F32)
    prm_out[...] = pltpu.roll(prm[...], 32, 1)
    prm_core = remote(prm_out, prm_in, prm_s.at[0], prm_r.at[0], core)
    prm_strip = remote(prm, prm_pair, prm_s.at[1], prm_r.at[1], peer(0, 1, 1))

    for c in loads:
        c.wait()

    def pack_send(i, carry):
        gather_rows(i, 1 - g, snd)
        snd_copy(i).start()
        return carry

    def pack_keep(i, carry):
        gather_rows(i, g, keep)
        return carry

    for i in (0, 4, 1):
        gather_rows(i, g, keep)
    pl.semaphore_wait(barrier, len(greet))
    a_copy(0).start()
    via_copy(1, 0).start()
    a_copy(1).start()
    lax.fori_loop(0, 5, pack_send, 0)
    prm_core.start()
    prm_strip.start()
    lax.fori_loop(2, 4, pack_keep, 0)
    for i in (0, 4, 1):
        snd_copy(i).wait_recv()
        if i == 4:
            via_copy(1, 1).start()
        else:
            b_copy(i).start()

    for c in tables:
        c.wait()
    lane = lax.broadcasted_iota(jnp.int32, (512, 1), 0)
    wave = lax.broadcasted_iota(jnp.int32, (1, 512), 1)
    turn = lax.rem(lane, 128)
    for half in range(2):
        late = (turn >= 64).astype(jnp.int32)
        late = late if half == 0 else 1 - late
        target = 8 * lax.rem(turn, 64) + 2 * (lane // 128) + late
        perm[half] = jnp.where(target == wave, 1.0, 0.0).astype(BF)
        c_hi, c_lo = split(waves[half, 0])
        s_hi, s_lo = split(waves[half, 1])
        for k, (c, w) in enumerate(((c_hi, s_hi), (c_hi, s_hi), (c_lo, s_lo))):
            table[half, 512 * k : 512 * k + 256, 0:256] = c
            table[half, 512 * k : 512 * k + 256, 256:512] = -w
            table[half, 512 * k + 256 : 512 * k + 512, 0:256] = w
            table[half, 512 * k + 256 : 512 * k + 512, 256:512] = c

    lanes = lax.rem(lax.broadcasted_iota(jnp.int32, (1, 512), 1), 128)
    for half in range(2):
        late = lanes >= 64 if half == 0 else lanes < 64
        sign = 1.0 - 2.0 * jnp.where(late, h, 0).astype(F32)
        stack = []
        for b in (half, half + 2):
            sine, cosine = sincos(phi[:, 512 * b : 512 * b + 512])
            stack += [*split(cosine), *split(sine)]
        got = dot_t(jnp.concatenate(stack, axis=0), perm[half])
        for k, b in enumerate((half, half + 2)):
            for part in range(2):
                at = 128 * k + 64 * part
                e_own[part, :, 512 * b : 512 * b + 512] = (got[at : at + 32] + got[at + 32 : at + 64]) * sign
    e_copy = remote(e_own, e_other, prm_s.at[2], prm_r.at[2], core)
    e_copy.start()

    prm_core.wait()
    prm_strip.wait()
    both = prm[...] + prm_in[...]
    shift = both[0:1, :]
    col = lax.broadcasted_iota(jnp.int32, (NT, 128), 1)
    freq = lax.rem(lax.rem(col, 64) + 32 * g, NF)
    angle = (2.0 * math.pi / NF) * lax.rem(lax.broadcasted_iota(jnp.int32, (NT, 128), 0) * freq, NF).astype(F32)
    scale = 1.0 / math.sqrt(NF)
    real_in = col < 64

    def base(tile):
        phase = jnp.zeros((1, 128), F32)
        for t in range(4):
            phase = phase + jnp.where(tile == float(t), both[1 + t : 2 + t, :], 0.0)
        im, re = sincos(angle + phase)
        im, re = im * scale, re * scale
        return jnp.concatenate([jnp.where(real_in, re, -im), jnp.where(real_in, im, re)], axis=0)

    far = (4 * (1 - 2 * odd)).astype(F32)
    inside = jnp.where(odd == 1, (s > 1).astype(F32), (s < strips - 2).astype(F32))
    for nd in range(4):
        dest = block_of(nd)
        here, there = base(prm[8 + nd : 9 + nd, :]), base(prm_pair[pl.ds(8 + dest, 1), :])
        rows = slice(64 * nd, 64 * nd + 64)
        for n in range(4):
            source = block_of(n)
            own_hi, own_lo = split(jnp.where(shift == (nd - source).astype(F32), here, 0.0))
            step = (dest - source).astype(F32)
            pair_hi, pair_lo = split(jnp.where(shift == step + far, there, 0.0))
            halo_hi, halo_lo = split(jnp.where(shift == step - far, there * inside, 0.0))
            below = slice(256 + 64 * nd, 320 + 64 * nd)
            for k, (u, v, w) in enumerate(
                ((own_hi, pair_hi, halo_hi), (own_hi, pair_hi, halo_hi), (own_lo, pair_lo, halo_lo))
            ):
                at = 512 * k + 128 * n
                ww[rows, at : at + 128] = u
                ww[below, at : at + 128] = v
                wh[n, rows, 128 * k : 128 * k + 128] = w
    for i in (2, 3):
        snd_copy(i).wait_recv()
    e_copy.wait()

    def spectrum(a, b, i, at, depth):
        re = jnp.concatenate([a[i, 0], b[i, 0]], axis=0)
        im = jnp.concatenate([a[i, 1], b[i, 1]], axis=0)
        for half_p, parts in enumerate(butterflies(re, im, tw)):
            for j, pieces in enumerate(parts):
                for half, w in enumerate(pieces):
                    hi, lo = split(w)
                    for k, x in enumerate((hi, lo, hi)):
                        at_k = 512 * k + 256 * half
                        spread[half_p, 64 * j : 64 * j + 64, at_k : at_k + 256] = x
        even, uneven = (dot(spread[k], table[k]) for k in range(2))
        early = lax.broadcasted_iota(jnp.int32, (64, 128), 1) < 64
        for j in range(4):
            for b4 in range(4):
                first, second = (even, uneven) if b4 % 2 == 0 else (uneven, even)
                rows = slice(64 * j, 64 * j + 64)
                c0 = 128 * (b4 // 2)
                u = jnp.where(early, first[rows, c0 : c0 + 128], second[rows, c0 : c0 + 128])
                v = jnp.where(early, first[rows, 256 + c0 : 384 + c0], second[rows, 256 + c0 : 384 + c0])
                e0 = 512 * b4 + 128 * j
                c, w = (
                    jnp.concatenate([e_own[part, :, e0 : e0 + 128], e_other[part, :, e0 : e0 + 128]], axis=0)
                    for part in range(2)
                )
                for half, value in enumerate((u * c - v * w, u * w + v * c)):
                    hi, lo = split(value)
                    for k, x in enumerate((hi, lo, hi)):
                        spec[b4, pl.ds(k * depth + at + 64 * half, 64), 128 * j : 128 * j + 128] = x

    def block_at(dg, dh):
        return 2 * lax.rem(g + dg, 2) + lax.rem(h + dh, 2)

    def near_copy(ii):
        return remote(near.at[1, ii], near_in.at[ii], near_s.at[ii], near_r.at[ii], core)

    def dest_rows(n):
        return pl.ds(pl.multiple_of(64 * (3 - block_of(n)), 64), 64)

    def row_copy(dg, i):
        at, ii = dest_rows(lax.rem(i, 4)), i // 4
        return remote(side.at[dg, ii, at], side_in.at[dg, ii, at], row_s.at[dg, i], row_r.at[dg, i], peer(dg, 0, 1))

    def opp_copy(dg, i, to):
        return remote(opp.at[i, dg], relay_in.at[i, dg], rel_s.at[i, dg], rel_r.at[i, dg], to)

    def opp_cross(dg, i):
        return opp_copy(dg, i, peer(0, 1, 1))

    def opp_direct(dg, i):
        return opp_copy(dg, i, peer(0, 0, 1))

    def cross_copy(dg, i):
        return remote(cross.at[dg, i], cross_in.at[dg, i], crs_s.at[dg, i], crs_r.at[dg, i], peer(dg, 1, 1))

    def own_rows(ii):
        def one(n, carry):
            @pl.when(jnp.logical_and(ii == 0, n == 1))
            def _():
                a_copy(2).start()
                b_copy(2).start()

            @pl.when(jnp.logical_and(ii == 0, n == 3))
            def _():
                pass_on(2, (0, 1))
                a_copy(3).start()
                b_copy(3).start()

            spectrum(keep, other, 4 * ii + n, pl.multiple_of(128 * n, 128), 512)
            return carry

        lax.fori_loop(0, 4, one, 0)
        for dh in (1, 0):
            for dg in range(2):
                total = dot(ww[...], spec[block_at(dg, dh)])
                if dh == 0:
                    near[dg, ii] = total[0:256]
                else:
                    side[dg, ii] = total[0:256]
                    row_copy(dg, 4 * ii + 1).start()

                    @pl.when(ii == 0)
                    def _():
                        row_copy(dg, 3).start()

                pp[2 * dg + dh, ii] = total[256:512]
        near_copy(ii).start()

    def collect(i):
        n, ii = lax.rem(i, 4), i // 4
        at = dest_rows(n)
        for dg in range(2):
            cross_copy(dg, i).wait()
        parts = [
            near[0, ii, at, :] + side_in[0, ii, at, :] + cross_in[0, i],
            near_in[ii, at, :] + side_in[1, ii, at, :] + cross_in[1, i],
        ]
        got = dot(jnp.concatenate(split(jnp.concatenate(parts, axis=0)), axis=0), perm[h])
        rows = got[0:128] + got[128:256]
        for dg in range(2):
            row = 4 * (3 - block_of(n)) + 2 * lax.rem(g + dg, 2) + ii
            for c in range(4):
                for part in range(2):
                    at = 64 * dg + 32 * part
                    flat[c, part, pl.ds(row, 32, stride=16), :] = rows[at : at + 32, 128 * c : 128 * c + 128]

    def relay(i):
        n, ii = lax.rem(i, 4), i // 4

        @pl.when(lax.rem(i, 2) == 0)
        def _():
            at = dest_rows(n)
            for dg in range(2):
                opp_cross(dg, i).wait()
                side[dg, ii, at, :] = side[dg, ii, at, :] + relay_in[i, dg]
                row_copy(dg, i).start()

        @pl.when(lax.rem(i, 2) == 1)
        def _():
            for dg in range(2):
                opp_direct(dg, i).wait()
                cross[dg, i] = cross[dg, i] + relay_in[i, dg]
                cross_copy(dg, i).start()

    def step(i, carry):
        n, ii = lax.rem(i, 4), i // 4

        @pl.when(i == 1)
        def _():
            lax.fori_loop(5, 8, pack_send, 0)
            lax.fori_loop(5, 8, pack_keep, 0)
            a_copy(5).start()
            for late in range(5, 8):
                snd_copy(late).wait_recv()
            b_copy(5).start()

        @pl.when(i == 2)
        def _():
            pass_on(3, (0, 1))
            a_copy(6).start()
            b_copy(6).start()

        @pl.when(i == 3)
        def _():
            a_copy(7).start()
            b_copy(7).start()

        @pl.when(i < 2)
        def _():
            own_rows(i)

        a_copy(i).wait_recv()
        b_copy(i).wait_recv()

        spectrum(halo_a, halo_b, i, 0, 128)
        mine = pl.ds(pl.multiple_of(64 * n, 64), 64)
        for dh in range(2):
            for dg in range(2):
                total = dot(wh[n], spec[block_at(dg, dh), 0:384, :])
                pp[2 * dg + dh, ii] = pp[2 * dg + dh, ii] + total
                if dh == 1:
                    cross[dg, i] = pp[2 * dg + 1, ii, mine, :]
                    continue
                opp[i, dg] = pp[2 * dg, ii, mine, :]

                @pl.when(lax.rem(i, 2) == 0)
                def _():
                    opp_cross(dg, i).start()

                @pl.when(lax.rem(i, 2) == 1)
                def _():
                    opp_direct(dg, i).start()

        @pl.when(lax.rem(i, 2) == 0)
        def _():
            for dg in range(2):
                cross_copy(dg, i).start()

        @pl.when(i >= 1)
        def _():
            relay(i - 1)

        @pl.when(i == 3)
        def _():
            for dg in range(2):
                row_copy(dg, 7).start()

        @pl.when(i >= 4)
        def _():
            @pl.when(i == 4)
            def _():
                near_copy(0).wait()

            for dg in range(2):
                row_copy(dg, i - 4).wait()
            collect(i - 4)

        return carry

    lax.fori_loop(0, 8, step, 0)
    near_copy(1).wait()

    def last(i, carry):
        for dg in range(2):
            row_copy(dg, i).wait()
        collect(i)
        return carry

    lax.fori_loop(4, 6, last, 0)
    relay(7)
    lax.fori_loop(6, 8, last, 0)
    results = [
        pltpu.make_async_copy(flat.at[c], out.at[:, :, pl.ds(128 * c, 128)], load_sem.at[c]) for c in range(4)
    ]
    for c in results:
        c.start()
    for i in range(8):
        snd_copy(i).wait_send()
        if i != 4:
            a_copy(i).wait_send()
        if i != 4:
            b_copy(i).wait_send()
    for hops in range(1, 4):
        for slot in range(2):
            via_copy(hops, slot).wait_send()
    for c in results:
        c.wait()


def local(strips, field, spectral_phase, chirp_shift, tile_map, tile_phase):
    waves, tw = dft_tables()
    vmem = pl.BlockSpec(memory_space=pltpu.VMEM)
    hbm = pl.BlockSpec(memory_space=pl.ANY)
    rows = pltpu.VMEM((8, 2, 32, 1024), F32)
    small = pltpu.VMEM((16, 128), F32)
    phase = pltpu.VMEM((2, 32, NY), F32)
    sums = pltpu.VMEM((2, 2, 256, 512), F32)
    dma = pltpu.SemaphoreType.DMA
    out = pl.pallas_call(
        functools.partial(kernel, strips),
        in_specs=[hbm, hbm, hbm, hbm, vmem, vmem, pl.BlockSpec(memory_space=pltpu.SMEM)],
        out_specs=pl.BlockSpec(memory_space=pl.ANY),
        out_shape=jax.ShapeDtypeStruct((2, 512, 512), F32),
        scratch_shapes=[
            pltpu.VMEM((8, 2, 512, 128), F32),
            rows, rows, rows, rows, rows,
            small, small, small, small,
            pltpu.VMEM((32, NY), F32),
            pltpu.VMEM(waves.shape, F32),
            pltpu.VMEM(tw.shape, F32),
            phase, phase,
            pltpu.VMEM((2, 1536, 512), BF),
            pltpu.VMEM((2, 512, 512), BF),
            pltpu.VMEM((512, 1536), BF),
            pltpu.VMEM((4, 256, 384), BF),
            pltpu.VMEM((2, 256, 1536), BF),
            pltpu.VMEM((4, 1536, 512), BF),
            sums,
            pltpu.VMEM((2, 256, 512), F32),
            sums, sums,
            pltpu.VMEM((4, 2, 256, 512), F32),
            pltpu.VMEM((8, 2, 64, 512), F32),
            pltpu.VMEM((8, 2, 64, 512), F32),
            pltpu.VMEM((2, 8, 64, 512), F32),
            pltpu.VMEM((2, 8, 64, 512), F32),
            pltpu.VMEM((2, 2, 32, 1024), F32),
            pltpu.VMEM((2, 2, 32, 1024), F32),
            dma((11,)),
            *[dma((8,))] * 6,
            dma((3,)), dma((3,)),
            dma((2,)), dma((2,)),
            dma((2, 8)), dma((2, 8)),
            dma((8, 2)), dma((8, 2)),
            dma((2, 8)), dma((2, 8)),
            *[dma((2,))] * 4,
        ],
        compiler_params=pltpu.CompilerParams(
            collective_id=0, has_side_effects=True, vmem_limit_bytes=VMEM * 2**20
        ),
        cost_estimate=pl.CostEstimate(flops=40 * 10**9, bytes_accessed=10 * 2**20, transcendentals=0),
    )(
        field.reshape(2, 512, 1024), spectral_phase, jnp.asarray(waves), jnp.asarray(tw),
        chirp_shift.reshape(1, 32), tile_phase, tile_map,
    )
    return out.reshape(2, NT, 16, 512)


def solution(mesh):
    placed = (P(None, "freq", "xs", "yh"), P("freq", None), P("freq"), P("xs"), P(None, "freq"))
    return jax.shard_map(
        functools.partial(local, mesh.shape["xs"]),
        mesh=mesh,
        in_specs=placed,
        out_specs=P(None, None, "xs", ("freq", "yh")),
        check_vma=False,
    )
```

```python
import functools
import math

import jax
import jax.numpy as jnp
import numpy as np
from jax import lax
from jax.experimental import pallas as pl
from jax.experimental.pallas import tpu as pltpu
from jax.sharding import PartitionSpec as P

NF = 64
NY = 2048
NT = 32
VMEM = 60
BF = jnp.bfloat16
F32 = jnp.float32
AXES = ("freq", "xs", "yh")
MESH = pl.DeviceIdType.MESH


def dft_tables():
    m = np.arange(256)
    angle = 2.0 * np.pi * (np.outer(m, m) % 256) / 256
    waves = np.stack([np.cos(angle), np.sin(angle)]) / math.sqrt(NY)
    odd_order = np.concatenate([np.arange(64) + 64 * b for b in (1, 0, 3, 2)])
    turn = 2.0 * np.pi * np.outer(np.arange(8), m) / NY
    twiddle = np.stack([np.cos(turn), np.sin(turn)])
    return np.stack([waves, waves[:, :, odd_order]]).astype(np.float32), twiddle.astype(np.float32)


def split(value):
    high = value.astype(BF)
    return high, (value - high.astype(F32)).astype(BF)


def dot(a, b):
    return jnp.dot(a, b, preferred_element_type=F32)


def dot_t(a, b):
    return lax.dot_general(a, b, (((1,), (1,)), ((), ())), preferred_element_type=F32)


def sincos(x):
    k = jnp.floor(x * (2.0 / math.pi) + 0.5)
    r = ((x - k * 1.5703125) - k * 4.837512969970703125e-4) - k * 7.54978995489188216e-8
    z = r * r
    sine = r + r * z * (-1.6666654611e-1 + z * (8.3321608736e-3 - z * 1.9515295891e-4))
    cosine = (1.0 - 0.5 * z) + z * z * (4.166664568298827e-2 + z * (-1.388731625493765e-3 + z * 2.443315711809948e-5))
    half = jnp.floor(k * 0.5)
    swap = (k - 2.0 * half) > 0.5
    sign = 1.0 - 2.0 * (half - 2.0 * jnp.floor(half * 0.5))
    return sign * jnp.where(swap, cosine, sine), sign * jnp.where(swap, -sine, cosine)


def butterflies(re, im, tw):
    a = [(re[:, 256 * c : 256 * c + 256], im[:, 256 * c : 256 * c + 256]) for c in range(4)]
    r = math.sqrt(0.5)

    def add(u, v):
        return u[0] + v[0], u[1] + v[1]

    def sub(u, v):
        return u[0] - v[0], u[1] - v[1]

    def mi(u):
        return u[1], -u[0]

    def four(b):
        e0, e1 = add(b[0], b[2]), sub(b[0], b[2])
        e2, e3 = add(b[1], b[3]), mi(sub(b[1], b[3]))
        return add(e0, e2), add(e1, e3), sub(e0, e2), sub(e1, e3)

    even = four(a)
    b1 = ((a[1][0] + a[1][1]) * r, (a[1][1] - a[1][0]) * r)
    b3 = ((a[3][1] - a[3][0]) * r, (-a[3][0] - a[3][1]) * r)
    odd = four((a[0], b1, mi(a[2]), b3))
    both = []
    for side, parts in enumerate((even, odd)):
        row = []
        for j in range(4):
            p = 2 * j + side
            u = parts[j]
            if p:
                c, s = tw[0, p : p + 1, :], tw[1, p : p + 1, :]
                u = u[0] * c + u[1] * s, u[1] * c - u[0] * s
            row.append(u)
        both.append(row)
    return both


def kernel(
    strips, field, phi_hbm, waves_hbm, tw_hbm, shift_row, tile_phase, tile_ids, out,
    flat, snd, keep, other, halo_a, halo_b, prm, prm_out, prm_in, prm_pair,
    phi, waves, tw, e_own, e_other, table, perm, ww, wh,
    spread, spec, near, near_in, side, side_in, pp, opp, relay_in, cross, cross_in, via_1, via_2, *rest,
):
    (load_sem, snd_s, snd_r, ha_s, ha_r, hb_s, hb_r, prm_s, prm_r,
     near_s, near_r, row_s, row_r, rel_s, rel_r, crs_s, crs_r, v1_s, v1_r, v2_s, v2_r) = rest
    g, s, h = (lax.axis_index(a) for a in AXES)
    odd = lax.rem(s, 2)
    pair = s + 1 - 2 * odd
    onward = lax.rem(s + strips + 4 * odd - 2, strips)
    back = lax.rem(s + strips + 2 - 4 * odd, strips)
    core = (1 - g, s, h)

    z, y, turns = s // 8, lax.rem(s // 2, 4), strips // 8
    hop = 1 - 2 * odd
    across = 8 * z + 2 * lax.rem(y + 4 + hop, 4) + odd
    across_from = 8 * z + 2 * lax.rem(y + 4 - hop, 4) + odd
    z_on = 8 * lax.rem(z + turns - hop, turns) + odd
    z_back = 8 * lax.rem(z + turns + hop, turns) + odd
    leaves = (y == 2 - odd).astype(jnp.int32)
    third = across + leaves * (z_on + 2 * (3 - 3 * odd) - across)
    enters = (y == 3 - 3 * odd).astype(jnp.int32)
    third_from = across_from + enters * (z_back + 2 * (2 - odd) - across_from)

    def peer(dg, ds, dh):
        return (lax.rem(g + dg, 2), pair if ds else s, lax.rem(h + dh, 2))

    def remote(src, dst, a, b, to):
        return pltpu.make_async_remote_copy(
            src_ref=src, dst_ref=dst, send_sem=a, recv_sem=b, device_id=to, device_id_type=MESH
        )

    def block_of(n):
        return n + odd * (3 - 2 * n)

    loads = [
        pltpu.make_async_copy(field.at[:, :, pl.ds(128 * y, 128)], flat.at[y], load_sem.at[y]) for y in range(8)
    ]
    tables = [
        pltpu.make_async_copy(src, dst, load_sem.at[8 + k])
        for k, (src, dst) in enumerate(((waves_hbm, waves), (tw_hbm, tw), (phi_hbm, phi)))
    ]
    for c in loads + tables:
        c.start()
    barrier = pltpu.get_barrier_semaphore()
    greet = [core, peer(0, 0, 1), peer(1, 0, 1), peer(0, 1, 1), peer(1, 1, 1), (g, onward, h), (g, back, h)]
    greet += [(g, across, h), (g, across_from, h), (g, third, h), (g, third_from, h)]
    for to in greet:
        pl.semaphore_signal(barrier, inc=1, device_id=to, device_id_type=MESH)

    def snd_copy(i):
        return remote(snd.at[i], other.at[i], snd_s.at[i], snd_r.at[i], core)

    def a_copy(i):
        return remote(keep.at[i], halo_a.at[i], ha_s.at[i], ha_r.at[i], (g, onward, h))

    def b_copy(i):
        return remote(other.at[i], halo_b.at[i], hb_s.at[i], hb_r.at[i], (g, onward, h))

    def via_copy(hops, slot):
        which, i = ((0, 4), (1, 4))[slot]
        if hops == 1:
            src = (keep, other)[which].at[i]
            return remote(src, via_1.at[slot], v1_s.at[slot], v1_r.at[slot], (g, across, h))
        if hops == 2:
            return remote(via_1.at[slot], via_2.at[slot], v2_s.at[slot], v2_r.at[slot], (g, across, h))
        dst, sems = ((halo_a, (ha_s, ha_r)), (halo_b, (hb_s, hb_r)))[which]
        return remote(via_2.at[slot], dst.at[i], sems[0].at[i], sems[1].at[i], (g, third, h))

    def pass_on(hops, slots):
        for slot in slots:
            via_copy(hops - 1, slot).wait_recv()
            via_copy(hops, slot).start()

    def gather_rows(i, whose, into):
        row = 4 * block_of(lax.rem(i, 4)) + 2 * whose + i // 4
        for c in range(2):
            for y in range(8):
                into[i, c, :, 128 * y : 128 * y + 128] = flat[y, c, pl.ds(row, 32, stride=16), :]

    gap = jnp.zeros((8, 32), F32)
    rows = jnp.concatenate([shift_row[...].astype(F32), tile_phase[...], jnp.zeros((3, 32), F32)], axis=0)
    prm[0:8, :] = jnp.concatenate([rows, gap, rows, gap], axis=1)
    for rb in range(4):
        prm[8 + rb : 9 + rb, :] = jnp.full((1, 128), tile_ids[rb], jnp.int32).astype(F32)
    prm[12:16, :] = jnp.zeros((4, 128), F32)
    prm_out[...] = pltpu.roll(prm[...], 32, 1)
    prm_core = remote(prm_out, prm_in, prm_s.at[0], prm_r.at[0], core)
    prm_strip = remote(prm, prm_pair, prm_s.at[1], prm_r.at[1], peer(0, 1, 1))

    for c in loads:
        c.wait()

    def pack_send(i, carry):
        gather_rows(i, 1 - g, snd)
        snd_copy(i).start()
        return carry

    def pack_keep(i, carry):
        gather_rows(i, g, keep)
        return carry

    for i in (0, 4, 1):
        gather_rows(i, g, keep)
    pl.semaphore_wait(barrier, len(greet))
    a_copy(0).start()
    via_copy(1, 0).start()
    a_copy(1).start()
    lax.fori_loop(0, 8, pack_send, 0)
    prm_core.start()
    prm_strip.start()
    lax.fori_loop(2, 4, pack_keep, 0)
    lax.fori_loop(5, 8, pack_keep, 0)
    for i in (0, 4, 1):
        snd_copy(i).wait_recv()
        if i == 4:
            via_copy(1, 1).start()
        else:
            b_copy(i).start()

    for c in tables:
        c.wait()
    lane = lax.broadcasted_iota(jnp.int32, (512, 1), 0)
    wave = lax.broadcasted_iota(jnp.int32, (1, 512), 1)
    turn = lax.rem(lane, 128)
    for half in range(2):
        late = (turn >= 64).astype(jnp.int32)
        late = late if half == 0 else 1 - late
        target = 8 * lax.rem(turn, 64) + 2 * (lane // 128) + late
        perm[half] = jnp.where(target == wave, 1.0, 0.0).astype(BF)
        c_hi, c_lo = split(waves[half, 0])
        s_hi, s_lo = split(waves[half, 1])
        for k, (c, w) in enumerate(((c_hi, s_hi), (c_hi, s_hi), (c_lo, s_lo))):
            table[half, 512 * k : 512 * k + 256, 0:256] = c
            table[half, 512 * k : 512 * k + 256, 256:512] = -w
            table[half, 512 * k + 256 : 512 * k + 512, 0:256] = w
            table[half, 512 * k + 256 : 512 * k + 512, 256:512] = c

    lanes = lax.rem(lax.broadcasted_iota(jnp.int32, (1, 512), 1), 128)
    for half in range(2):
        late = lanes >= 64 if half == 0 else lanes < 64
        sign = 1.0 - 2.0 * jnp.where(late, h, 0).astype(F32)
        stack = []
        for b in (half, half + 2):
            sine, cosine = sincos(phi[:, 512 * b : 512 * b + 512])
            stack += [*split(cosine), *split(sine)]
        got = dot_t(jnp.concatenate(stack, axis=0), perm[half])
        for k, b in enumerate((half, half + 2)):
            for part in range(2):
                at = 128 * k + 64 * part
                e_own[part, :, 512 * b : 512 * b + 512] = (got[at : at + 32] + got[at + 32 : at + 64]) * sign
    e_copy = remote(e_own, e_other, prm_s.at[2], prm_r.at[2], core)
    e_copy.start()

    prm_core.wait()
    prm_strip.wait()
    both = prm[...] + prm_in[...]
    shift = both[0:1, :]
    col = lax.broadcasted_iota(jnp.int32, (NT, 128), 1)
    freq = lax.rem(lax.rem(col, 64) + 32 * g, NF)
    angle = (2.0 * math.pi / NF) * lax.rem(lax.broadcasted_iota(jnp.int32, (NT, 128), 0) * freq, NF).astype(F32)
    scale = 1.0 / math.sqrt(NF)
    real_in = col < 64

    def base(tile):
        phase = jnp.zeros((1, 128), F32)
        for t in range(4):
            phase = phase + jnp.where(tile == float(t), both[1 + t : 2 + t, :], 0.0)
        im, re = sincos(angle + phase)
        im, re = im * scale, re * scale
        return jnp.concatenate([jnp.where(real_in, re, -im), jnp.where(real_in, im, re)], axis=0)

    far = (4 * (1 - 2 * odd)).astype(F32)
    inside = jnp.where(odd == 1, (s > 1).astype(F32), (s < strips - 2).astype(F32))
    for nd in range(4):
        dest = block_of(nd)
        here, there = base(prm[8 + nd : 9 + nd, :]), base(prm_pair[pl.ds(8 + dest, 1), :])
        rows = slice(64 * nd, 64 * nd + 64)
        for n in range(4):
            source = block_of(n)
            own_hi, own_lo = split(jnp.where(shift == (nd - source).astype(F32), here, 0.0))
            step = (dest - source).astype(F32)
            pair_hi, pair_lo = split(jnp.where(shift == step + far, there, 0.0))
            halo_hi, halo_lo = split(jnp.where(shift == step - far, there * inside, 0.0))
            below = slice(256 + 64 * nd, 320 + 64 * nd)
            for k, (u, v, w) in enumerate(
                ((own_hi, pair_hi, halo_hi), (own_hi, pair_hi, halo_hi), (own_lo, pair_lo, halo_lo))
            ):
                at = 512 * k + 128 * n
                ww[rows, at : at + 128] = u
                ww[below, at : at + 128] = v
                wh[n, rows, 128 * k : 128 * k + 128] = w
    for i in (2, 3, 5, 6, 7):
        snd_copy(i).wait_recv()
    e_copy.wait()

    def spread_out(k, a, b, i):
        re = jnp.concatenate([a[i, 0], b[i, 0]], axis=0)
        im = jnp.concatenate([a[i, 1], b[i, 1]], axis=0)
        for half_p, parts in enumerate(butterflies(re, im, tw)):
            for j, pieces in enumerate(parts):
                for half, w in enumerate(pieces):
                    hi, lo = split(w)
                    for third, x in enumerate((hi, lo, hi)):
                        at = 512 * third + 256 * half
                        spread[k, half_p, 64 * j : 64 * j + 64, at : at + 256] = x

    def transform(k):
        return [dot(spread[k, p], table[p]) for p in range(2)]

    def turn_phase(even, uneven, at, depth):
        early = lax.broadcasted_iota(jnp.int32, (64, 128), 1) < 64
        for j in range(4):
            for b4 in range(4):
                first, second = (even, uneven) if b4 % 2 == 0 else (uneven, even)
                rows = slice(64 * j, 64 * j + 64)
                c0 = 128 * (b4 // 2)
                u = jnp.where(early, first[rows, c0 : c0 + 128], second[rows, c0 : c0 + 128])
                v = jnp.where(early, first[rows, 256 + c0 : 384 + c0], second[rows, 256 + c0 : 384 + c0])
                e0 = 512 * b4 + 128 * j
                c, w = (
                    jnp.concatenate([e_own[part, :, e0 : e0 + 128], e_other[part, :, e0 : e0 + 128]], axis=0)
                    for part in range(2)
                )
                for half, value in enumerate((u * c - v * w, u * w + v * c)):
                    hi, lo = split(value)
                    for k, x in enumerate((hi, lo, hi)):
                        spec[b4, pl.ds(k * depth + at + 64 * half, 64), 128 * j : 128 * j + 128] = x

    def block_at(dg, dh):
        return 2 * lax.rem(g + dg, 2) + lax.rem(h + dh, 2)

    def near_copy(ii):
        return remote(near.at[1, ii], near_in.at[ii], near_s.at[ii], near_r.at[ii], core)

    def dest_rows(n):
        return pl.ds(pl.multiple_of(64 * (3 - block_of(n)), 64), 64)

    def row_copy(dg, i):
        at, ii = dest_rows(lax.rem(i, 4)), i // 4
        return remote(side.at[dg, ii, at], side_in.at[dg, ii, at], row_s.at[dg, i], row_r.at[dg, i], peer(dg, 0, 1))

    def opp_copy(dg, i, to):
        return remote(opp.at[i, dg], relay_in.at[i, dg], rel_s.at[i, dg], rel_r.at[i, dg], to)

    def opp_cross(dg, i):
        return opp_copy(dg, i, peer(0, 1, 1))

    def opp_direct(dg, i):
        return opp_copy(dg, i, peer(0, 0, 1))

    def cross_copy(dg, i):
        return remote(cross.at[dg, i], cross_in.at[dg, i], crs_s.at[dg, i], crs_r.at[dg, i], peer(dg, 1, 1))

    def own_rows(ii):
        def two(m, carry):
            @pl.when(jnp.logical_and(ii == 0, m == 0))
            def _():
                a_copy(2).start()
                b_copy(2).start()

            @pl.when(jnp.logical_and(ii == 0, m == 1))
            def _():
                pass_on(2, (0, 1))
                a_copy(3).start()
                b_copy(3).start()

            i, at = 4 * ii + 2 * m, pl.multiple_of(256 * m, 256)
            spread_out(0, keep, other, i)
            spread_out(1, keep, other, i + 1)
            turn_phase(*transform(0), at, 512)
            turn_phase(*transform(1), at + 128, 512)
            return carry

        lax.fori_loop(0, 2, two, 0)
        for dh in (1, 0):
            for dg in range(2):
                total = dot(ww[...], spec[block_at(dg, dh)])
                if dh == 0:
                    near[dg, ii] = total[0:256]
                else:
                    side[dg, ii] = total[0:256]
                    row_copy(dg, 4 * ii + 1).start()

                    @pl.when(ii == 0)
                    def _():
                        row_copy(dg, 3).start()

                pp[2 * dg + dh, ii] = total[256:512]
        near_copy(ii).start()

    def collect(i):
        n, ii = lax.rem(i, 4), i // 4
        at = dest_rows(n)
        for dg in range(2):
            cross_copy(dg, i).wait()
        parts = [
            near[0, ii, at, :] + side_in[0, ii, at, :] + cross_in[0, i],
            near_in[ii, at, :] + side_in[1, ii, at, :] + cross_in[1, i],
        ]
        got = dot(jnp.concatenate(split(jnp.concatenate(parts, axis=0)), axis=0), perm[h])
        rows = got[0:128] + got[128:256]
        for dg in range(2):
            row = 4 * (3 - block_of(n)) + 2 * lax.rem(g + dg, 2) + ii
            for c in range(4):
                for part in range(2):
                    at = 64 * dg + 32 * part
                    flat[c, part, pl.ds(row, 32, stride=16), :] = rows[at : at + 32, 128 * c : 128 * c + 128]

    def relay(i):
        n, ii = lax.rem(i, 4), i // 4

        @pl.when(lax.rem(i, 2) == 0)
        def _():
            at = dest_rows(n)
            for dg in range(2):
                opp_cross(dg, i).wait()
                side[dg, ii, at, :] = side[dg, ii, at, :] + relay_in[i, dg]
                row_copy(dg, i).start()

        @pl.when(lax.rem(i, 2) == 1)
        def _():
            for dg in range(2):
                opp_direct(dg, i).wait()
                cross[dg, i] = cross[dg, i] + relay_in[i, dg]
                cross_copy(dg, i).start()

    def step(i, carry):
        n, ii = lax.rem(i, 4), i // 4

        @pl.when(i == 1)
        def _():
            a_copy(5).start()
            b_copy(5).start()

        @pl.when(i == 2)
        def _():
            pass_on(3, (0, 1))
            a_copy(6).start()
            b_copy(6).start()

        @pl.when(i == 3)
        def _():
            a_copy(7).start()
            b_copy(7).start()

        @pl.when(i < 2)
        def _():
            own_rows(i)

        a_copy(i).wait_recv()
        b_copy(i).wait_recv()

        spread_out(0, halo_a, halo_b, i)
        turn_phase(*transform(0), 0, 128)
        for nn in range(4):

            @pl.when(n == nn)
            def _():
                rows = slice(64 * nn, 64 * nn + 64)
                for dh in range(2):
                    for dg in range(2):
                        blk = 2 * dg + dh
                        total = dot(wh[nn, 64 * nn :, :], spec[block_at(dg, dh), 0:384, :])
                        value = pp[blk, ii, rows, :] + total[0:64]
                        if nn < 3:
                            pp[blk, ii, 64 * nn + 64 :, :] = pp[blk, ii, 64 * nn + 64 :, :] + total[64:]
                        if dh == 1:
                            cross[dg, i] = value
                        else:
                            opp[i, dg] = value
                            (opp_direct if nn % 2 else opp_cross)(dg, i).start()
                if nn % 2 == 0:
                    for dg in range(2):
                        cross_copy(dg, i).start()

        @pl.when(i >= 1)
        def _():
            relay(i - 1)

        @pl.when(i == 3)
        def _():
            for dg in range(2):
                row_copy(dg, 7).start()

        @pl.when(i >= 4)
        def _():
            @pl.when(i == 4)
            def _():
                near_copy(0).wait()

            for dg in range(2):
                row_copy(dg, i - 4).wait()
            collect(i - 4)

        return carry

    lax.fori_loop(0, 8, step, 0)
    near_copy(1).wait()

    def last(i, carry):
        for dg in range(2):
            row_copy(dg, i).wait()
        collect(i)
        return carry

    lax.fori_loop(4, 6, last, 0)
    relay(7)
    lax.fori_loop(6, 8, last, 0)
    results = [
        pltpu.make_async_copy(flat.at[c], out.at[:, :, pl.ds(128 * c, 128)], load_sem.at[c]) for c in range(4)
    ]
    for c in results:
        c.start()
    for i in range(8):
        snd_copy(i).wait_send()
        if i != 4:
            a_copy(i).wait_send()
        if i != 4:
            b_copy(i).wait_send()
    for hops in range(1, 4):
        for slot in range(2):
            via_copy(hops, slot).wait_send()
    for c in results:
        c.wait()


def local(strips, field, spectral_phase, chirp_shift, tile_map, tile_phase):
    waves, tw = dft_tables()
    vmem = pl.BlockSpec(memory_space=pltpu.VMEM)
    hbm = pl.BlockSpec(memory_space=pl.ANY)
    rows = pltpu.VMEM((8, 2, 32, 1024), F32)
    small = pltpu.VMEM((16, 128), F32)
    phase = pltpu.VMEM((2, 32, NY), F32)
    sums = pltpu.VMEM((2, 2, 256, 512), F32)
    dma = pltpu.SemaphoreType.DMA
    out = pl.pallas_call(
        functools.partial(kernel, strips),
        in_specs=[hbm, hbm, hbm, hbm, vmem, vmem, pl.BlockSpec(memory_space=pltpu.SMEM)],
        out_specs=pl.BlockSpec(memory_space=pl.ANY),
        out_shape=jax.ShapeDtypeStruct((2, 512, 512), F32),
        scratch_shapes=[
            pltpu.VMEM((8, 2, 512, 128), F32),
            rows, rows, rows, rows, rows,
            small, small, small, small,
            pltpu.VMEM((32, NY), F32),
            pltpu.VMEM(waves.shape, F32),
            pltpu.VMEM(tw.shape, F32),
            phase, phase,
            pltpu.VMEM((2, 1536, 512), BF),
            pltpu.VMEM((2, 512, 512), BF),
            pltpu.VMEM((512, 1536), BF),
            pltpu.VMEM((4, 256, 384), BF),
            pltpu.VMEM((2, 2, 256, 1536), BF),
            pltpu.VMEM((4, 1536, 512), BF),
            sums,
            pltpu.VMEM((2, 256, 512), F32),
            sums, sums,
            pltpu.VMEM((4, 2, 256, 512), F32),
            pltpu.VMEM((8, 2, 64, 512), F32),
            pltpu.VMEM((8, 2, 64, 512), F32),
            pltpu.VMEM((2, 8, 64, 512), F32),
            pltpu.VMEM((2, 8, 64, 512), F32),
            pltpu.VMEM((2, 2, 32, 1024), F32),
            pltpu.VMEM((2, 2, 32, 1024), F32),
            dma((11,)),
            *[dma((8,))] * 6,
            dma((3,)), dma((3,)),
            dma((2,)), dma((2,)),
            dma((2, 8)), dma((2, 8)),
            dma((8, 2)), dma((8, 2)),
            dma((2, 8)), dma((2, 8)),
            *[dma((2,))] * 4,
        ],
        compiler_params=pltpu.CompilerParams(
            collective_id=0, has_side_effects=True, vmem_limit_bytes=VMEM * 2**20
        ),
        cost_estimate=pl.CostEstimate(flops=40 * 10**9, bytes_accessed=10 * 2**20, transcendentals=0),
    )(
        field.reshape(2, 512, 1024), spectral_phase, jnp.asarray(waves), jnp.asarray(tw),
        chirp_shift.reshape(1, 32), tile_phase, tile_map,
    )
    return out.reshape(2, NT, 16, 512)


def solution(mesh):
    placed = (P(None, "freq", "xs", "yh"), P("freq", None), P("freq"), P("xs"), P(None, "freq"))
    return jax.shard_map(
        functools.partial(local, mesh.shape["xs"]),
        mesh=mesh,
        in_specs=placed,
        out_specs=P(None, None, "xs", ("freq", "yh")),
        check_vma=False,
    )
```

```python
import functools
import math

import jax
import jax.numpy as jnp
import numpy as np
from jax import lax
from jax.experimental import pallas as pl
from jax.experimental.pallas import tpu as pltpu
from jax.sharding import PartitionSpec as P

NF = 64
NY = 2048
NT = 32
VMEM = 60
BF = jnp.bfloat16
F32 = jnp.float32
AXES = ("freq", "xs", "yh")
MESH = pl.DeviceIdType.MESH


def dft_tables():
    m = np.arange(256)
    angle = 2.0 * np.pi * (np.outer(m, m) % 256) / 256
    waves = np.stack([np.cos(angle), np.sin(angle)]) / math.sqrt(NY)
    odd_order = np.concatenate([np.arange(64) + 64 * b for b in (1, 0, 3, 2)])
    turn = 2.0 * np.pi * np.outer(np.arange(8), m) / NY
    twiddle = np.stack([np.cos(turn), np.sin(turn)])
    return np.stack([waves, waves[:, :, odd_order]]).astype(np.float32), twiddle.astype(np.float32)


def split(value):
    high = value.astype(BF)
    return high, (value - high.astype(F32)).astype(BF)


def dot(a, b):
    return jnp.dot(a, b, preferred_element_type=F32)


def dot_t(a, b):
    return lax.dot_general(a, b, (((1,), (1,)), ((), ())), preferred_element_type=F32)


def sincos(x):
    k = jnp.floor(x * (2.0 / math.pi) + 0.5)
    r = ((x - k * 1.5703125) - k * 4.837512969970703125e-4) - k * 7.54978995489188216e-8
    z = r * r
    sine = r + r * z * (-1.6666654611e-1 + z * (8.3321608736e-3 - z * 1.9515295891e-4))
    cosine = (1.0 - 0.5 * z) + z * z * (4.166664568298827e-2 + z * (-1.388731625493765e-3 + z * 2.443315711809948e-5))
    half = jnp.floor(k * 0.5)
    swap = (k - 2.0 * half) > 0.5
    sign = 1.0 - 2.0 * (half - 2.0 * jnp.floor(half * 0.5))
    return sign * jnp.where(swap, cosine, sine), sign * jnp.where(swap, -sine, cosine)


def butterflies(re, im, tw):
    a = [(re[:, 256 * c : 256 * c + 256], im[:, 256 * c : 256 * c + 256]) for c in range(4)]
    r = math.sqrt(0.5)

    def add(u, v):
        return u[0] + v[0], u[1] + v[1]

    def sub(u, v):
        return u[0] - v[0], u[1] - v[1]

    def mi(u):
        return u[1], -u[0]

    def four(b):
        e0, e1 = add(b[0], b[2]), sub(b[0], b[2])
        e2, e3 = add(b[1], b[3]), mi(sub(b[1], b[3]))
        return add(e0, e2), add(e1, e3), sub(e0, e2), sub(e1, e3)

    even = four(a)
    b1 = ((a[1][0] + a[1][1]) * r, (a[1][1] - a[1][0]) * r)
    b3 = ((a[3][1] - a[3][0]) * r, (-a[3][0] - a[3][1]) * r)
    odd = four((a[0], b1, mi(a[2]), b3))
    both = []
    for side, parts in enumerate((even, odd)):
        row = []
        for j in range(4):
            p = 2 * j + side
            u = parts[j]
            if p:
                c, s = tw[0, p : p + 1, :], tw[1, p : p + 1, :]
                u = u[0] * c + u[1] * s, u[1] * c - u[0] * s
            row.append(u)
        both.append(row)
    return both


def kernel(
    strips, field, phi_hbm, waves_hbm, tw_hbm, shift_row, tile_phase, tile_ids, out,
    flat, snd, keep, other, halo_a, halo_b, prm, prm_out, prm_in, prm_pair,
    phi, waves, tw, e_own, e_other, table, perm, ww, wh,
    spread, spec, near, near_in, side, side_in, pp, opp, relay_in, cross, cross_in, via_1, via_2, *rest,
):
    (load_sem, snd_s, snd_r, ha_s, ha_r, hb_s, hb_r, prm_s, prm_r,
     near_s, near_r, row_s, row_r, rel_s, rel_r, crs_s, crs_r, v1_s, v1_r, v2_s, v2_r) = rest
    g, s, h = (lax.axis_index(a) for a in AXES)
    odd = lax.rem(s, 2)
    pair = s + 1 - 2 * odd
    onward = lax.rem(s + strips + 4 * odd - 2, strips)
    back = lax.rem(s + strips + 2 - 4 * odd, strips)
    core = (1 - g, s, h)

    z, y, turns = s // 8, lax.rem(s // 2, 4), strips // 8
    hop = 1 - 2 * odd
    across = 8 * z + 2 * lax.rem(y + 4 + hop, 4) + odd
    across_from = 8 * z + 2 * lax.rem(y + 4 - hop, 4) + odd
    z_on = 8 * lax.rem(z + turns - hop, turns) + odd
    z_back = 8 * lax.rem(z + turns + hop, turns) + odd
    leaves = (y == 2 - odd).astype(jnp.int32)
    third = across + leaves * (z_on + 2 * (3 - 3 * odd) - across)
    enters = (y == 3 - 3 * odd).astype(jnp.int32)
    third_from = across_from + enters * (z_back + 2 * (2 - odd) - across_from)

    def peer(dg, ds, dh):
        return (lax.rem(g + dg, 2), pair if ds else s, lax.rem(h + dh, 2))

    def remote(src, dst, a, b, to):
        return pltpu.make_async_remote_copy(
            src_ref=src, dst_ref=dst, send_sem=a, recv_sem=b, device_id=to, device_id_type=MESH
        )

    def block_of(n):
        return n + odd * (3 - 2 * n)

    loads = [
        pltpu.make_async_copy(field.at[:, :, pl.ds(128 * y, 128)], flat.at[y], load_sem.at[y]) for y in range(8)
    ]
    tables = [
        pltpu.make_async_copy(src, dst, load_sem.at[8 + k])
        for k, (src, dst) in enumerate(((waves_hbm, waves), (tw_hbm, tw), (phi_hbm, phi)))
    ]
    for c in loads + tables:
        c.start()
    barrier = pltpu.get_barrier_semaphore()
    greet = [core, peer(0, 0, 1), peer(1, 0, 1), peer(0, 1, 1), peer(1, 1, 1), (g, onward, h), (g, back, h)]
    greet += [(g, across, h), (g, across_from, h), (g, third, h), (g, third_from, h)]
    for to in greet:
        pl.semaphore_signal(barrier, inc=1, device_id=to, device_id_type=MESH)

    def snd_copy(i):
        return remote(snd.at[i], other.at[i], snd_s.at[i], snd_r.at[i], core)

    def a_copy(i):
        return remote(keep.at[i], halo_a.at[i], ha_s.at[i], ha_r.at[i], (g, onward, h))

    def b_copy(i):
        return remote(other.at[i], halo_b.at[i], hb_s.at[i], hb_r.at[i], (g, onward, h))

    def via_copy(hops, slot):
        which, i = ((0, 4), (1, 4))[slot]
        if hops == 1:
            src = (keep, other)[which].at[i]
            return remote(src, via_1.at[slot], v1_s.at[slot], v1_r.at[slot], (g, across, h))
        if hops == 2:
            return remote(via_1.at[slot], via_2.at[slot], v2_s.at[slot], v2_r.at[slot], (g, across, h))
        dst, sems = ((halo_a, (ha_s, ha_r)), (halo_b, (hb_s, hb_r)))[which]
        return remote(via_2.at[slot], dst.at[i], sems[0].at[i], sems[1].at[i], (g, third, h))

    def pass_on(hops, slots):
        for slot in slots:
            via_copy(hops - 1, slot).wait_recv()
            via_copy(hops, slot).start()

    def gather_rows(i, whose, into):
        row = 4 * block_of(lax.rem(i, 4)) + 2 * whose + i // 4
        for c in range(2):
            for y in range(8):
                into[i, c, :, 128 * y : 128 * y + 128] = flat[y, c, pl.ds(row, 32, stride=16), :]

    gap = jnp.zeros((8, 32), F32)
    rows = jnp.concatenate([shift_row[...].astype(F32), tile_phase[...], jnp.zeros((3, 32), F32)], axis=0)
    prm[0:8, :] = jnp.concatenate([rows, gap, rows, gap], axis=1)
    for rb in range(4):
        prm[8 + rb : 9 + rb, :] = jnp.full((1, 128), tile_ids[rb], jnp.int32).astype(F32)
    prm[12:16, :] = jnp.zeros((4, 128), F32)
    prm_out[...] = pltpu.roll(prm[...], 32, 1)
    prm_core = remote(prm_out, prm_in, prm_s.at[0], prm_r.at[0], core)
    prm_strip = remote(prm, prm_pair, prm_s.at[1], prm_r.at[1], peer(0, 1, 1))

    for c in loads:
        c.wait()

    def pack_send(i, carry):
        gather_rows(i, 1 - g, snd)
        snd_copy(i).start()
        return carry

    def pack_keep(i, carry):
        gather_rows(i, g, keep)
        return carry

    for i in (0, 4, 1):
        gather_rows(i, g, keep)
    pl.semaphore_wait(barrier, len(greet))
    a_copy(0).start()
    via_copy(1, 0).start()
    a_copy(1).start()
    lax.fori_loop(0, 8, pack_send, 0)
    prm_core.start()
    prm_strip.start()
    lax.fori_loop(2, 4, pack_keep, 0)
    lax.fori_loop(5, 8, pack_keep, 0)
    for i in (0, 4, 1):
        snd_copy(i).wait_recv()
        if i == 4:
            via_copy(1, 1).start()
        else:
            b_copy(i).start()

    for c in tables:
        c.wait()
    lane = lax.broadcasted_iota(jnp.int32, (512, 1), 0)
    wave = lax.broadcasted_iota(jnp.int32, (1, 512), 1)
    turn = lax.rem(lane, 128)
    for half in range(2):
        late = (turn >= 64).astype(jnp.int32)
        late = late if half == 0 else 1 - late
        target = 8 * lax.rem(turn, 64) + 2 * (lane // 128) + late
        perm[half] = jnp.where(target == wave, 1.0, 0.0).astype(BF)
        c_hi, c_lo = split(waves[half, 0])
        s_hi, s_lo = split(waves[half, 1])
        for k, (c, w) in enumerate(((c_hi, s_hi), (c_hi, s_hi), (c_lo, s_lo))):
            table[half, 512 * k : 512 * k + 256, 0:256] = c
            table[half, 512 * k : 512 * k + 256, 256:512] = -w
            table[half, 512 * k + 256 : 512 * k + 512, 0:256] = w
            table[half, 512 * k + 256 : 512 * k + 512, 256:512] = c

    lanes = lax.rem(lax.broadcasted_iota(jnp.int32, (1, 512), 1), 128)
    for half in range(2):
        late = lanes >= 64 if half == 0 else lanes < 64
        sign = 1.0 - 2.0 * jnp.where(late, h, 0).astype(F32)
        stack = []
        for b in (half, half + 2):
            sine, cosine = sincos(phi[:, 512 * b : 512 * b + 512])
            stack += [*split(cosine), *split(sine)]
        got = dot_t(jnp.concatenate(stack, axis=0), perm[half])
        for k, b in enumerate((half, half + 2)):
            for part in range(2):
                at = 128 * k + 64 * part
                e_own[part, :, 512 * b : 512 * b + 512] = (got[at : at + 32] + got[at + 32 : at + 64]) * sign
    e_copy = remote(e_own, e_other, prm_s.at[2], prm_r.at[2], core)
    e_copy.start()

    prm_core.wait()
    prm_strip.wait()
    both = prm[...] + prm_in[...]
    shift = both[0:1, :]
    col = lax.broadcasted_iota(jnp.int32, (NT, 128), 1)
    freq = lax.rem(lax.rem(col, 64) + 32 * g, NF)
    angle = (2.0 * math.pi / NF) * lax.rem(lax.broadcasted_iota(jnp.int32, (NT, 128), 0) * freq, NF).astype(F32)
    scale = 1.0 / math.sqrt(NF)
    real_in = col < 64

    def base(tile):
        phase = jnp.zeros((1, 128), F32)
        for t in range(4):
            phase = phase + jnp.where(tile == float(t), both[1 + t : 2 + t, :], 0.0)
        im, re = sincos(angle + phase)
        im, re = im * scale, re * scale
        return jnp.concatenate([jnp.where(real_in, re, -im), jnp.where(real_in, im, re)], axis=0)

    far = (4 * (1 - 2 * odd)).astype(F32)
    inside = jnp.where(odd == 1, (s > 1).astype(F32), (s < strips - 2).astype(F32))
    for nd in range(4):
        dest = block_of(nd)
        here, there = base(prm[8 + nd : 9 + nd, :]), base(prm_pair[pl.ds(8 + dest, 1), :])
        rows = slice(64 * nd, 64 * nd + 64)
        for n in range(4):
            source = block_of(n)
            own_hi, own_lo = split(jnp.where(shift == (nd - source).astype(F32), here, 0.0))
            step = (dest - source).astype(F32)
            pair_hi, pair_lo = split(jnp.where(shift == step + far, there, 0.0))
            halo_hi, halo_lo = split(jnp.where(shift == step - far, there * inside, 0.0))
            below = slice(256 + 64 * nd, 320 + 64 * nd)
            for k, (u, v, w) in enumerate(
                ((own_hi, pair_hi, halo_hi), (own_hi, pair_hi, halo_hi), (own_lo, pair_lo, halo_lo))
            ):
                at = 512 * k + 128 * n
                ww[rows, at : at + 128] = u
                ww[below, at : at + 128] = v
                wh[n, rows, 128 * k : 128 * k + 128] = w
    for i in (2, 3):
        snd_copy(i).wait_recv()
    e_copy.wait()

    def spread_out(k, a, b, i):
        re = jnp.concatenate([a[i, 0], b[i, 0]], axis=0)
        im = jnp.concatenate([a[i, 1], b[i, 1]], axis=0)
        for half_p, parts in enumerate(butterflies(re, im, tw)):
            for j, pieces in enumerate(parts):
                for half, w in enumerate(pieces):
                    hi, lo = split(w)
                    for third, x in enumerate((hi, lo, hi)):
                        at = 512 * third + 256 * half
                        spread[k, half_p, 64 * j : 64 * j + 64, at : at + 256] = x

    def transform(k):
        return [dot(spread[k, p], table[p]) for p in range(2)]

    def turn_phase(even, uneven, at, depth):
        early = lax.broadcasted_iota(jnp.int32, (64, 128), 1) < 64
        for j in range(4):
            for b4 in range(4):
                first, second = (even, uneven) if b4 % 2 == 0 else (uneven, even)
                rows = slice(64 * j, 64 * j + 64)
                c0 = 128 * (b4 // 2)
                u = jnp.where(early, first[rows, c0 : c0 + 128], second[rows, c0 : c0 + 128])
                v = jnp.where(early, first[rows, 256 + c0 : 384 + c0], second[rows, 256 + c0 : 384 + c0])
                e0 = 512 * b4 + 128 * j
                c, w = (
                    jnp.concatenate([e_own[part, :, e0 : e0 + 128], e_other[part, :, e0 : e0 + 128]], axis=0)
                    for part in range(2)
                )
                for half, value in enumerate((u * c - v * w, u * w + v * c)):
                    hi, lo = split(value)
                    for k, x in enumerate((hi, lo, hi)):
                        spec[b4, pl.ds(k * depth + at + 64 * half, 64), 128 * j : 128 * j + 128] = x

    def block_at(dg, dh):
        return 2 * lax.rem(g + dg, 2) + lax.rem(h + dh, 2)

    def near_copy(ii):
        return remote(near.at[1, ii], near_in.at[ii], near_s.at[ii], near_r.at[ii], core)

    def dest_rows(n):
        return pl.ds(pl.multiple_of(64 * (3 - block_of(n)), 64), 64)

    def row_copy(dg, i):
        at, ii = dest_rows(lax.rem(i, 4)), i // 4
        return remote(side.at[dg, ii, at], side_in.at[dg, ii, at], row_s.at[dg, i], row_r.at[dg, i], peer(dg, 0, 1))

    def opp_copy(dg, i, to):
        return remote(opp.at[i, dg], relay_in.at[i, dg], rel_s.at[i, dg], rel_r.at[i, dg], to)

    def opp_cross(dg, i):
        return opp_copy(dg, i, peer(0, 1, 1))

    def opp_direct(dg, i):
        return opp_copy(dg, i, peer(0, 0, 1))

    def cross_copy(dg, i):
        return remote(cross.at[dg, i], cross_in.at[dg, i], crs_s.at[dg, i], crs_r.at[dg, i], peer(dg, 1, 1))

    def own_rows(ii):
        def two(m, carry):
            @pl.when(jnp.logical_and(ii == 0, m == 0))
            def _():
                a_copy(2).start()
                b_copy(2).start()

            @pl.when(jnp.logical_and(ii == 0, m == 1))
            def _():
                pass_on(2, (0, 1))
                a_copy(3).start()
                b_copy(3).start()

            i, at = 4 * ii + 2 * m, pl.multiple_of(256 * m, 256)
            spread_out(0, keep, other, i)
            spread_out(1, keep, other, i + 1)
            turn_phase(*transform(0), at, 512)
            turn_phase(*transform(1), at + 128, 512)
            return carry

        lax.fori_loop(0, 2, two, 0)
        for dh in (1, 0):
            for dg in range(2):
                total = dot(ww[...], spec[block_at(dg, dh)])
                if dh == 0:
                    near[dg, ii] = total[0:256]
                else:
                    side[dg, ii] = total[0:256]
                    row_copy(dg, 4 * ii + 1).start()

                    @pl.when(ii == 0)
                    def _():
                        row_copy(dg, 3).start()

                pp[2 * dg + dh, ii] = total[256:512]
        near_copy(ii).start()

    def collect(i):
        n, ii = lax.rem(i, 4), i // 4
        at = dest_rows(n)
        for dg in range(2):
            cross_copy(dg, i).wait()
        parts = [
            near[0, ii, at, :] + side_in[0, ii, at, :] + cross_in[0, i],
            near_in[ii, at, :] + side_in[1, ii, at, :] + cross_in[1, i],
        ]
        got = dot(jnp.concatenate(split(jnp.concatenate(parts, axis=0)), axis=0), perm[h])
        rows = got[0:128] + got[128:256]
        for dg in range(2):
            row = 4 * (3 - block_of(n)) + 2 * lax.rem(g + dg, 2) + ii
            for c in range(4):
                for part in range(2):
                    at = 64 * dg + 32 * part
                    flat[c, part, pl.ds(row, 32, stride=16), :] = rows[at : at + 32, 128 * c : 128 * c + 128]

    def by_cross(i):
        return jnp.logical_and(lax.rem(i, 2) == 0, i < 6)

    def relay(i):
        n, ii = lax.rem(i, 4), i // 4

        @pl.when(by_cross(i))
        def _():
            at = dest_rows(n)
            for dg in range(2):
                opp_cross(dg, i).wait()
                side[dg, ii, at, :] = side[dg, ii, at, :] + relay_in[i, dg]
                row_copy(dg, i).start()

        @pl.when(jnp.logical_not(by_cross(i)))
        def _():
            for dg in range(2):
                opp_direct(dg, i).wait()
                cross[dg, i] = cross[dg, i] + relay_in[i, dg]
                cross_copy(dg, i).start()

    def step(i, carry):
        n, ii = lax.rem(i, 4), i // 4

        @pl.when(i == 1)
        def _():
            for late in range(5, 8):
                snd_copy(late).wait_recv()
            a_copy(5).start()
            b_copy(5).start()

        @pl.when(i == 2)
        def _():
            pass_on(3, (0, 1))
            a_copy(6).start()
            b_copy(6).start()

        @pl.when(i == 3)
        def _():
            a_copy(7).start()
            b_copy(7).start()

        @pl.when(i < 2)
        def _():
            own_rows(i)

        a_copy(i).wait_recv()
        b_copy(i).wait_recv()

        spread_out(0, halo_a, halo_b, i)
        turn_phase(*transform(0), 0, 128)
        for nn in range(4):

            @pl.when(n == nn)
            def _():
                rows = slice(64 * nn, 64 * nn + 64)
                for dh in range(2):
                    for dg in range(2):
                        blk = 2 * dg + dh
                        total = dot(wh[nn, 64 * nn :, :], spec[block_at(dg, dh), 0:384, :])
                        value = pp[blk, ii, rows, :] + total[0:64]
                        if nn < 3:
                            pp[blk, ii, 64 * nn + 64 :, :] = pp[blk, ii, 64 * nn + 64 :, :] + total[64:]
                        if dh == 1:
                            cross[dg, i] = value
                        else:
                            opp[i, dg] = value

                            @pl.when(by_cross(i))
                            def _():
                                opp_cross(dg, i).start()

                            @pl.when(jnp.logical_not(by_cross(i)))
                            def _():
                                opp_direct(dg, i).start()

                @pl.when(by_cross(i))
                def _():
                    for dg in range(2):
                        cross_copy(dg, i).start()

        @pl.when(i >= 1)
        def _():
            relay(i - 1)

        @pl.when(i == 3)
        def _():
            for dg in range(2):
                row_copy(dg, 7).start()

        @pl.when(i == 4)
        def _():
            for dg in range(2):
                row_copy(dg, 6).start()

        @pl.when(i >= 4)
        def _():
            @pl.when(i == 4)
            def _():
                near_copy(0).wait()

            for dg in range(2):
                row_copy(dg, i - 4).wait()
            collect(i - 4)

        return carry

    lax.fori_loop(0, 8, step, 0)
    near_copy(1).wait()

    def last(i, carry):
        for dg in range(2):
            row_copy(dg, i).wait()
        collect(i)
        return carry

    lax.fori_loop(4, 6, last, 0)
    relay(7)
    lax.fori_loop(6, 8, last, 0)
    results = [
        pltpu.make_async_copy(flat.at[c], out.at[:, :, pl.ds(128 * c, 128)], load_sem.at[c]) for c in range(4)
    ]
    for c in results:
        c.start()
    for i in range(8):
        snd_copy(i).wait_send()
        if i != 4:
            a_copy(i).wait_send()
        if i != 4:
            b_copy(i).wait_send()
    for hops in range(1, 4):
        for slot in range(2):
            via_copy(hops, slot).wait_send()
    for c in results:
        c.wait()


def local(strips, field, spectral_phase, chirp_shift, tile_map, tile_phase):
    waves, tw = dft_tables()
    vmem = pl.BlockSpec(memory_space=pltpu.VMEM)
    hbm = pl.BlockSpec(memory_space=pl.ANY)
    rows = pltpu.VMEM((8, 2, 32, 1024), F32)
    small = pltpu.VMEM((16, 128), F32)
    phase = pltpu.VMEM((2, 32, NY), F32)
    sums = pltpu.VMEM((2, 2, 256, 512), F32)
    dma = pltpu.SemaphoreType.DMA
    out = pl.pallas_call(
        functools.partial(kernel, strips),
        in_specs=[hbm, hbm, hbm, hbm, vmem, vmem, pl.BlockSpec(memory_space=pltpu.SMEM)],
        out_specs=pl.BlockSpec(memory_space=pl.ANY),
        out_shape=jax.ShapeDtypeStruct((2, 512, 512), F32),
        scratch_shapes=[
            pltpu.VMEM((8, 2, 512, 128), F32),
            rows, rows, rows, rows, rows,
            small, small, small, small,
            pltpu.VMEM((32, NY), F32),
            pltpu.VMEM(waves.shape, F32),
            pltpu.VMEM(tw.shape, F32),
            phase, phase,
            pltpu.VMEM((2, 1536, 512), BF),
            pltpu.VMEM((2, 512, 512), BF),
            pltpu.VMEM((512, 1536), BF),
            pltpu.VMEM((4, 256, 384), BF),
            pltpu.VMEM((2, 2, 256, 1536), BF),
            pltpu.VMEM((4, 1536, 512), BF),
            sums,
            pltpu.VMEM((2, 256, 512), F32),
            sums, sums,
            pltpu.VMEM((4, 2, 256, 512), F32),
            pltpu.VMEM((8, 2, 64, 512), F32),
            pltpu.VMEM((8, 2, 64, 512), F32),
            pltpu.VMEM((2, 8, 64, 512), F32),
            pltpu.VMEM((2, 8, 64, 512), F32),
            pltpu.VMEM((2, 2, 32, 1024), F32),
            pltpu.VMEM((2, 2, 32, 1024), F32),
            dma((11,)),
            *[dma((8,))] * 6,
            dma((3,)), dma((3,)),
            dma((2,)), dma((2,)),
            dma((2, 8)), dma((2, 8)),
            dma((8, 2)), dma((8, 2)),
            dma((2, 8)), dma((2, 8)),
            *[dma((2,))] * 4,
        ],
        compiler_params=pltpu.CompilerParams(
            collective_id=0, has_side_effects=True, vmem_limit_bytes=VMEM * 2**20
        ),
        cost_estimate=pl.CostEstimate(flops=40 * 10**9, bytes_accessed=10 * 2**20, transcendentals=0),
    )(
        field.reshape(2, 512, 1024), spectral_phase, jnp.asarray(waves), jnp.asarray(tw),
        chirp_shift.reshape(1, 32), tile_phase, tile_map,
    )
    return out.reshape(2, NT, 16, 512)


def solution(mesh):
    placed = (P(None, "freq", "xs", "yh"), P("freq", None), P("freq"), P("xs"), P(None, "freq"))
    return jax.shard_map(
        functools.partial(local, mesh.shape["xs"]),
        mesh=mesh,
        in_specs=placed,
        out_specs=P(None, None, "xs", ("freq", "yh")),
        check_vma=False,
    )
```

```python
import functools
import math

import jax
import jax.numpy as jnp
import numpy as np
from jax import lax
from jax.experimental import pallas as pl
from jax.experimental.pallas import tpu as pltpu
from jax.sharding import PartitionSpec as P

NF = 64
NY = 2048
NT = 32
VMEM = 60
BF = jnp.bfloat16
F32 = jnp.float32
AXES = ("freq", "xs", "yh")
MESH = pl.DeviceIdType.MESH


def dft_tables():
    m = np.arange(256)
    angle = 2.0 * np.pi * (np.outer(m, m) % 256) / 256
    waves = np.stack([np.cos(angle), np.sin(angle)]) / math.sqrt(NY)
    odd_order = np.concatenate([np.arange(64) + 64 * b for b in (1, 0, 3, 2)])
    turn = 2.0 * np.pi * np.outer(np.arange(8), m) / NY
    twiddle = np.stack([np.cos(turn), np.sin(turn)])
    return np.stack([waves, waves[:, :, odd_order]]).astype(np.float32), twiddle.astype(np.float32)


def split(value):
    high = value.astype(BF)
    return high, (value - high.astype(F32)).astype(BF)


def dot(a, b):
    return jnp.dot(a, b, preferred_element_type=F32)


def dot_t(a, b):
    return lax.dot_general(a, b, (((1,), (1,)), ((), ())), preferred_element_type=F32)


def sincos(x):
    k = jnp.floor(x * (2.0 / math.pi) + 0.5)
    r = ((x - k * 1.5703125) - k * 4.837512969970703125e-4) - k * 7.54978995489188216e-8
    z = r * r
    sine = r + r * z * (-1.6666654611e-1 + z * (8.3321608736e-3 - z * 1.9515295891e-4))
    cosine = (1.0 - 0.5 * z) + z * z * (4.166664568298827e-2 + z * (-1.388731625493765e-3 + z * 2.443315711809948e-5))
    half = jnp.floor(k * 0.5)
    swap = (k - 2.0 * half) > 0.5
    sign = 1.0 - 2.0 * (half - 2.0 * jnp.floor(half * 0.5))
    return sign * jnp.where(swap, cosine, sine), sign * jnp.where(swap, -sine, cosine)


def butterflies(re, im, tw):
    a = [(re[:, 256 * c : 256 * c + 256], im[:, 256 * c : 256 * c + 256]) for c in range(4)]
    r = math.sqrt(0.5)

    def add(u, v):
        return u[0] + v[0], u[1] + v[1]

    def sub(u, v):
        return u[0] - v[0], u[1] - v[1]

    def mi(u):
        return u[1], -u[0]

    def four(b):
        e0, e1 = add(b[0], b[2]), sub(b[0], b[2])
        e2, e3 = add(b[1], b[3]), mi(sub(b[1], b[3]))
        return add(e0, e2), add(e1, e3), sub(e0, e2), sub(e1, e3)

    even = four(a)
    b1 = ((a[1][0] + a[1][1]) * r, (a[1][1] - a[1][0]) * r)
    b3 = ((a[3][1] - a[3][0]) * r, (-a[3][0] - a[3][1]) * r)
    odd = four((a[0], b1, mi(a[2]), b3))
    both = []
    for side, parts in enumerate((even, odd)):
        row = []
        for j in range(4):
            p = 2 * j + side
            u = parts[j]
            if p:
                c, s = tw[0, p : p + 1, :], tw[1, p : p + 1, :]
                u = u[0] * c + u[1] * s, u[1] * c - u[0] * s
            row.append(u)
        both.append(row)
    return both


def kernel(
    strips, field, phi_hbm, waves_hbm, tw_hbm, shift_row, tile_phase, tile_ids, out,
    flat, snd, keep, other, halo_a, halo_b, prm, prm_out, prm_in, prm_pair,
    phi, waves, tw, e_own, e_other, table, perm, ww, wh,
    spread, spec, near, near_in, side, side_in, pp, opp, relay_in, cross, cross_in, via_1, via_2, *rest,
):
    (load_sem, snd_s, snd_r, ha_s, ha_r, hb_s, hb_r, prm_s, prm_r,
     near_s, near_r, row_s, row_r, rel_s, rel_r, crs_s, crs_r, v1_s, v1_r, v2_s, v2_r) = rest
    g, s, h = (lax.axis_index(a) for a in AXES)
    odd = lax.rem(s, 2)
    pair = s + 1 - 2 * odd
    onward = lax.rem(s + strips + 4 * odd - 2, strips)
    back = lax.rem(s + strips + 2 - 4 * odd, strips)
    core = (1 - g, s, h)

    z, y, turns = s // 8, lax.rem(s // 2, 4), strips // 8
    hop = 1 - 2 * odd
    across = 8 * z + 2 * lax.rem(y + 4 + hop, 4) + odd
    across_from = 8 * z + 2 * lax.rem(y + 4 - hop, 4) + odd
    z_on = 8 * lax.rem(z + turns - hop, turns) + odd
    z_back = 8 * lax.rem(z + turns + hop, turns) + odd
    leaves = (y == 2 - odd).astype(jnp.int32)
    third = across + leaves * (z_on + 2 * (3 - 3 * odd) - across)
    enters = (y == 3 - 3 * odd).astype(jnp.int32)
    third_from = across_from + enters * (z_back + 2 * (2 - odd) - across_from)

    def peer(dg, ds, dh):
        return (lax.rem(g + dg, 2), pair if ds else s, lax.rem(h + dh, 2))

    def remote(src, dst, a, b, to):
        return pltpu.make_async_remote_copy(
            src_ref=src, dst_ref=dst, send_sem=a, recv_sem=b, device_id=to, device_id_type=MESH
        )

    def block_of(n):
        return n + odd * (3 - 2 * n)

    loads = [
        pltpu.make_async_copy(field.at[:, :, pl.ds(128 * y, 128)], flat.at[y], load_sem.at[y]) for y in range(8)
    ]
    tables = [
        pltpu.make_async_copy(src, dst, load_sem.at[8 + k])
        for k, (src, dst) in enumerate(((waves_hbm, waves), (tw_hbm, tw), (phi_hbm, phi)))
    ]
    for c in loads + tables:
        c.start()
    barrier = pltpu.get_barrier_semaphore()
    greet = [core, peer(0, 0, 1), peer(1, 0, 1), peer(0, 1, 1), peer(1, 1, 1), (g, onward, h), (g, back, h)]
    greet += [(g, across, h), (g, across_from, h), (g, third, h), (g, third_from, h)]
    for to in greet:
        pl.semaphore_signal(barrier, inc=1, device_id=to, device_id_type=MESH)

    def snd_copy(i):
        return remote(snd.at[i], other.at[i], snd_s.at[i], snd_r.at[i], core)

    def a_copy(i):
        return remote(keep.at[i], halo_a.at[i], ha_s.at[i], ha_r.at[i], (g, onward, h))

    def b_copy(i):
        return remote(other.at[i], halo_b.at[i], hb_s.at[i], hb_r.at[i], (g, onward, h))

    def via_copy(hops, slot):
        which, i = ((0, 4), (1, 4))[slot]
        if hops == 1:
            src = (keep, other)[which].at[i]
            return remote(src, via_1.at[slot], v1_s.at[slot], v1_r.at[slot], (g, across, h))
        if hops == 2:
            return remote(via_1.at[slot], via_2.at[slot], v2_s.at[slot], v2_r.at[slot], (g, across, h))
        dst, sems = ((halo_a, (ha_s, ha_r)), (halo_b, (hb_s, hb_r)))[which]
        return remote(via_2.at[slot], dst.at[i], sems[0].at[i], sems[1].at[i], (g, third, h))

    def pass_on(hops, slots):
        for slot in slots:
            via_copy(hops - 1, slot).wait_recv()
            via_copy(hops, slot).start()

    def gather_rows(i, whose, into):
        row = 4 * block_of(lax.rem(i, 4)) + 2 * whose + i // 4
        for c in range(2):
            for y in range(8):
                into[i, c, :, 128 * y : 128 * y + 128] = flat[y, c, pl.ds(row, 32, stride=16), :]

    gap = jnp.zeros((8, 32), F32)
    rows = jnp.concatenate([shift_row[...].astype(F32), tile_phase[...], jnp.zeros((3, 32), F32)], axis=0)
    prm[0:8, :] = jnp.concatenate([rows, gap, rows, gap], axis=1)
    for rb in range(4):
        prm[8 + rb : 9 + rb, :] = jnp.full((1, 128), tile_ids[rb], jnp.int32).astype(F32)
    prm[12:16, :] = jnp.zeros((4, 128), F32)
    prm_out[...] = pltpu.roll(prm[...], 32, 1)
    prm_core = remote(prm_out, prm_in, prm_s.at[0], prm_r.at[0], core)
    prm_strip = remote(prm, prm_pair, prm_s.at[1], prm_r.at[1], peer(0, 1, 1))

    for c in loads:
        c.wait()

    def pack_send(i, carry):
        gather_rows(i, 1 - g, snd)
        snd_copy(i).start()
        return carry

    def pack_keep(i, carry):
        gather_rows(i, g, keep)
        return carry

    for i in (0, 4, 1):
        gather_rows(i, g, keep)
    pl.semaphore_wait(barrier, len(greet))
    a_copy(0).start()
    via_copy(1, 0).start()
    a_copy(1).start()
    lax.fori_loop(0, 8, pack_send, 0)
    prm_core.start()
    prm_strip.start()
    lax.fori_loop(2, 4, pack_keep, 0)
    lax.fori_loop(5, 8, pack_keep, 0)
    for i in (0, 4, 1):
        snd_copy(i).wait_recv()
        if i == 4:
            via_copy(1, 1).start()
        else:
            b_copy(i).start()

    for c in tables:
        c.wait()
    lane = lax.broadcasted_iota(jnp.int32, (512, 1), 0)
    wave = lax.broadcasted_iota(jnp.int32, (1, 512), 1)
    turn = lax.rem(lane, 128)
    for half in range(2):
        late = (turn >= 64).astype(jnp.int32)
        late = late if half == 0 else 1 - late
        target = 8 * lax.rem(turn, 64) + 2 * (lane // 128) + late
        perm[half] = jnp.where(target == wave, 1.0, 0.0).astype(BF)
        c_hi, c_lo = split(waves[half, 0])
        s_hi, s_lo = split(waves[half, 1])
        for k, (c, w) in enumerate(((c_hi, s_hi), (c_hi, s_hi), (c_lo, s_lo))):
            table[half, 512 * k : 512 * k + 256, 0:256] = c
            table[half, 512 * k : 512 * k + 256, 256:512] = -w
            table[half, 512 * k + 256 : 512 * k + 512, 0:256] = w
            table[half, 512 * k + 256 : 512 * k + 512, 256:512] = c

    lanes = lax.rem(lax.broadcasted_iota(jnp.int32, (1, 512), 1), 128)
    for half in range(2):
        late = lanes >= 64 if half == 0 else lanes < 64
        sign = 1.0 - 2.0 * jnp.where(late, h, 0).astype(F32)
        stack = []
        for b in (half, half + 2):
            sine, cosine = sincos(phi[:, 512 * b : 512 * b + 512])
            stack += [*split(cosine), *split(sine)]
        got = dot_t(jnp.concatenate(stack, axis=0), perm[half])
        for k, b in enumerate((half, half + 2)):
            for part in range(2):
                at = 128 * k + 64 * part
                e_own[part, :, 512 * b : 512 * b + 512] = (got[at : at + 32] + got[at + 32 : at + 64]) * sign
    e_copy = remote(e_own, e_other, prm_s.at[2], prm_r.at[2], core)
    e_copy.start()

    prm_core.wait()
    prm_strip.wait()
    both = prm[...] + prm_in[...]
    shift = both[0:1, :]
    col = lax.broadcasted_iota(jnp.int32, (NT, 128), 1)
    freq = lax.rem(lax.rem(col, 64) + 32 * g, NF)
    angle = (2.0 * math.pi / NF) * lax.rem(lax.broadcasted_iota(jnp.int32, (NT, 128), 0) * freq, NF).astype(F32)
    scale = 1.0 / math.sqrt(NF)
    real_in = col < 64

    def base(tile):
        phase = jnp.zeros((1, 128), F32)
        for t in range(4):
            phase = phase + jnp.where(tile == float(t), both[1 + t : 2 + t, :], 0.0)
        im, re = sincos(angle + phase)
        im, re = im * scale, re * scale
        return jnp.concatenate([jnp.where(real_in, re, -im), jnp.where(real_in, im, re)], axis=0)

    far = (4 * (1 - 2 * odd)).astype(F32)
    inside = jnp.where(odd == 1, (s > 1).astype(F32), (s < strips - 2).astype(F32))
    for nd in range(4):
        dest = block_of(nd)
        here, there = base(prm[8 + nd : 9 + nd, :]), base(prm_pair[pl.ds(8 + dest, 1), :])
        rows = slice(64 * nd, 64 * nd + 64)
        for n in range(4):
            source = block_of(n)
            own_hi, own_lo = split(jnp.where(shift == (nd - source).astype(F32), here, 0.0))
            step = (dest - source).astype(F32)
            pair_hi, pair_lo = split(jnp.where(shift == step + far, there, 0.0))
            halo_hi, halo_lo = split(jnp.where(shift == step - far, there * inside, 0.0))
            below = slice(256 + 64 * nd, 320 + 64 * nd)
            for k, (u, v, w) in enumerate(
                ((own_hi, pair_hi, halo_hi), (own_hi, pair_hi, halo_hi), (own_lo, pair_lo, halo_lo))
            ):
                at = 512 * k + 128 * n
                ww[rows, at : at + 128] = u
                ww[below, at : at + 128] = v
                wh[n, rows, 128 * k : 128 * k + 128] = w
    for i in (2, 3):
        snd_copy(i).wait_recv()
    e_copy.wait()

    def spread_out(k, a, b, i):
        re = jnp.concatenate([a[i, 0], b[i, 0]], axis=0)
        im = jnp.concatenate([a[i, 1], b[i, 1]], axis=0)
        for half_p, parts in enumerate(butterflies(re, im, tw)):
            for j, pieces in enumerate(parts):
                for half, w in enumerate(pieces):
                    hi, lo = split(w)
                    for third, x in enumerate((hi, lo, hi)):
                        at = 512 * third + 256 * half
                        spread[k, half_p, 64 * j : 64 * j + 64, at : at + 256] = x

    def transform(k):
        return [dot(spread[k, p], table[p]) for p in range(2)]

    def turn_phase(even, uneven, at, depth):
        early = lax.broadcasted_iota(jnp.int32, (64, 128), 1) < 64
        for j in range(4):
            for b4 in range(4):
                first, second = (even, uneven) if b4 % 2 == 0 else (uneven, even)
                rows = slice(64 * j, 64 * j + 64)
                c0 = 128 * (b4 // 2)
                u = jnp.where(early, first[rows, c0 : c0 + 128], second[rows, c0 : c0 + 128])
                v = jnp.where(early, first[rows, 256 + c0 : 384 + c0], second[rows, 256 + c0 : 384 + c0])
                e0 = 512 * b4 + 128 * j
                c, w = (
                    jnp.concatenate([e_own[part, :, e0 : e0 + 128], e_other[part, :, e0 : e0 + 128]], axis=0)
                    for part in range(2)
                )
                for half, value in enumerate((u * c - v * w, u * w + v * c)):
                    hi, lo = split(value)
                    for k, x in enumerate((hi, lo, hi)):
                        spec[b4, pl.ds(k * depth + at + 64 * half, 64), 128 * j : 128 * j + 128] = x

    def block_at(dg, dh):
        return 2 * lax.rem(g + dg, 2) + lax.rem(h + dh, 2)

    def near_copy(ii):
        return remote(near.at[1, ii], near_in.at[ii], near_s.at[ii], near_r.at[ii], core)

    def dest_rows(n):
        return pl.ds(pl.multiple_of(64 * (3 - block_of(n)), 64), 64)

    def row_copy(dg, i):
        at, ii = dest_rows(lax.rem(i, 4)), i // 4
        return remote(side.at[dg, ii, at], side_in.at[dg, ii, at], row_s.at[dg, i], row_r.at[dg, i], peer(dg, 0, 1))

    def opp_copy(dg, i, to):
        return remote(opp.at[i, dg], relay_in.at[i, dg], rel_s.at[i, dg], rel_r.at[i, dg], to)

    def opp_cross(dg, i):
        return opp_copy(dg, i, peer(0, 1, 1))

    def opp_direct(dg, i):
        return opp_copy(dg, i, peer(0, 0, 1))

    def cross_copy(dg, i):
        return remote(cross.at[dg, i], cross_in.at[dg, i], crs_s.at[dg, i], crs_r.at[dg, i], peer(dg, 1, 1))

    def own_rows(ii):
        def two(m, carry):
            @pl.when(jnp.logical_and(ii == 0, m == 0))
            def _():
                a_copy(2).start()
                b_copy(2).start()

            @pl.when(jnp.logical_and(ii == 0, m == 1))
            def _():
                pass_on(2, (0, 1))
                a_copy(3).start()
                b_copy(3).start()

            i, at = 4 * ii + 2 * m, pl.multiple_of(256 * m, 256)
            spread_out(0, keep, other, i)
            spread_out(1, keep, other, i + 1)
            turn_phase(*transform(0), at, 512)
            turn_phase(*transform(1), at + 128, 512)
            return carry

        lax.fori_loop(0, 2, two, 0)
        for dh in (1, 0):
            for dg in range(2):
                total = dot(ww[...], spec[block_at(dg, dh)])
                if dh == 0:
                    near[dg, ii] = total[0:256]
                else:
                    side[dg, ii] = total[0:256]

                    @pl.when(ii == 0)
                    def _():
                        row_copy(dg, 1).start()
                        row_copy(dg, 3).start()

                pp[2 * dg + dh, ii] = total[256:512]
        near_copy(ii).start()

    def collect(i):
        n, ii = lax.rem(i, 4), i // 4
        at = dest_rows(n)
        for dg in range(2):
            cross_copy(dg, i).wait()
        parts = [
            near[0, ii, at, :] + side_in[0, ii, at, :] + cross_in[0, i],
            near_in[ii, at, :] + side_in[1, ii, at, :] + cross_in[1, i],
        ]
        got = dot(jnp.concatenate(split(jnp.concatenate(parts, axis=0)), axis=0), perm[h])
        rows = got[0:128] + got[128:256]
        for dg in range(2):
            row = 4 * (3 - block_of(n)) + 2 * lax.rem(g + dg, 2) + ii
            for c in range(4):
                for part in range(2):
                    at = 64 * dg + 32 * part
                    flat[c, part, pl.ds(row, 32, stride=16), :] = rows[at : at + 32, 128 * c : 128 * c + 128]

    def by_cross(i):
        return jnp.logical_or(lax.rem(i, 2) == 0, i == 5)

    def relay(i):
        n, ii = lax.rem(i, 4), i // 4

        @pl.when(by_cross(i))
        def _():
            at = dest_rows(n)
            for dg in range(2):
                opp_cross(dg, i).wait()
                side[dg, ii, at, :] = side[dg, ii, at, :] + relay_in[i, dg]
                row_copy(dg, i).start()

        @pl.when(jnp.logical_not(by_cross(i)))
        def _():
            for dg in range(2):
                opp_direct(dg, i).wait()
                cross[dg, i] = cross[dg, i] + relay_in[i, dg]
                cross_copy(dg, i).start()

    def step(i, carry):
        n, ii = lax.rem(i, 4), i // 4

        @pl.when(i == 1)
        def _():
            for late in range(5, 8):
                snd_copy(late).wait_recv()
            a_copy(5).start()
            b_copy(5).start()

        @pl.when(i == 2)
        def _():
            pass_on(3, (0, 1))
            a_copy(6).start()
            b_copy(6).start()

        @pl.when(i == 3)
        def _():
            a_copy(7).start()
            b_copy(7).start()

        @pl.when(i < 2)
        def _():
            own_rows(i)

        a_copy(i).wait_recv()
        b_copy(i).wait_recv()

        spread_out(0, halo_a, halo_b, i)
        turn_phase(*transform(0), 0, 128)
        for nn in range(4):

            @pl.when(n == nn)
            def _():
                rows = slice(64 * nn, 64 * nn + 64)
                for dh in range(2):
                    for dg in range(2):
                        blk = 2 * dg + dh
                        total = dot(wh[nn, 64 * nn :, :], spec[block_at(dg, dh), 0:384, :])
                        value = pp[blk, ii, rows, :] + total[0:64]
                        if nn < 3:
                            pp[blk, ii, 64 * nn + 64 :, :] = pp[blk, ii, 64 * nn + 64 :, :] + total[64:]
                        if dh == 1:
                            cross[dg, i] = value
                        else:
                            opp[i, dg] = value

                            @pl.when(by_cross(i))
                            def _():
                                opp_cross(dg, i).start()

                            @pl.when(jnp.logical_not(by_cross(i)))
                            def _():
                                opp_direct(dg, i).start()

                @pl.when(by_cross(i))
                def _():
                    for dg in range(2):
                        cross_copy(dg, i).start()

        @pl.when(i >= 1)
        def _():
            relay(i - 1)

        @pl.when(i == 2)
        def _():
            for dg in range(2):
                row_copy(dg, 7).start()


        @pl.when(i >= 4)
        def _():
            @pl.when(i == 4)
            def _():
                near_copy(0).wait()

            for dg in range(2):
                row_copy(dg, i - 4).wait()
            collect(i - 4)

        return carry

    lax.fori_loop(0, 8, step, 0)
    near_copy(1).wait()

    def last(i, carry):
        for dg in range(2):
            row_copy(dg, i).wait()
        collect(i)
        return carry

    lax.fori_loop(4, 6, last, 0)
    relay(7)
    lax.fori_loop(6, 8, last, 0)
    results = [
        pltpu.make_async_copy(flat.at[c], out.at[:, :, pl.ds(128 * c, 128)], load_sem.at[c]) for c in range(4)
    ]
    for c in results:
        c.start()
    for i in range(8):
        snd_copy(i).wait_send()
        if i != 4:
            a_copy(i).wait_send()
        if i != 4:
            b_copy(i).wait_send()
    for hops in range(1, 4):
        for slot in range(2):
            via_copy(hops, slot).wait_send()
    for c in results:
        c.wait()


def local(strips, field, spectral_phase, chirp_shift, tile_map, tile_phase):
    waves, tw = dft_tables()
    vmem = pl.BlockSpec(memory_space=pltpu.VMEM)
    hbm = pl.BlockSpec(memory_space=pl.ANY)
    rows = pltpu.VMEM((8, 2, 32, 1024), F32)
    small = pltpu.VMEM((16, 128), F32)
    phase = pltpu.VMEM((2, 32, NY), F32)
    sums = pltpu.VMEM((2, 2, 256, 512), F32)
    dma = pltpu.SemaphoreType.DMA
    out = pl.pallas_call(
        functools.partial(kernel, strips),
        in_specs=[hbm, hbm, hbm, hbm, vmem, vmem, pl.BlockSpec(memory_space=pltpu.SMEM)],
        out_specs=pl.BlockSpec(memory_space=pl.ANY),
        out_shape=jax.ShapeDtypeStruct((2, 512, 512), F32),
        scratch_shapes=[
            pltpu.VMEM((8, 2, 512, 128), F32),
            rows, rows, rows, rows, rows,
            small, small, small, small,
            pltpu.VMEM((32, NY), F32),
            pltpu.VMEM(waves.shape, F32),
            pltpu.VMEM(tw.shape, F32),
            phase, phase,
            pltpu.VMEM((2, 1536, 512), BF),
            pltpu.VMEM((2, 512, 512), BF),
            pltpu.VMEM((512, 1536), BF),
            pltpu.VMEM((4, 256, 384), BF),
            pltpu.VMEM((2, 2, 256, 1536), BF),
            pltpu.VMEM((4, 1536, 512), BF),
            sums,
            pltpu.VMEM((2, 256, 512), F32),
            sums, sums,
            pltpu.VMEM((4, 2, 256, 512), F32),
            pltpu.VMEM((8, 2, 64, 512), F32),
            pltpu.VMEM((8, 2, 64, 512), F32),
            pltpu.VMEM((2, 8, 64, 512), F32),
            pltpu.VMEM((2, 8, 64, 512), F32),
            pltpu.VMEM((2, 2, 32, 1024), F32),
            pltpu.VMEM((2, 2, 32, 1024), F32),
            dma((11,)),
            *[dma((8,))] * 6,
            dma((3,)), dma((3,)),
            dma((2,)), dma((2,)),
            dma((2, 8)), dma((2, 8)),
            dma((8, 2)), dma((8, 2)),
            dma((2, 8)), dma((2, 8)),
            *[dma((2,))] * 4,
        ],
        compiler_params=pltpu.CompilerParams(
            collective_id=0, has_side_effects=True, vmem_limit_bytes=VMEM * 2**20
        ),
        cost_estimate=pl.CostEstimate(flops=40 * 10**9, bytes_accessed=10 * 2**20, transcendentals=0),
    )(
        field.reshape(2, 512, 1024), spectral_phase, jnp.asarray(waves), jnp.asarray(tw),
        chirp_shift.reshape(1, 32), tile_phase, tile_map,
    )
    return out.reshape(2, NT, 16, 512)


def solution(mesh):
    placed = (P(None, "freq", "xs", "yh"), P("freq", None), P("freq"), P("xs"), P(None, "freq"))
    return jax.shard_map(
        functools.partial(local, mesh.shape["xs"]),
        mesh=mesh,
        in_specs=placed,
        out_specs=P(None, None, "xs", ("freq", "yh")),
        check_vma=False,
    )
```
